256 devices in a mesh: row: 16 (over y_hi, z), col: 16 (over x, y_lo, core).
Axes of the slice: x: 4, y: 4 (y_hi: 2, y_lo: 2; y = y_hi * 2 + y_lo), z: 8, core: 2. Of those that a mesh axis runs over, the one named last changes fastest.
Arguments:
- factor: bfloat16 [16384, 16384], P('row', 'col'), may hold values from -0.078125 to 0.078125
- diag_inv: bfloat16 [16384, 1024], P('row'), may hold values from -1 to 1.5, as said below
- rhs: bfloat16 [16384, 256], P('row'), may hold values from -6 to 6
- forward_values: bfloat16 [16384, 256], P('row'), may hold values from -6 to 6
Outputs:
- forward_solved: bfloat16 [3072, 256], replicated
- forward_rest: float32 [16384, 256], P('row', 'col')
- back_sums: float32 [16384, 256], P('col', 'row')
- solution: float32 [16384, 256], P('row')
The draws below stay inside these ranges and needn't reach their ends.
Inputs may be any that keep to these rules, and one draw needn't show every extreme that they name: Each 1024 x 1024 block of diag_inv is lower triangular with diagonal entries between 0.5 and 1.5.
All inputs are finite; a program needn't handle non-finite values.
Results may differ from the reference program's by a relative error of at most 0.0095.
Values may be sent and summed in bfloat16 or wider, within the bound.
A program may use at most 64 MiB of HBM per device.

```python
import math
import jax
import jax.numpy as jnp
from jax import lax

NB = 1024
R = 256
STEPS = 3
NBLK = 16
N = 16384
N_ROW = 16
N_COL = 16


def draw_diag_inv(key, part):
    key = jax.random.fold_in(key, 7)
    first_key, second_key = jax.random.split(key)
    shape = (NBLK, NB, NB)
    row_pos = lax.broadcasted_iota(jnp.int32, shape, 1)
    col_pos = lax.broadcasted_iota(jnp.int32, shape, 2)
    scale = 1.0 / math.sqrt(NB)
    diagonal = jax.random.uniform(first_key, shape, jnp.float32, 0.7, 1.3)
    lower = jax.random.normal(second_key, shape, jnp.float32) * (0.6 * scale)
    full = jnp.where(row_pos == col_pos, diagonal, jnp.where(row_pos > col_pos, lower, 0.0))
    return full.reshape(NBLK * NB, NB).astype(jnp.bfloat16)


def steps_of(stream_key, extent, shards, low, largest):
    factor_of, own = 1.0, jax.random.fold_in(stream_key, 6)
    for dim, shards_of in shards:
        steps = jnp.exp(jax.random.uniform(jax.random.fold_in(own, dim), (shards_of,), jnp.float32, low / len(shards), largest / len(shards)))
        factor_of = factor_of * jnp.repeat(steps, extent[dim] // shards_of).reshape([-1 if axis == dim else 1 for axis in range(len(extent))])
    return factor_of


def scatter_about(rng, dims, scale, most, cuts=(), held_as=jnp.bfloat16):
    values = jax.random.normal(rng, dims, jnp.float32) * scale
    if len(cuts) > 0:
        values = steps_of(rng, dims, cuts, -0.22, 0.18) * values
    return jnp.clip(values, min=-most, max=most).astype(held_as)


def setup_inputs(seed: int = 0) -> dict:
    key_of = jax.random.split(jax.random.key(seed), 5)
    return {
        "factor": scatter_about(key_of[0], (N, N), (2 * NB * STEPS) ** -0.5, 0.078125, ((0, 16), (1, 16))),
        "diag_inv": draw_diag_inv(jax.random.fold_in(key_of[4], 71), 0),
        "rhs": scatter_about(key_of[2], (N, R), 1.0, 6.0, ((0, 16),)),
        "forward_values": scatter_about(key_of[3], (N, R), 1.0, 6.0, ((0, 16),)),
    }


def block_at(factor, row_index, col_index):
    return factor[row_index * NB:(row_index + 1) * NB, col_index * NB:(col_index + 1) * NB]


def reference(factor, diag_inv, rhs, forward_values):
    row_blocks = NBLK // N_ROW
    col_blocks = NBLK // N_COL
    forward_blocks = []
    rest_blocks = []
    for position in range(NBLK):
        summed = jnp.zeros((NB, R), jnp.float32)
        for group in range(N_COL):
            group_sum = jnp.zeros((NB, R), jnp.float32)
            for other in range(group * col_blocks, (group + 1) * col_blocks):
                if other < min(position, STEPS):
                    group_sum = group_sum + jnp.dot(block_at(factor, position, other), forward_blocks[other], preferred_element_type=jnp.float32)
            summed = summed + lax.optimization_barrier(group_sum.astype(jnp.bfloat16)).astype(jnp.float32)
        rest = rhs[position * NB:(position + 1) * NB].astype(jnp.float32) - summed
        rest_blocks.append(rest)
        if position < STEPS:
            residue = rest.astype(jnp.bfloat16)
            inverse = diag_inv[position * NB:(position + 1) * NB]
            forward_blocks.append(jnp.dot(inverse, residue, preferred_element_type=jnp.float32).astype(jnp.bfloat16))
    first_back = NBLK - STEPS
    answers = [None] * NBLK
    rounded_answers = [None] * NBLK
    sum_blocks = [None] * NBLK
    for position in reversed(range(NBLK)):
        summed = jnp.zeros((NB, R), jnp.float32)
        for group in range(N_ROW):
            group_sum = jnp.zeros((NB, R), jnp.float32)
            for other in range(group * row_blocks, (group + 1) * row_blocks):
                if other > position and other >= first_back:
                    group_sum = group_sum + jnp.dot(block_at(factor, other, position).T, rounded_answers[other], preferred_element_type=jnp.float32)
            summed = summed + lax.optimization_barrier(group_sum.astype(jnp.bfloat16)).astype(jnp.float32)
        sum_blocks[position] = summed
        if position >= first_back:
            gathered_sum = summed.astype(jnp.bfloat16)
            earlier = forward_values[position * NB:(position + 1) * NB]
            centred = (earlier.astype(jnp.float32) - gathered_sum.astype(jnp.float32)).astype(jnp.bfloat16)
            inverse = diag_inv[position * NB:(position + 1) * NB]
            answers[position] = jnp.dot(inverse.T, centred, preferred_element_type=jnp.float32)
            rounded_answers[position] = answers[position].astype(jnp.bfloat16)
        else:
            answers[position] = jnp.zeros((NB, R), jnp.float32)
    return (jnp.concatenate(forward_blocks, axis=0), jnp.concatenate(rest_blocks, axis=0), jnp.concatenate(sum_blocks, axis=0), jnp.concatenate(answers, axis=0))
```

```python
import jax
import jax.numpy as jnp
from jax import lax
from jax.experimental import pallas as pl
from jax.experimental.pallas import tpu as pltpu
from jax.sharding import PartitionSpec as P

NB = 1024
COLS = 256
STEPS = 3
NROW = 16
NCOL = 16
PIECE = 16
CHUNK = 64
HALF = 512
MESH = pl.DeviceIdType.MESH
F32 = jnp.float32
BF16 = jnp.bfloat16


def product(left, right):
    return lax.dot_general(left, right, (((1,), (0,)), ((), ())), preferred_element_type=F32)


def loop(count, body):
    def step(index, carry):
        body(index)
        return carry

    lax.fori_loop(0, count, step, 0)


def kernel(
    factor, inverse, rhs, start,
    solved_out, rest_out, back_out, solution_out,
    lv, dv, bv, uv, lt, dt, bt, ut,
    yt, yc, pc, yr, pf, rp, qf, qr, qc, tb, wg, vf, vb, so, sl,
    ld_s, out_s,
    yc_r, pc_r, own_r, s3_r, s4_r, rp_r, qr_r, qc_r, tb_r, ag_r, sib_r,
    y0_s, s1_s, s2_s, s3_s, s4_s, pf_s, fw_s, ch_s, pc_s, qf_s, qc_s, tb_s, ag_s, sib_s,
):
    r = lax.axis_index("row")
    c = lax.axis_index("col")
    x = c // 4
    yl = (c // 2) % 2
    e = c % 2
    yh = r // 8
    z = r % 8
    y = 2 * yh + yl
    mine = 4 * x + y
    row0 = r == 0
    chain1 = (r == 1) & (c == 0)
    chain20 = (r == 2) & (c == 0)
    chain2 = (r == 2) & (c == 1)
    row13 = r == 13
    row14 = r == 14
    row15 = r == 15
    late = r >= 13
    back1 = (r == 14) & (c == 13)
    half = pl.multiple_of(e * HALF, HALF)

    def remote(src, dst, send, recv, row, col):
        return pltpu.make_async_remote_copy(
            src_ref=src, dst_ref=dst, send_sem=send, recv_sem=recv, device_id=(row, col), device_id_type=MESH
        )

    def got(ref, sem):
        remote(ref, ref, sem, sem, r, c).wait_recv()

    def sent(ref, sem):
        remote(ref, ref, sem, sem, r, c).wait_send()

    def rows(index, count):
        return pl.ds(pl.multiple_of(index * count, count), count)

    loads = [
        pltpu.make_async_copy(source, target, ld_s.at[index])
        for index, (source, target) in enumerate(((inverse, dv), (rhs, bv), (factor, lv), (start, uv)))
    ]
    for load in loads:
        load.start()
    barrier = pltpu.get_barrier_semaphore()

    def greet(row, col):
        pl.semaphore_signal(barrier, inc=1, device_id=(row, col), device_id_type=MESH)

    loop(15, lambda k: greet(r, lax.rem(c + 1 + k, 16)))
    loop(15, lambda k: greet(lax.rem(r + 1 + k, 16), c))
    loop(16, lambda k: greet(lax.rem(r + 8, 16), k))

    @pl.when(chain1)
    def _():
        greet(0, 2)
        greet(0, 4)
        greet(0, 12)

    @pl.when(chain2)
    def _():
        greet(1, 0)

    @pl.when(row14 & (c != 14))
    def _():
        greet(15, 14)

    @pl.when(row13 & (c != 13))
    def _():
        greet(15, 13)
        greet(14, 13)

    sl[...] = jnp.zeros_like(sl)
    loads[0].wait()
    loads[1].wait()

    @pl.when(row0)
    def _():
        value = jnp.dot(dv[...], bv[...], preferred_element_type=F32)
        yr[...] = value.astype(BF16).T

    bt[...] = bv[...].T
    loads[2].wait()
    loads[3].wait()

    @pl.when(late)
    def _():
        ut[...] = uv[...].T

    @pl.when(row15)
    def _():
        value = product(ut[...], dv[...])
        vf[...] = value
        vb[...] = value.astype(BF16)

        @pl.when(c < 15)
        def _():
            qf[...] = product(vb[...], lv[...]).astype(BF16)

    @pl.when(chain1 | chain2)
    def _():
        dt[...] = dv[...].T

    @pl.when((c < 3) & (r > c))
    def _():
        lt[...] = lv[...].T

    extra = jnp.where(
        ((r == 15) & ((c == 14) | (c == 13))) | back1,
        15,
        jnp.where(chain1 | (row0 & ((c == 2) | (c == 4) | (c == 12))), 1, 0),
    )
    pl.semaphore_wait(barrier, 46 + extra)

    def scatter_pf(chunk):
        for k in range(4):
            g = 4 * chunk + k

            @pl.when(g != c)
            def _():
                remote(pf.at[rows(g, PIECE)], rp.at[c], pf_s, rp_r.at[c], r, g).start()

    def scatter_qf(chunk):
        for k in range(4):
            h = 4 * chunk + k

            @pl.when(h != r)
            def _():
                remote(qf.at[rows(h, PIECE)], qr.at[r - 13], qf_s, qr_r.at[r - 13], h, c).start()

    def send_t(slot, row):
        def one(g):
            remote(qf.at[rows(g, PIECE)], tb.at[slot], tb_s, tb_r.at[slot], row, g).start()

        return one

    @pl.when(row0)
    def _():
        for col, chunk in ((0, 2), (4, 1), (12, 0), (2, 3)):

            @pl.when(c == col)
            def _():
                part = pl.ds(chunk * CHUNK, CHUNK)
                remote(yr.at[part], yc.at[part], y0_s, yc_r.at[chunk], 1, 0).start()

        other = 3 - y
        part = rows(4 * x + other, PIECE)
        remote(
            yr.at[part, pl.ds(half, HALF)], yt.at[0, part, pl.ds(half, HALF)], s1_s.at[0], own_r.at[0],
            8, 4 * x + 2 * (other - 2) + e,
        ).start()
        part = rows(mine, PIECE)
        yt[0, part, pl.ds(half, HALF)] = yr[part, pl.ds(half, HALF)]

    @pl.when(row15 & (c == 14))
    def _():
        def one(step):
            chunk = lax.rem(5 - step, 4)
            part = rows(chunk, CHUNK)
            remote(qf.at[part], qc.at[part], qc_s.at[chunk], qc_r.at[chunk], 14, 13).start()

        loop(4, one)
        loop(16, send_t(0, 14))

    @pl.when(row15 & (c == 13))
    def _():
        loop(16, send_t(0, 13))

    @pl.when(row15 & (c < 15))
    def _():
        loop(4, scatter_qf)

    def scatter_s1(j, chunk):
        for k in range(4):
            for side in range(2):
                part = pl.ds(pl.multiple_of(chunk * CHUNK + k * PIECE, PIECE), PIECE)
                lanes = pl.ds(side * HALF, HALF)
                row = (k // 2) * 8 + j
                col = 4 * chunk + (k % 2) * 2 + side
                own = (r == row) & (c == col)

                @pl.when(jnp.logical_not(own))
                def _():
                    remote(yr.at[part, lanes], yt.at[j, part, lanes], s1_s.at[chunk], own_r.at[j], row, col).start()

                @pl.when(own)
                def _():
                    yt[j, part, lanes] = yr[part, lanes]

    @pl.when(chain1)
    def _():
        def one(step):
            chunk = lax.rem(6 - step, 4)
            part = rows(chunk, CHUNK)
            got(yc.at[part], yc_r.at[chunk])
            partial = product(yc[part], lt[...]).astype(BF16)
            pf[part] = partial
            residue = (bt[part].astype(F32) - partial.astype(F32)).astype(BF16)
            yr[part] = product(residue, dt[...]).astype(BF16)
            remote(yr.at[part], yc.at[part], ch_s.at[chunk], yc_r.at[chunk], 2, 1).start()
            remote(yc.at[part], yc.at[part], fw_s.at[chunk], yc_r.at[chunk], 2, 0).start()

        loop(4, one)

        def rest(step):
            chunk = lax.rem(6 - step, 4)
            scatter_s1(1, chunk)
            scatter_pf(chunk)

        loop(4, rest)

    @pl.when(chain20)
    def _():
        def one(step):
            chunk = lax.rem(6 - step, 4)
            part = rows(chunk, CHUNK)
            got(yc.at[part], yc_r.at[chunk])
            pf[part] = product(yc[part], lt[...]).astype(BF16)
            remote(pf.at[part], pc.at[part], pc_s.at[chunk], pc_r.at[chunk], 2, 1).start()

        loop(4, one)
        loop(4, scatter_pf)

    @pl.when(chain2)
    def _():
        def one(step):
            chunk = lax.rem(6 - step, 4)
            part = rows(chunk, CHUNK)
            got(yc.at[part], yc_r.at[chunk])
            partial = product(yc[part], lt[...]).astype(BF16)
            pf[part] = partial
            got(pc.at[part], pc_r.at[chunk])
            total = pc[part].astype(F32) + partial.astype(F32)
            residue = (bt[part].astype(F32) - total).astype(BF16)
            yr[part] = product(residue, dt[...]).astype(BF16)
            scatter_s1(2, chunk)

        loop(4, one)
        loop(4, scatter_pf)

    @pl.when(back1)
    def _():
        def one(step):
            chunk = lax.rem(5 - step, 4)
            part = rows(chunk, CHUNK)
            got(qc.at[part], qc_r.at[chunk])
            centred = (ut[part].astype(F32) - qc[part].astype(F32)).astype(BF16)
            answer = product(centred, dv[...]).astype(BF16)
            qf[part] = product(answer, lv[...]).astype(BF16)
            for k in range(4):
                send_t(1, 13)(4 * chunk + k)

        loop(4, one)

    def spread(j):
        part = rows(mine, PIECE)
        lanes = pl.ds(half, HALF)
        block = yt.at[j, part, lanes]

        root = (chain1 if j == 1 else chain2 if j == 2 else row0)

        @pl.when(jnp.logical_not(root if j == 0 else root & (mine == 0) & (e == (j - 1))))
        def _():
            got(block, own_r.at[j])

        @pl.when(z == j)
        def _():
            def along(k):
                far = lax.rem(z + jnp.where(k == 0, 4, jnp.where(k < 4, k, k + 1)), 8)
                remote(block, block, s2_s, own_r.at[j], yh * 8 + far, c).start()

            loop(7, along)

        def across(k):
            to = lax.rem(mine + 1 + k, 16)
            row = ((to % 4) // 2) * 8 + z
            col = 4 * (to // 4) + 2 * (to % 2) + e
            remote(block, block, s3_s.at[j], s3_r.at[j, x], row, col).start()

        loop(15, across)

    def collect(j):
        lanes = pl.ds(half, HALF)

        def one(step):
            chunk = lax.rem(6 - step, 4)
            part = rows(chunk, CHUNK)

            @pl.when(chunk == x)
            def _():
                got(yt.at[j, pl.ds(0, 48), lanes], s3_r.at[j, chunk])

            @pl.when(chunk != x)
            def _():
                got(yt.at[j, part, lanes], s3_r.at[j, chunk])

            block = yt.at[j, part, lanes]
            remote(block, block, s4_s.at[j, chunk], s4_r.at[j, chunk], r, c + 1 - 2 * e).start()

        loop(4, one)

    def apply(j):
        other = pl.ds(pl.multiple_of(HALF - half, HALF), HALF)

        def one(step):
            chunk = lax.rem(6 - step, 4)
            part = rows(chunk, CHUNK)
            got(yt.at[j, part, other], s4_r.at[j, chunk])

            @pl.when((c == j) & (r >= 3))
            def _():
                pf[part] = product(yt[j, part], lt[...]).astype(BF16)
                scatter_pf(chunk)

        loop(4, one)
        whole = pl.ds(j * NB, NB)
        so[whole] = yt[j].T
        pltpu.make_async_copy(so.at[whole], solved_out.at[whole], out_s.at[j]).start()

    def centre():
        @pl.when(row14 | row13)
        def _():
            got(tb.at[0], tb_r.at[0])

            @pl.when(row13)
            def _():
                got(tb.at[1], tb_r.at[1])

            total = tb[0].astype(F32)
            total = total + jnp.where(row13, tb[1].astype(F32), 0.0)
            summed = total.astype(BF16).astype(F32)
            piece = (ut[rows(c, PIECE)].astype(F32) - summed).astype(BF16)
            wg[x, yl, e] = piece
            block = wg.at[x, yl, e]

            def one(k):
                to = lax.rem(2 * x + yl + 1 + k, 8)
                remote(block, block, ag_s, ag_r.at[x], r, 2 * to + e).start()

            loop(7, one)

    def gather():
        @pl.when(row14 | row13)
        def _():
            def one(step):
                chunk = lax.rem(5 - step, 4)

                @pl.when(chunk == x)
                def _():
                    got(wg.at[chunk, 0, e], ag_r.at[chunk])

                @pl.when(chunk != x)
                def _():
                    got(wg.at[chunk, :, e], ag_r.at[chunk])

                block = wg.at[chunk, :, e]
                remote(block, block, sib_s.at[chunk], sib_r.at[chunk], r, c + 1 - 2 * e).start()

            loop(4, one)

    def solve():
        @pl.when(row14 | row13)
        def _():
            def one(step):
                chunk = lax.rem(5 - step, 4)
                part = rows(chunk, CHUNK)
                got(wg.at[chunk, :, 1 - e], sib_r.at[chunk])
                answer = product(wg[chunk].reshape(CHUNK, NB), dv[...])
                vf[part] = answer

                @pl.when((c < r) & jnp.logical_not(back1))
                def _():
                    qf[part] = product(answer.astype(BF16), lv[...]).astype(BF16)
                    scatter_qf(chunk)

            loop(4, one)

            @pl.when(back1)
            def _():
                loop(4, scatter_qf)

    spread(0)
    centre()
    collect(0)
    spread(1)
    gather()
    apply(0)
    solve()
    collect(1)
    apply(1)
    spread(2)
    collect(2)

    @pl.when(late)
    def _():
        sl[...] = vf[...].T

    done = pltpu.make_async_copy(sl, solution_out, out_s.at[3])
    done.start()
    apply(2)

    rest_out[...] = bt[rows(c, PIECE)].astype(F32)
    for j in range(STEPS):

        @pl.when(r > j)
        def _():
            @pl.when(c == j)
            def _():
                rest_out[...] -= pf[rows(c, PIECE)].astype(F32)

            @pl.when(c != j)
            def _():
                got(rp.at[j], rp_r.at[j])
                rest_out[...] -= rp[j].astype(F32)

    back_out[...] = jnp.zeros_like(back_out)
    for j in range(STEPS):

        @pl.when(c < 13 + j)
        def _():
            @pl.when(r == 13 + j)
            def _():
                back_out[...] += qf[rows(r, PIECE)].astype(F32)

            @pl.when(r != 13 + j)
            def _():
                got(qr.at[j], qr_r.at[j])
                back_out[...] += qr[j].astype(F32)

    lanes = pl.ds(0, HALF)
    for j in range(STEPS):
        sent(yt.at[j, pl.ds(0, 240), lanes], s3_s.at[j])
        loop(4, lambda k: sent(yt.at[j, pl.ds(0, CHUNK), lanes], s4_s.at[j, k]))

    @pl.when(z < STEPS)
    def _():
        sent(yt.at[0, pl.ds(0, 112), lanes], s2_s)

    @pl.when(row0)
    def _():
        @pl.when((c == 0) | (c == 2) | (c == 4) | (c == 12))
        def _():
            sent(yr.at[pl.ds(0, CHUNK)], y0_s)

        sent(yr.at[pl.ds(0, PIECE), lanes], s1_s.at[0])

    @pl.when(chain1 | chain2)
    def _():
        sent(yr.at[pl.ds(0, 112), lanes], s1_s.at[0])
        for k in range(1, 4):
            sent(yr.at[pl.ds(0, 128), lanes], s1_s.at[k])

    @pl.when(chain1)
    def _():
        for k in range(4):
            sent(yr.at[pl.ds(0, CHUNK)], ch_s.at[k])
            sent(yc.at[pl.ds(0, CHUNK)], fw_s.at[k])

    @pl.when(chain20)
    def _():
        for k in range(4):
            sent(pf.at[pl.ds(0, CHUNK)], pc_s.at[k])

    @pl.when((c < STEPS) & (r > c))
    def _():
        sent(pf.at[pl.ds(0, 240)], pf_s)

    @pl.when(late & (c < r))
    def _():
        sent(qf.at[pl.ds(0, 240)], qf_s)

    @pl.when(row15 & (c == 14))
    def _():
        for k in range(4):
            sent(qf.at[pl.ds(0, CHUNK)], qc_s.at[k])

    @pl.when((row15 & ((c == 14) | (c == 13))) | back1)
    def _():
        sent(qf, tb_s)

    @pl.when(row14 | row13)
    def _():
        sent(qf.at[pl.ds(0, 112)], ag_s)
        for k in range(4):
            sent(wg.at[0, :, 0], sib_s.at[k])

    for j in range(STEPS):
        whole = pl.ds(j * NB, NB)
        pltpu.make_async_copy(so.at[whole], solved_out.at[whole], out_s.at[j]).wait()
    done.wait()


def local(factor, diag_inv, rhs, forward_values):
    anywhere = pl.BlockSpec(memory_space=pl.ANY)
    vmem = pl.BlockSpec(memory_space=pltpu.VMEM)
    dma = pltpu.SemaphoreType.DMA
    square = pltpu.VMEM((NB, NB), BF16)
    tall = pltpu.VMEM((NB, COLS), BF16)
    wide = pltpu.VMEM((COLS, NB), BF16)
    solved, rest, back, answer = pl.pallas_call(
        kernel,
        name="solves",
        out_shape=(
            jax.ShapeDtypeStruct((STEPS * NB, COLS), BF16),
            jax.ShapeDtypeStruct((PIECE, NB), F32),
            jax.ShapeDtypeStruct((PIECE, NB), F32),
            jax.ShapeDtypeStruct((NB, COLS), F32),
        ),
        in_specs=[anywhere] * 4,
        out_specs=(anywhere, vmem, vmem, anywhere),
        scratch_shapes=[
            square, square, tall, tall, square, square, wide, wide,
            pltpu.VMEM((STEPS, COLS, NB), BF16),
            wide, wide, wide, wide,
            pltpu.VMEM((STEPS, PIECE, NB), BF16),
            wide,
            pltpu.VMEM((STEPS, PIECE, NB), BF16),
            wide,
            pltpu.VMEM((2, PIECE, NB), BF16),
            pltpu.VMEM((4, 2, 2, PIECE, NB), BF16),
            pltpu.VMEM((COLS, NB), F32),
            wide,
            pltpu.VMEM((STEPS * NB, COLS), BF16),
            pltpu.VMEM((NB, COLS), F32),
            dma((4,)), dma((4,)),
            dma((4,)), dma((4,)), dma((3,)), dma((3, 4)), dma((3, 4)), dma((3,)), dma((3,)), dma((4,)), dma((2,)),
            dma((4,)), dma((4,)),
            dma(()), dma((4,)), dma(()), dma((3,)), dma((3, 4)), dma(()), dma((4,)), dma((4,)), dma((4,)),
            dma(()), dma((4,)), dma(()), dma(()), dma((4,)),
        ],
        compiler_params=pltpu.CompilerParams(
            collective_id=0, has_side_effects=True, vmem_limit_bytes=48 * 1024 * 1024
        ),
    )(factor, diag_inv, rhs, forward_values)
    return solved, rest.T, back.T, answer


def solution(mesh):
    placed = (P("row", "col"), P("row", None), P("row", None), P("row", None))
    return jax.shard_map(
        local,
        mesh=mesh,
        in_specs=placed,
        out_specs=(P(), P("row", "col"), P("col", "row"), P("row", None)),
        check_vma=False,
    )
```

```python
import jax
import jax.numpy as jnp
from jax import lax
from jax.experimental import pallas as pl
from jax.experimental.pallas import tpu as pltpu
from jax.sharding import PartitionSpec as P

NB = 1024
COLS = 256
STEPS = 3
NROW = 16
NCOL = 16
PIECE = 16
CHUNK = 64
HALF = 512
MESH = pl.DeviceIdType.MESH
F32 = jnp.float32
BF16 = jnp.bfloat16


def product(left, right):
    return lax.dot_general(left, right, (((1,), (0,)), ((), ())), preferred_element_type=F32)


def loop(count, body):
    def step(index, carry):
        body(index)
        return carry

    lax.fori_loop(0, count, step, 0)


def kernel(
    factor, inverse, rhs, start,
    solved_out, rest_out, back_out, solution_out,
    lv, dv, bv, uv, lt, dt, bt, ut,
    yt, yc, pc, yr, pf, rp, qf, qr, qc, tb, wg, vf, vb,
    ready, ld_s, out_s,
    yc_r, pc_r, own_r, s3_r, s4_r, rp_r, qr_r, qc_r, tb_r, ag_r, sib_r,
    y0_s, s1_s, s1b_s, s2_s, s3_s, s4_s, pf_s, ch_s, pc_s, qf_s, qc_s, tb_s, ag_s, sib_s,
):
    r = lax.axis_index("row")
    c = lax.axis_index("col")
    x = c // 4
    yl = (c // 2) % 2
    e = c % 2
    yh = r // 8
    z = r % 8
    y = 2 * yh + yl
    row0 = r == 0
    chain1 = (r == 1) & (c == 0)
    chain20 = (r == 2) & (c == 0)
    chain2 = (r == 2) & (c == 1)
    row13 = r == 13
    row14 = r == 14
    row15 = r == 15
    late = r >= 13
    first = jnp.where(e == 0, (x < 2) & (y < 2), ((x == 0) | (x == 3)) & ((y == 0) | (y == 3)))
    back1 = (r == 14) & (c == 13)
    half = pl.multiple_of(e * HALF, HALF)
    lanes = pl.ds(half, HALF)
    group = 2 * (x % 2) + y % 2
    mine = pl.ds(pl.multiple_of(group * CHUNK, CHUNK), CHUNK)

    def remote(src, dst, send, recv, row, col):
        return pltpu.make_async_remote_copy(
            src_ref=src, dst_ref=dst, send_sem=send, recv_sem=recv, device_id=(row, col), device_id_type=MESH
        )

    def got(ref, sem):
        remote(ref, ref, sem, sem, r, c).wait_recv()

    def sent(ref, sem):
        remote(ref, ref, sem, sem, r, c).wait_send()

    def rows(index, count):
        return pl.ds(pl.multiple_of(index * count, count), count)

    uses_l = ((c < STEPS) & (r > c)) | (late & (c < r))
    uses_d = row0 | chain1 | chain2 | late
    needs = (uses_d, r >= 0, uses_l, late)
    pairs = ((inverse, dv), (rhs, bv), (factor, lv), (start, uv))
    loads = [pltpu.make_async_copy(source, target, ld_s.at[k]) for k, (source, target) in enumerate(pairs)]
    for need, load in zip(needs, loads):
        pl.when(need)(load.start)
    barrier = pltpu.get_barrier_semaphore()

    def greet(row, col):
        pl.semaphore_signal(barrier, inc=1, device_id=(row, col), device_id_type=MESH)

    def greet_other(row, col):
        pl.when((row != r) | (col != c))(lambda: greet(row, col))

    @pl.when(chain1)
    def _():
        for col in (0, 2, 4, 12):
            greet(0, col)

    @pl.when(chain20)
    def _():
        for col in (6, 8, 13, 14):
            greet(0, col)

    @pl.when(chain2)
    def _():
        greet(1, 0)

    pl.when(z == 1)(lambda: greet_other(1, 0))
    pl.when(z == 2)(lambda: greet_other(2, 1))
    greet(r, c + 1 - 2 * e)
    loop(7, lambda k: greet(r, lax.rem(c + 2 + 2 * k, 16)))
    loop(8, lambda k: greet(lax.rem(r + 8, 16), 2 * k + e))
    for col in range(STEPS):
        pl.when(c != col)(lambda: greet(r, col))
    pl.when(r != 13)(lambda: greet(13, c))
    pl.when(r != 14)(lambda: greet(14, c))
    pl.when(r != 15)(lambda: greet(15, c))
    def depth(j):
        return lax.rem(z - j + 8, 8)

    def column(j, far):
        return yh * 8 + lax.rem(far + j, 8)

    def with_children(j, run):
        for parent, children in ((0, (3, 1, 7)), (3, (5, 4, 2)), (7, (6,))):

            @pl.when(depth(j) == parent)
            def _():
                run(children)

    for j in range(STEPS):
        with_children(j, lambda children: [greet(column(j, far), c) for far in children])

    @pl.when(row14 & (c != 14))
    def _():
        greet(15, 14)

    @pl.when(row13 & (c != 13))
    def _():
        greet(15, 13)
        greet(14, 13)

    pl.when(uses_d)(loads[0].wait)
    loads[1].wait()

    @pl.when(row0)
    def _():
        value = jnp.dot(dv[...], bv[...], preferred_element_type=F32)
        yr[...] = value.astype(BF16).T

    bt[...] = bv[...].T
    pl.when(uses_l)(loads[2].wait)

    @pl.when(late)
    def _():
        loads[3].wait()
        ut[...] = uv[...].T

    @pl.when(row15)
    def _():
        value = product(ut[...], dv[...])
        vf[...] = value
        vb[...] = value.astype(BF16)

        @pl.when(c < 15)
        def _():
            qf[...] = product(vb[...], lv[...]).astype(BF16)

    @pl.when(chain1 | chain2)
    def _():
        dt[...] = dv[...].T

    @pl.when((c < 3) & (r > c))
    def _():
        lt[...] = lv[...].T

    def source_of(cols):
        found = c == cols[0]
        for col in cols[1:]:
            found = found | (c == col)
        return row0 & found

    to_one = source_of((0, 2, 4, 12))
    to_two = source_of((6, 8, 13, 14))
    count = 16 + jnp.where(c < STEPS, 15, 0) + jnp.where(z < STEPS, 2, 3) + jnp.where(late, 15, 0)
    count = count + jnp.where(chain1 | chain2, 31, 0)
    count = count + jnp.where(to_one | to_two | chain1, 1, 0)
    count = count + jnp.where((row15 & ((c == 14) | (c == 13))) | back1, 15, 0)
    pl.semaphore_wait(barrier, count)

    for j in range(STEPS):
        near = jnp.where(depth(j) == 6, 7, jnp.where((depth(j) == 1) | (depth(j) == 3) | (depth(j) == 7), 0, 3))

        @pl.when(depth(j) != 0)
        def _():
            pl.semaphore_signal(ready.at[j], inc=1, device_id=(column(j, near), c), device_id_type=MESH)

    def scatter_pf(chunk):
        for k in range(4):
            g = 4 * chunk + k

            @pl.when(g != c)
            def _():
                remote(pf.at[rows(g, PIECE)], rp.at[c], pf_s, rp_r.at[c], r, g).start()

    def scatter_qf(chunk):
        for k in range(4):
            h = 4 * chunk + k

            @pl.when(h != r)
            def _():
                remote(qf.at[rows(h, PIECE)], qr.at[r - 13], qf_s, qr_r.at[r - 13], h, c).start()

    def send_t(slot, row):
        def one(g):
            remote(qf.at[rows(g, PIECE)], tb.at[slot], tb_s, tb_r.at[slot], row, g).start()

        return one

    @pl.when(row0)
    def _():
        for col, chunk in ((0, 3), (4, 2), (12, 1), (2, 0)):

            @pl.when(c == col)
            def _():
                part = pl.ds(chunk * CHUNK, CHUNK)
                remote(yr.at[part], yc.at[part], y0_s, yc_r.at[chunk], 1, 0).start()

        for col, chunk in ((6, 3), (8, 2), (14, 1), (13, 0)):

            @pl.when(c == col)
            def _():
                part = pl.ds(chunk * CHUNK, CHUNK)
                remote(yr.at[part], yc.at[part], y0_s, yc_r.at[chunk], 2, 0).start()

        other = 3 - y
        part = rows(2 * (x % 2) + other % 2, CHUNK)
        remote(yr.at[part, lanes], yt.at[0, part, lanes], s1_s.at[0], own_r.at[0], 8, 4 * x + 2 * (other - 2) + e).start()
        yt[0, mine, lanes] = yr[mine, lanes]

    @pl.when(row15 & (c == 14))
    def _():
        def one(step):
            chunk = lax.rem(5 - step, 4)
            part = rows(chunk, CHUNK)
            remote(qf.at[part], qc.at[part], qc_s.at[chunk], qc_r.at[chunk], 14, 13).start()

        loop(4, one)
        for k in range(4):
            sent(qf.at[pl.ds(0, CHUNK)], qc_s.at[k])
        loop(16, send_t(0, 14))

    @pl.when(row15 & (c == 13))
    def _():
        loop(16, send_t(0, 13))

    def scatter_s1(j, chunk):
        part = rows(chunk, CHUNK)
        a, b = chunk // 2, chunk % 2
        for side in range(2):
            far = pl.ds(side * HALF, HALF)
            row = j + (8 * b if side else 0)
            col = (12 * a + 2 * b + 1) if side else (4 * a + 2 * b)
            own = (r == row) & (c == col)

            @pl.when(jnp.logical_not(own))
            def _():
                remote(yr.at[part, far], yt.at[j, part, far], s1_s.at[chunk], own_r.at[j], row, col).start()

            @pl.when(own)
            def _():
                yt[j, part, far] = yr[part, far]

    def spread(step):
        j = jnp.where(z == 1, (1, 0, 2)[step], jnp.where(z == 2, (2, 0, 1)[step], step))
        block = yt.at[j, mine, lanes]
        local = (row0 & (j == 0)) | (chain1 & (j == 1)) | (chain2 & (j == 2))

        @pl.when(jnp.logical_not(local))
        def _():
            got(block, own_r.at[j])

        def to_chip(send, recv, tx, ty):
            remote(block, block, send, recv, 8 * (ty // 2) + z, 4 * tx + 2 * (ty % 2) + e).start()

        @pl.when((z == j) & (j > 0) & first)
        def _():
            x2, y2 = lax.rem(x + 2, 4), lax.rem(y + 2, 4)
            to_chip(s1b_s, own_r.at[j], x2, y2)
            to_chip(s1b_s, own_r.at[j], x2, y)
            to_chip(s1b_s, own_r.at[j], x, y2)

        x1, y1 = lax.rem(x + 1 + 2 * e, 4), lax.rem(y + 1 + 2 * e, 4)
        to_chip(s3_s.at[j], s3_r.at[j, group], x1, y1)
        to_chip(s3_s.at[j], s3_r.at[j, group], x1, y)
        to_chip(s3_s.at[j], s3_r.at[j, group], x, y1)
        remote(block, block, s4_s.at[j], s4_r.at[j, group], r, c + 1 - 2 * e).start()

        def run(children):
            pl.semaphore_wait(ready.at[j], len(children))
            for far in children:
                remote(block, block, s2_s.at[j], own_r.at[j], column(j, far), c).start()

        with_children(j, run)

    def collect(j):
        def one(step):
            chunk = 3 - step
            block = yt.at[j, rows(chunk, CHUNK), lanes]

            @pl.when(chunk != group)
            def _():
                got(block, s3_r.at[j, chunk])
                remote(block, block, s4_s.at[j], s4_r.at[j, chunk], r, c + 1 - 2 * e).start()

        loop(4, one)

    def apply(j):
        other = pl.ds(pl.multiple_of(HALF - half, HALF), HALF)

        def one(step):
            chunk = 3 - step
            part = rows(chunk, CHUNK)
            got(yt.at[j, part, other], s4_r.at[j, chunk])

            @pl.when((c == j) & (r >= 3))
            def _():
                partial = product(yt[j, part], lt[...]).astype(BF16)
                if j == 1:
                    got(pc.at[part], pc_r.at[chunk])
                    partial = (pc[part].astype(F32) + partial.astype(F32)).astype(BF16)
                pf[part] = partial
                if j == 0:
                    remote(pf.at[part], pc.at[part], pc_s.at[chunk], pc_r.at[chunk], r, 1).start()
                else:
                    scatter_pf(chunk)

        loop(4, one)
        pltpu.make_async_copy(yt.at[j], solved_out.at[j], out_s.at[j]).start()

    def centre():
        @pl.when(row14 | row13)
        def _():
            got(tb.at[0], tb_r.at[0])

            @pl.when(row13)
            def _():
                got(tb.at[1], tb_r.at[1])

            total = tb[0].astype(F32)
            total = total + jnp.where(row13, tb[1].astype(F32), 0.0)
            summed = total.astype(BF16).astype(F32)
            piece = (ut[rows(c, PIECE)].astype(F32) - summed).astype(BF16)
            wg[x, yl, e] = piece
            block = wg.at[x, yl, e]

            def one(k):
                to = lax.rem(2 * x + yl + 1 + k, 8)
                remote(block, block, ag_s, ag_r.at[x], r, 2 * to + e).start()

            loop(7, one)

    def gather():
        @pl.when(row14 | row13)
        def _():
            def one(step):
                chunk = lax.rem(5 - step, 4)

                @pl.when(chunk == x)
                def _():
                    got(wg.at[chunk, 0, e], ag_r.at[chunk])

                @pl.when(chunk != x)
                def _():
                    got(wg.at[chunk, :, e], ag_r.at[chunk])

                block = wg.at[chunk, :, e]
                remote(block, block, sib_s.at[chunk], sib_r.at[chunk], r, c + 1 - 2 * e).start()

            loop(4, one)

    def solve():
        @pl.when(row14 | row13)
        def _():
            def one(step):
                chunk = lax.rem(5 - step, 4)
                part = rows(chunk, CHUNK)
                got(wg.at[chunk, :, 1 - e], sib_r.at[chunk])
                answer = product(wg[chunk].reshape(CHUNK, NB), dv[...])
                vf[part] = answer

                @pl.when((c < r) & jnp.logical_not(back1))
                def _():
                    qf[part] = product(answer.astype(BF16), lv[...]).astype(BF16)
                    scatter_qf(chunk)

            loop(4, one)

            @pl.when(back1)
            def _():
                loop(4, scatter_qf)

    @pl.when(chain1)
    def _():
        def one(step):
            chunk = 3 - step
            part = rows(chunk, CHUNK)
            got(yc.at[part], yc_r.at[chunk])
            partial = product(yc[part], lt[...]).astype(BF16)
            pf[part] = partial
            residue = (bt[part].astype(F32) - partial.astype(F32)).astype(BF16)
            yr[part] = product(residue, dt[...]).astype(BF16)
            remote(yr.at[part], yc.at[part], ch_s.at[chunk], yc_r.at[chunk], 2, 1).start()
            for k in range(4):
                pl.when(chunk == k)(lambda: scatter_s1(1, k))

        loop(4, one)

    @pl.when(chain20)
    def _():
        def one(step):
            chunk = 3 - step
            part = rows(chunk, CHUNK)
            got(yc.at[part], yc_r.at[chunk])
            pf[part] = product(yc[part], lt[...]).astype(BF16)
            remote(pf.at[part], pc.at[part], pc_s.at[chunk], pc_r.at[chunk], 2, 1).start()

        loop(4, one)

    @pl.when(chain2)
    def _():
        def one(step):
            chunk = 3 - step
            part = rows(chunk, CHUNK)
            got(yc.at[part], yc_r.at[chunk])
            partial = product(yc[part], lt[...]).astype(BF16)
            got(pc.at[part], pc_r.at[chunk])
            total = pc[part].astype(F32) + partial.astype(F32)
            pf[part] = total.astype(BF16)
            residue = (bt[part].astype(F32) - total).astype(BF16)
            yr[part] = product(residue, dt[...]).astype(BF16)
            for k in range(4):
                pl.when(chunk == k)(lambda: scatter_s1(2, k))

        loop(4, one)

    @pl.when(back1)
    def _():
        def one(step):
            chunk = lax.rem(5 - step, 4)
            part = rows(chunk, CHUNK)
            got(qc.at[part], qc_r.at[chunk])
            centred = (ut[part].astype(F32) - qc[part].astype(F32)).astype(BF16)
            answer = product(centred, dv[...]).astype(BF16)
            qf[part] = product(answer, lv[...]).astype(BF16)
            for k in range(4):
                send_t(1, 13)(4 * chunk + k)

        loop(4, one)

    spread(0)

    @pl.when(row15 & (c < 15))
    def _():
        loop(4, scatter_qf)

    spread(1)
    centre()
    collect(0)
    apply(0)
    gather()
    spread(2)
    solve()

    @pl.when(chain1 | chain2)
    def _():
        loop(4, scatter_pf)

    collect(1)
    apply(1)
    collect(2)
    done = pltpu.make_async_copy(vf, solution_out, out_s.at[3])
    pl.when(late)(done.start)
    apply(2)

    rest_out[...] = bt[rows(c, PIECE)].astype(F32)
    for j in range(STEPS):

        @pl.when((r == 1) if j == 0 else (r > j))
        def _():
            @pl.when(c == j)
            def _():
                rest_out[...] -= pf[rows(c, PIECE)].astype(F32)

            @pl.when(c != j)
            def _():
                got(rp.at[j], rp_r.at[j])
                rest_out[...] -= rp[j].astype(F32)

    back_out[...] = jnp.zeros_like(back_out)
    for j in range(STEPS):

        @pl.when(c < 13 + j)
        def _():
            @pl.when(r == 13 + j)
            def _():
                back_out[...] += qf[rows(r, PIECE)].astype(F32)

            @pl.when(r != 13 + j)
            def _():
                got(qr.at[j], qr_r.at[j])
                back_out[...] += qr[j].astype(F32)

    side = pl.ds(0, HALF)
    for j in range(STEPS):
        sent(yt.at[j, pl.ds(0, 192), side], s3_s.at[j])
        sent(yt.at[j, :, side], s4_s.at[j])
        with_children(j, lambda children: sent(yt.at[j, pl.ds(0, len(children) * CHUNK), side], s2_s.at[j]))

    @pl.when(((z == 1) | (z == 2)) & first)
    def _():
        sent(yt.at[0, pl.ds(0, 192), side], s1b_s)

    @pl.when(row0)
    def _():
        @pl.when(to_one | to_two)
        def _():
            sent(yr.at[pl.ds(0, CHUNK)], y0_s)

        sent(yr.at[pl.ds(0, CHUNK), side], s1_s.at[0])

    @pl.when(chain1 | chain2)
    def _():
        sent(yr.at[pl.ds(0, CHUNK), side], s1_s.at[0])
        for k in range(1, 4):
            sent(yr.at[pl.ds(0, 2 * CHUNK), side], s1_s.at[k])

    @pl.when(chain1)
    def _():
        for k in range(4):
            sent(yr.at[pl.ds(0, CHUNK)], ch_s.at[k])

    @pl.when((c == 0) & (r >= 2))
    def _():
        for k in range(4):
            sent(pf.at[pl.ds(0, CHUNK)], pc_s.at[k])

    @pl.when(chain1 | ((c == 1) & (r >= 2)) | ((c == 2) & (r >= 3)))
    def _():
        sent(pf.at[pl.ds(0, 240)], pf_s)

    @pl.when(late & (c < r))
    def _():
        sent(qf.at[pl.ds(0, 240)], qf_s)

    @pl.when((row15 & ((c == 14) | (c == 13))) | back1)
    def _():
        sent(qf, tb_s)

    @pl.when(row14 | row13)
    def _():
        sent(qf.at[pl.ds(0, 112)], ag_s)
        for k in range(4):
            sent(wg.at[0, :, 0], sib_s.at[k])

    for j in range(STEPS):
        pltpu.make_async_copy(yt.at[j], solved_out.at[j], out_s.at[j]).wait()
    pl.when(late)(done.wait)


def hand_over(yt, rest, back, vf, solved_out, rest_out, back_out, solution_out, yv, so, rv, bv, sv, sl, in_s, out_s):
    late = lax.axis_index("row") >= 13
    loads = [pltpu.make_async_copy(yt.at[j], yv.at[j], in_s.at[j]) for j in range(STEPS)]
    loads += [pltpu.make_async_copy(rest, rv, in_s.at[3]), pltpu.make_async_copy(back, bv, in_s.at[4])]
    for load in loads:
        load.start()
    extra = pltpu.make_async_copy(vf, sv, in_s.at[5])
    pl.when(late)(extra.start)
    answer = pltpu.make_async_copy(sl, solution_out, out_s.at[5])

    @pl.when(jnp.logical_not(late))
    def _():
        sl[...] = jnp.zeros_like(sl)
        answer.start()

    stores = []
    for j in range(STEPS):
        whole = pl.ds(j * NB, NB)
        loads[j].wait()
        so[whole] = yv[j].T
        stores.append(pltpu.make_async_copy(so.at[whole], solved_out.at[whole], out_s.at[j]))
        stores[-1].start()
    for k, (source, target) in enumerate(((rv, rest_out), (bv, back_out))):
        loads[3 + k].wait()
        stores.append(pltpu.make_async_copy(source, target, out_s.at[3 + k]))
        stores[-1].start()

    @pl.when(late)
    def _():
        extra.wait()
        sl[...] = sv[...].T
        answer.start()

    for store in stores:
        store.wait()
    answer.wait()


def local(factor, diag_inv, rhs, forward_values):
    anywhere = pl.BlockSpec(memory_space=pl.ANY)
    vmem = pl.BlockSpec(memory_space=pltpu.VMEM)
    dma = pltpu.SemaphoreType.DMA
    square = pltpu.VMEM((NB, NB), BF16)
    tall = pltpu.VMEM((NB, COLS), BF16)
    wide = pltpu.VMEM((COLS, NB), BF16)
    piece = pltpu.VMEM((PIECE, NB), F32)
    results = pl.pallas_call(
        kernel,
        name="solves",
        out_shape=(
            jax.ShapeDtypeStruct((STEPS, COLS, NB), BF16),
            jax.ShapeDtypeStruct((PIECE, NB), F32),
            jax.ShapeDtypeStruct((PIECE, NB), F32),
            jax.ShapeDtypeStruct((COLS, NB), F32),
        ),
        in_specs=[anywhere] * 4,
        out_specs=(anywhere, vmem, vmem, anywhere),
        scratch_shapes=[
            square, square, tall, tall, square, square, wide, wide,
            pltpu.VMEM((STEPS, COLS, NB), BF16),
            wide, wide, wide, wide,
            pltpu.VMEM((STEPS, PIECE, NB), BF16),
            wide,
            pltpu.VMEM((STEPS, PIECE, NB), BF16),
            wide,
            pltpu.VMEM((2, PIECE, NB), BF16),
            pltpu.VMEM((4, 2, 2, PIECE, NB), BF16),
            pltpu.VMEM((COLS, NB), F32),
            wide,
            pltpu.SemaphoreType.REGULAR((3,)), dma((4,)), dma((4,)),
            dma((4,)), dma((4,)), dma((3,)), dma((3, 4)), dma((3, 4)), dma((3,)), dma((3,)), dma((4,)), dma((2,)),
            dma((4,)), dma((4,)),
            dma(()), dma((4,)), dma(()), dma((3,)), dma((3,)), dma((3,)), dma(()), dma((4,)), dma((4,)),
            dma(()), dma((4,)), dma(()), dma(()), dma((4,)),
        ],
        compiler_params=pltpu.CompilerParams(
            collective_id=0, has_side_effects=True, vmem_limit_bytes=60 * 1024 * 1024
        ),
    )(factor, diag_inv, rhs, forward_values)
    solved, rest, back, answer = pl.pallas_call(
        hand_over,
        name="hand_over",
        out_shape=(
            jax.ShapeDtypeStruct((STEPS * NB, COLS), BF16),
            jax.ShapeDtypeStruct((PIECE, NB), F32),
            jax.ShapeDtypeStruct((PIECE, NB), F32),
            jax.ShapeDtypeStruct((NB, COLS), F32),
        ),
        in_specs=[anywhere] * 4,
        out_specs=(anywhere,) * 4,
        scratch_shapes=[
            pltpu.VMEM((STEPS, COLS, NB), BF16), pltpu.VMEM((STEPS * NB, COLS), BF16), piece, piece,
            pltpu.VMEM((COLS, NB), F32), pltpu.VMEM((NB, COLS), F32), dma((6,)), dma((6,)),
        ],
        compiler_params=pltpu.CompilerParams(vmem_limit_bytes=60 * 1024 * 1024),
    )(*results)
    return solved, rest.T, back.T, answer


def solution(mesh):
    placed = (P("row", "col"), P("row", None), P("row", None), P("row", None))
    return jax.shard_map(
        local,
        mesh=mesh,
        in_specs=placed,
        out_specs=(P(), P("row", "col"), P("col", "row"), P("row", None)),
        check_vma=False,
    )
```

```python
import jax
import jax.numpy as jnp
from jax import lax
from jax.experimental import pallas as pl
from jax.experimental.pallas import tpu as pltpu
from jax.sharding import PartitionSpec as P

NB = 1024
COLS = 256
STEPS = 3
NROW = 16
NCOL = 16
PIECE = 16
CHUNK = 64
HALF = 512
SIDE = (0, 0, 1)
MESH = pl.DeviceIdType.MESH
F32 = jnp.float32
BF16 = jnp.bfloat16


def product(left, right):
    return lax.dot_general(left, right, (((1,), (0,)), ((), ())), preferred_element_type=F32)


def loop(count, body):
    def step(index, carry):
        body(index)
        return carry

    lax.fori_loop(0, count, step, 0)


def kernel(
    factor, inverse, rhs, start,
    solved_out, rest_out, back_out, solution_out,
    lv, dv, bv, uv, lt, dt, bt, ut,
    yt, yc, pc, yr, pf, rp, qf, qr, qc, tb, wg, wl, vf, vb,
    ready, ld_s, out_s,
    yc_r, pc_r, own_r, s3_r, s4_r, rp_r, qr_r, qc_r, tb_r, ag_r, sib_r,
    y0_s, s1_s, s1b_s, s2_s, s3_s, s4_s, pf_s, ch_s, pc_s, qf_s, qc_s, tb_s, w_s, ag_s, sib_s,
):
    r = lax.axis_index("row")
    c = lax.axis_index("col")
    x = c // 4
    yl = (c // 2) % 2
    e = c % 2
    yh = r // 8
    z = r % 8
    y = 2 * yh + yl
    row0 = r == 0
    chain1 = (r == 1) & (c == 0)
    chain20 = (r == 2) & (c == 0)
    chain2 = (r == 2) & (c == 1)
    row13 = r == 13
    row14 = r == 14
    row15 = r == 15
    late = r >= 13
    back1 = (r == 14) & (c == 13)
    group = 2 * (x % 2) + y % 2
    mine = pl.ds(pl.multiple_of(group * CHUNK, CHUNK), CHUNK)

    def remote(src, dst, send, recv, row, col):
        return pltpu.make_async_remote_copy(
            src_ref=src, dst_ref=dst, send_sem=send, recv_sem=recv, device_id=(row, col), device_id_type=MESH
        )

    def got(ref, sem):
        remote(ref, ref, sem, sem, r, c).wait_recv()

    def sent(ref, sem):
        remote(ref, ref, sem, sem, r, c).wait_send()

    def rows(index, count):
        return pl.ds(pl.multiple_of(index * count, count), count)

    uses_l = ((c < STEPS) & (r > c)) | (late & (c < r))
    uses_d = row0 | chain1 | chain2 | late
    needs = (uses_d, r >= 0, uses_l, late)
    pairs = ((inverse, dv), (rhs, bv), (factor, lv), (start, uv))
    loads = [pltpu.make_async_copy(source, target, ld_s.at[k]) for k, (source, target) in enumerate(pairs)]
    for need, load in zip(needs, loads):
        pl.when(need)(load.start)
    barrier = pltpu.get_barrier_semaphore()

    def greet(row, col):
        pl.semaphore_signal(barrier, inc=1, device_id=(row, col), device_id_type=MESH)

    def greet_other(row, col):
        pl.when((row != r) | (col != c))(lambda: greet(row, col))

    @pl.when(chain1)
    def _():
        for col in (0, 2, 4, 12):
            greet(0, col)

    @pl.when(chain20)
    def _():
        for col in (6, 8, 13, 14):
            greet(0, col)

    @pl.when(chain2)
    def _():
        greet(1, 0)

    greet(r, c + 1 - 2 * e)
    loop(7, lambda k: greet(r, lax.rem(c + 2 + 2 * k, 16)))
    loop(8, lambda k: greet(lax.rem(r + 8, 16), 2 * k + e))
    pl.when((r == 1) & (c != 0))(lambda: greet(1, 0))
    pl.when(c != 1)(lambda: greet(r, 1))
    pl.when(c != 2)(lambda: greet(r, 2))
    pl.when(r != 13)(lambda: greet(13, c))
    pl.when(r != 14)(lambda: greet(14, c))
    pl.when(r != 15)(lambda: greet(15, c))

    def depth(j):
        return lax.rem(z - j + 8, 8)

    def column(j, far):
        return yh * 8 + lax.rem(far + j, 8)

    def with_children(j, run):
        for parent, children in ((0, (3, 7, 1)), (3, (4, 2)), (7, (6,)), (6, (5,))):

            @pl.when(depth(j) == parent)
            def _():
                run(children)

    for j in range(STEPS):

        @pl.when(e == SIDE[j])
        def _():
            with_children(j, lambda children: [greet(column(j, far), c) for far in children])

    @pl.when(row14 & (c != 13))
    def _():
        greet(14, 13)

    @pl.when(row13 & (c != 13))
    def _():
        greet(14, 13)

    @pl.when(back1)
    def _():
        greet(15, 14)

    pl.when(uses_d)(loads[0].wait)
    loads[1].wait()

    @pl.when(row0)
    def _():
        value = jnp.dot(dv[...], bv[...], preferred_element_type=F32)
        yr[...] = value.astype(BF16).T

    bt[...] = bv[...].T
    pl.when(uses_l)(loads[2].wait)

    @pl.when(late)
    def _():
        loads[3].wait()
        ut[...] = uv[...].T

    @pl.when(row15)
    def _():
        value = product(ut[...], dv[...])
        vf[...] = value
        vb[...] = value.astype(BF16)

        @pl.when(c < 15)
        def _():
            qf[...] = product(vb[...], lv[...]).astype(BF16)

    @pl.when(chain1 | chain2)
    def _():
        dt[...] = dv[...].T

    @pl.when((c < 3) & (r > c))
    def _():
        lt[...] = lv[...].T

    def source_of(cols):
        found = c == cols[0]
        for col in cols[1:]:
            found = found | (c == col)
        return row0 & found

    to_one = source_of((0, 2, 4, 12))
    to_two = source_of((6, 8, 13, 14))
    count = 16 + jnp.where((c == 1) | (c == 2) | chain1, 15, 0) + jnp.where(late, 15, 0)
    count = count + jnp.where(e == 0, jnp.where(z < 2, 1, 2), jnp.where(z == 2, 0, 1))
    count = count + jnp.where(to_one | to_two | chain1 | (row15 & (c == 14)), 1, 0) + jnp.where(back1, 30, 0)
    pl.semaphore_wait(barrier, count)

    for j in range(STEPS):
        near = jnp.where(depth(j) == 5, 6, jnp.where(depth(j) == 6, 7, jnp.where((depth(j) == 4) | (depth(j) == 2), 3, 0)))

        @pl.when((e == SIDE[j]) & (depth(j) != 0))
        def _():
            pl.semaphore_signal(ready.at[j], inc=1, device_id=(column(j, near), c), device_id_type=MESH)

    def scatter_pf(chunk):
        for k in range(4):
            g = 4 * chunk + k

            @pl.when(g != c)
            def _():
                remote(pf.at[rows(g, PIECE)], rp.at[c], pf_s, rp_r.at[c], r, g).start()

    def scatter_qf(chunk, wanted=lambda h: True):
        for k in range(4):
            h = 4 * chunk + k

            @pl.when((h != r) & wanted(h))
            def _():
                remote(qf.at[rows(h, PIECE)], qr.at[r - 13], qf_s, qr_r.at[r - 13], h, c).start()

    @pl.when(row0)
    def _():
        for col, chunk in ((0, 3), (4, 2), (12, 1), (2, 0)):

            @pl.when(c == col)
            def _():
                part = pl.ds(chunk * CHUNK, CHUNK)
                remote(yr.at[part], yc.at[part], y0_s, yc_r.at[chunk], 1, 0).start()

        for col, chunk in ((6, 3), (8, 2), (14, 1), (13, 0)):

            @pl.when(c == col)
            def _():
                part = pl.ds(chunk * CHUNK, CHUNK)
                remote(yr.at[part], yc.at[part], y0_s, yc_r.at[chunk], 2, 0).start()

        @pl.when(e == SIDE[0])
        def _():
            other = 3 - y
            part = rows(2 * (x % 2) + other % 2, CHUNK)
            remote(yr.at[part], yt.at[0, part], s1_s.at[0], own_r.at[0, 0], 8, 4 * x + 2 * (other - 2) + e).start()
            yt[0, mine] = yr[mine]

    def send_back(target, recv):
        def one(step):
            chunk = lax.rem(5 - step, 4)
            part = rows(chunk, CHUNK)
            remote(qf.at[part], target.at[part], qc_s.at[chunk], recv.at[chunk], 14, 13).start()

        loop(4, one)

    pl.when(row15 & (c == 14))(lambda: send_back(qc, qc_r))
    pl.when(row15 & (c == 13))(lambda: send_back(pc, pc_r))

    def scatter_s1(j, chunk):
        part = rows(chunk, CHUNK)
        a, b = chunk // 2, chunk % 2
        if chunk == 0:
            yt[j, part] = yr[part]
            return
        for side in range(2):
            far = pl.ds(side * HALF, HALF)
            row = j + (8 * b if side else 0)
            col = (12 * a if side else 4 * a) + 2 * b + SIDE[j]
            remote(yr.at[part, far], yt.at[j, part, far], s1_s.at[chunk], own_r.at[j, side], row, col).start()

    halves = (pl.ds(0, HALF), pl.ds(HALF, HALF))
    heads = ((x < 2) & (y < 2), ((x == 0) | (x == 3)) & ((y == 0) | (y == 3)))

    def spread(j):
        block = yt.at[j, mine]
        parts = [yt.at[j, mine, side] for side in halves]
        local = (row0 & (j == 0)) | (chain1 & (j == 1)) | (chain2 & (j == 2))
        starts = (z == j) & (j > 0)

        def to_chip(part, send, recv, tx, ty):
            remote(part, part, send, recv, 8 * (ty // 2) + z, 4 * tx + 2 * (ty % 2) + e).start()

        for k in range(2):

            @pl.when(starts & heads[k])
            def _():
                @pl.when(jnp.logical_not(local))
                def _():
                    got(parts[k], own_r.at[j, k])

                x2, y2 = lax.rem(x + 2, 4), lax.rem(y + 2, 4)
                to_chip(parts[k], s1b_s.at[k], own_r.at[j, k], x2, y2)
                to_chip(parts[k], s1b_s.at[k], own_r.at[j, k], x2, y)
                to_chip(parts[k], s1b_s.at[k], own_r.at[j, k], x, y2)

        for k in range(2):

            @pl.when(starts & jnp.logical_not(heads[k]))
            def _():
                got(parts[k], own_r.at[j, k])

        @pl.when(jnp.logical_not(starts | local))
        def _():
            got(block, own_r.at[j, 0])

        for k in range(2):
            x1, y1 = lax.rem(x + 1 + 2 * k, 4), lax.rem(y + 1 + 2 * k, 4)
            to_chip(parts[k], s3_s.at[j], s3_r.at[j, group], x1, y1)
            to_chip(parts[k], s3_s.at[j], s3_r.at[j, group], x1, y)
            to_chip(parts[k], s3_s.at[j], s3_r.at[j, group], x, y1)
        remote(block, block, s4_s.at[j], s4_r.at[j, group], r, c + 1 - 2 * e).start()

        def run(children):
            pl.semaphore_wait(ready.at[j], len(children))
            for far in children:
                remote(block, block, s2_s.at[j], own_r.at[j, 0], column(j, far), c).start()

        with_children(j, run)

    def collect(j):
        def one(step):
            chunk = 3 - step
            block = yt.at[j, rows(chunk, CHUNK)]

            @pl.when(chunk != group)
            def _():
                got(block, s3_r.at[j, chunk])
                remote(block, block, s4_s.at[j], s4_r.at[j, chunk], r, c + 1 - 2 * e).start()

        loop(4, one)

    def apply(j):
        def one(step):
            chunk = 3 - step
            part = rows(chunk, CHUNK)

            @pl.when(e != SIDE[j])
            def _():
                got(yt.at[j, part], s4_r.at[j, chunk])

            @pl.when((c == j) & (r >= 3))
            def _():
                partial = product(yt[j, part], lt[...]).astype(BF16)
                if j == 1:
                    got(pc.at[part], pc_r.at[chunk])
                    partial = (pc[part].astype(F32) + partial.astype(F32)).astype(BF16)
                pf[part] = partial
                if j == 0:
                    remote(pf.at[part], pc.at[part], pc_s.at[chunk], pc_r.at[chunk], r, 1).start()
                else:
                    scatter_pf(chunk)

        loop(4, one)
        pltpu.make_async_copy(yt.at[j], solved_out.at[j], out_s.at[j]).start()

    def centre():
        block = wg.at[x, yl, e]

        @pl.when(row13)
        def _():
            got(tb, tb_r.at[0])
            block[...] = (ut[rows(c, PIECE)].astype(F32) - tb[...].astype(F32)).astype(BF16)

        @pl.when(row14 & (c != 13))
        def _():
            got(block, tb_r.at[0])

        @pl.when(row14 | row13)
        def _():
            def one(k):
                to = lax.rem(2 * x + yl + 1 + k, 8)
                remote(block, block, ag_s, ag_r.at[x], r, 2 * to + e).start()

            loop(7, one)

    def gather():
        @pl.when(row14 | row13)
        def _():
            def one(step):
                chunk = lax.rem(5 - step, 4)

                @pl.when(chunk == x)
                def _():
                    got(wg.at[chunk, 0, e], ag_r.at[chunk])

                @pl.when(chunk != x)
                def _():
                    got(wg.at[chunk, :, e], ag_r.at[chunk])

                block = wg.at[chunk, :, e]
                remote(block, block, sib_s.at[chunk], sib_r.at[chunk], r, c + 1 - 2 * e).start()

            loop(4, one)

    def solve():
        @pl.when(row14 | row13)
        def _():
            def one(step):
                chunk = lax.rem(5 - step, 4)
                part = rows(chunk, CHUNK)
                got(wg.at[chunk, :, 1 - e], sib_r.at[chunk])
                answer = product(wg[chunk].reshape(CHUNK, NB), dv[...])
                vf[part] = answer

                @pl.when((c < r) & jnp.logical_not(back1))
                def _():
                    qf[part] = product(answer.astype(BF16), lv[...]).astype(BF16)
                    scatter_qf(chunk)

            loop(4, one)

            @pl.when(back1)
            def _():
                loop(4, scatter_qf)

    @pl.when(chain1)
    def _():
        def one(step):
            chunk = 3 - step
            part = rows(chunk, CHUNK)
            got(yc.at[part], yc_r.at[chunk])
            partial = product(yc[part], lt[...]).astype(BF16)
            pf[part] = partial
            residue = (bt[part].astype(F32) - partial.astype(F32)).astype(BF16)
            yr[part] = product(residue, dt[...]).astype(BF16)
            remote(yr.at[part], yc.at[part], ch_s.at[chunk], yc_r.at[chunk], 2, 1).start()
            for k in range(4):
                pl.when(chunk == k)(lambda: scatter_s1(1, k))

        loop(4, one)

    @pl.when(chain20)
    def _():
        def one(step):
            chunk = 3 - step
            part = rows(chunk, CHUNK)
            got(yc.at[part], yc_r.at[chunk])
            pf[part] = product(yc[part], lt[...]).astype(BF16)
            remote(pf.at[part], pc.at[part], pc_s.at[chunk], pc_r.at[chunk], 2, 1).start()

        loop(4, one)

    @pl.when(chain2)
    def _():
        def one(step):
            chunk = 3 - step
            part = rows(chunk, CHUNK)
            got(yc.at[part], yc_r.at[chunk])
            partial = product(yc[part], lt[...]).astype(BF16)
            got(pc.at[part], pc_r.at[chunk])
            total = pc[part].astype(F32) + partial.astype(F32)
            pf[part] = total.astype(BF16)
            residue = (bt[part].astype(F32) - total).astype(BF16)
            yr[part] = product(residue, dt[...]).astype(BF16)
            for k in range(4):
                pl.when(chunk == k)(lambda: scatter_s1(2, k))

        loop(4, one)

    @pl.when(back1)
    def _():
        def one(step):
            chunk = lax.rem(5 - step, 4)
            part = rows(chunk, CHUNK)
            got(qc.at[part], qc_r.at[chunk])
            centred = (ut[part].astype(F32) - qc[part].astype(F32)).astype(BF16)
            wl[part] = centred
            answer = product(centred, dv[...]).astype(BF16)
            partial = product(answer, lv[...]).astype(BF16)
            qf[part] = partial
            got(pc.at[part], pc_r.at[chunk])
            yc[part] = (pc[part].astype(F32) + partial.astype(F32)).astype(BF16)
            for k in range(4):
                g = 4 * chunk + k
                remote(yc.at[rows(g, PIECE)], tb, tb_s, tb_r.at[0], 13, g).start()
            for k in range(4):
                piece = rows(4 * chunk + k, PIECE)
                target = wg.at[chunk, k // 2, k % 2]

                @pl.when(4 * chunk + k != c)
                def _():
                    remote(wl.at[piece], target, w_s, tb_r.at[0], 14, 4 * chunk + k).start()

                @pl.when(4 * chunk + k == c)
                def _():
                    target[...] = wl[piece]

        loop(4, one)

    middle = row13 | row14
    first_two = (jnp.where(z == 1, 1, 0), jnp.where(e == 1, 2, jnp.where(z == 1, 0, 1)))

    def below(h):
        return (h % 8 >= 4) & (h % 8 < 7)

    @pl.when((e == 0) & jnp.logical_not(row13))
    def _():
        spread(first_two[0])

    @pl.when(row15 & (c < 15))
    def _():
        loop(4, lambda chunk: scatter_qf(chunk, lambda h: jnp.logical_not(below(h))))

    centre()

    @pl.when(jnp.logical_not(middle))
    def _():
        spread(first_two[1])

    @pl.when(row15 & (c < 15))
    def _():
        loop(4, lambda chunk: scatter_qf(chunk, below))

    @pl.when((e == 0) & jnp.logical_not(middle))
    def _():
        collect(0)
        apply(0)

    gather()

    @pl.when(row13)
    def _():
        pl.when(e == 0)(lambda: spread(0))
        spread(first_two[1])

    solve()

    @pl.when(row14)
    def _():
        spread(first_two[1])

    @pl.when((e == 0) & middle)
    def _():
        collect(0)
        apply(0)

    @pl.when(chain1 | chain2)
    def _():
        loop(4, scatter_pf)

    @pl.when(e == 0)
    def _():
        collect(1)
        apply(1)

    @pl.when(e == 1)
    def _():
        collect(2)
        apply(0)
        apply(1)

    done = pltpu.make_async_copy(vf, solution_out, out_s.at[3])
    pl.when(late)(done.start)
    apply(2)

    for j in range(STEPS):

        @pl.when(e == SIDE[j])
        def _():
            sent(yt.at[j, pl.ds(0, 192)], s3_s.at[j])
            sent(yt.at[j], s4_s.at[j])
            with_children(j, lambda children: sent(yt.at[j, pl.ds(0, len(children) * CHUNK)], s2_s.at[j]))

    for k in range(2):

        @pl.when(((z == 1) & (e == 0) | (z == 2) & (e == 1)) & heads[k])
        def _():
            sent(yt.at[0, pl.ds(0, 192), halves[k]], s1b_s.at[k])

    @pl.when(row0)
    def _():
        @pl.when(to_one | to_two)
        def _():
            sent(yr.at[pl.ds(0, CHUNK)], y0_s)

        @pl.when(e == SIDE[0])
        def _():
            sent(yr.at[pl.ds(0, CHUNK)], s1_s.at[0])

    @pl.when(chain1 | chain2)
    def _():
        for k in range(1, 4):
            sent(yr.at[pl.ds(0, CHUNK)], s1_s.at[k])

    @pl.when(chain1)
    def _():
        for k in range(4):
            sent(yr.at[pl.ds(0, CHUNK)], ch_s.at[k])

    @pl.when((c == 0) & (r >= 2))
    def _():
        for k in range(4):
            sent(pf.at[pl.ds(0, CHUNK)], pc_s.at[k])

    @pl.when(chain1 | ((c == 1) & (r >= 2)) | ((c == 2) & (r >= 3)))
    def _():
        sent(pf.at[pl.ds(0, 240)], pf_s)

    @pl.when(late & (c < r))
    def _():
        sent(qf.at[pl.ds(0, 240)], qf_s)

    @pl.when(row15 & ((c == 13) | (c == 14)))
    def _():
        for k in range(4):
            sent(qf.at[pl.ds(0, CHUNK)], qc_s.at[k])

    @pl.when(back1)
    def _():
        sent(qf, tb_s)

    @pl.when(back1)
    def _():
        sent(qf.at[pl.ds(0, 240)], w_s)

    @pl.when(row14 | row13)
    def _():
        sent(qf.at[pl.ds(0, 112)], ag_s)
        for k in range(4):
            sent(wg.at[0, :, 0], sib_s.at[k])

    rest_out[...] = bt[rows(c, PIECE)].astype(F32)
    for j in range(STEPS):

        @pl.when((r == 1) if j == 0 else (r > j))
        def _():
            @pl.when(c == j)
            def _():
                rest_out[...] -= pf[rows(c, PIECE)].astype(F32)

            @pl.when(c != j)
            def _():
                got(rp.at[j], rp_r.at[j])
                rest_out[...] -= rp[j].astype(F32)

    back_out[...] = jnp.zeros_like(back_out)
    for j in range(STEPS):

        @pl.when(c < 13 + j)
        def _():
            @pl.when(r == 13 + j)
            def _():
                back_out[...] += qf[rows(r, PIECE)].astype(F32)

            @pl.when(r != 13 + j)
            def _():
                got(qr.at[j], qr_r.at[j])
                back_out[...] += qr[j].astype(F32)

    for j in range(STEPS):
        pltpu.make_async_copy(yt.at[j], solved_out.at[j], out_s.at[j]).wait()
    pl.when(late)(done.wait)


def hand_over(yt, rest, back, vf, solved_out, rest_out, back_out, solution_out, yv, so, rv, bv, sv, sl, in_s, out_s):
    late = lax.axis_index("row") >= 13
    loads = [pltpu.make_async_copy(yt.at[j], yv.at[j], in_s.at[j]) for j in range(STEPS)]
    loads += [pltpu.make_async_copy(rest, rv, in_s.at[3]), pltpu.make_async_copy(back, bv, in_s.at[4])]
    for load in loads:
        load.start()
    extra = pltpu.make_async_copy(vf, sv, in_s.at[5])
    pl.when(late)(extra.start)
    answer = pltpu.make_async_copy(sl, solution_out, out_s.at[5])

    @pl.when(jnp.logical_not(late))
    def _():
        sl[...] = jnp.zeros_like(sl)
        answer.start()

    stores = []
    for j in range(STEPS):
        whole = pl.ds(j * NB, NB)
        loads[j].wait()
        so[whole] = yv[j].T
        stores.append(pltpu.make_async_copy(so.at[whole], solved_out.at[whole], out_s.at[j]))
        stores[-1].start()
    for k, (source, target) in enumerate(((rv, rest_out), (bv, back_out))):
        loads[3 + k].wait()
        stores.append(pltpu.make_async_copy(source, target, out_s.at[3 + k]))
        stores[-1].start()

    @pl.when(late)
    def _():
        extra.wait()
        sl[...] = sv[...].T
        answer.start()

    for store in stores:
        store.wait()
    answer.wait()


def local(factor, diag_inv, rhs, forward_values):
    anywhere = pl.BlockSpec(memory_space=pl.ANY)
    vmem = pl.BlockSpec(memory_space=pltpu.VMEM)
    dma = pltpu.SemaphoreType.DMA
    square = pltpu.VMEM((NB, NB), BF16)
    tall = pltpu.VMEM((NB, COLS), BF16)
    wide = pltpu.VMEM((COLS, NB), BF16)
    piece = pltpu.VMEM((PIECE, NB), F32)
    results = pl.pallas_call(
        kernel,
        name="solves",
        out_shape=(
            jax.ShapeDtypeStruct((STEPS, COLS, NB), BF16),
            jax.ShapeDtypeStruct((PIECE, NB), F32),
            jax.ShapeDtypeStruct((PIECE, NB), F32),
            jax.ShapeDtypeStruct((COLS, NB), F32),
        ),
        in_specs=[anywhere] * 4,
        out_specs=(anywhere, vmem, vmem, anywhere),
        scratch_shapes=[
            square, square, tall, tall, square, square, wide, wide,
            pltpu.VMEM((STEPS, COLS, NB), BF16),
            wide, wide, wide, wide,
            pltpu.VMEM((STEPS, PIECE, NB), BF16),
            wide,
            pltpu.VMEM((STEPS, PIECE, NB), BF16),
            wide,
            pltpu.VMEM((PIECE, NB), BF16),
            pltpu.VMEM((4, 2, 2, PIECE, NB), BF16),
            wide,
            pltpu.VMEM((COLS, NB), F32),
            wide,
            pltpu.SemaphoreType.REGULAR((3,)), dma((4,)), dma((4,)),
            dma((4,)), dma((4,)), dma((3, 2)), dma((3, 4)), dma((3, 4)), dma((3,)), dma((3,)), dma((4,)), dma((2,)),
            dma((4,)), dma((4,)),
            dma(()), dma((4,)), dma((2,)), dma((3,)), dma((3,)), dma((3,)), dma(()), dma((4,)), dma((4,)),
            dma(()), dma((4,)), dma(()), dma(()), dma(()), dma((4,)),
        ],
        compiler_params=pltpu.CompilerParams(
            collective_id=0, has_side_effects=True, vmem_limit_bytes=60 * 1024 * 1024
        ),
    )(factor, diag_inv, rhs, forward_values)
    solved, rest, back, answer = pl.pallas_call(
        hand_over,
        name="hand_over",
        out_shape=(
            jax.ShapeDtypeStruct((STEPS * NB, COLS), BF16),
            jax.ShapeDtypeStruct((PIECE, NB), F32),
            jax.ShapeDtypeStruct((PIECE, NB), F32),
            jax.ShapeDtypeStruct((NB, COLS), F32),
        ),
        in_specs=[anywhere] * 4,
        out_specs=(anywhere,) * 4,
        scratch_shapes=[
            pltpu.VMEM((STEPS, COLS, NB), BF16), pltpu.VMEM((STEPS * NB, COLS), BF16), piece, piece,
            pltpu.VMEM((COLS, NB), F32), pltpu.VMEM((NB, COLS), F32), dma((6,)), dma((6,)),
        ],
        compiler_params=pltpu.CompilerParams(vmem_limit_bytes=60 * 1024 * 1024),
    )(*results)
    return solved, rest.T, back.T, answer


def solution(mesh):
    placed = (P("row", "col"), P("row", None), P("row", None), P("row", None))
    return jax.shard_map(
        local,
        mesh=mesh,
        in_specs=placed,
        out_specs=(P(), P("row", "col"), P("col", "row"), P("row", None)),
        check_vma=False,
    )
```

```python
import jax
import jax.numpy as jnp
from jax import lax
from jax.experimental import pallas as pl
from jax.experimental.pallas import tpu as pltpu
from jax.sharding import PartitionSpec as P

NB = 1024
COLS = 256
STEPS = 3
NROW = 16
NCOL = 16
PIECE = 16
CHUNK = 64
HALF = 512
SIDE = (0, 0, 1)
MESH = pl.DeviceIdType.MESH
F32 = jnp.float32
BF16 = jnp.bfloat16


def product(left, right):
    return lax.dot_general(left, right, (((1,), (0,)), ((), ())), preferred_element_type=F32)


def loop(count, body):
    def step(index, carry):
        body(index)
        return carry

    lax.fori_loop(0, count, step, 0)


def kernel(
    factor, inverse, rhs, start,
    yt, rest_out, back_out, vf,
    lv, dv, bv, uv, lt, dt, bt, ut,
    yc, pc, yr, pf, rp, qf, qr, qc, tb, wg, wl, vb,
    ready, ld_s,
    yc_r, pc_r, own_r, s3_r, s4_r, rp_r, qr_r, qc_r, tb_r, ag_r, sib_r,
    y0_s, s1_s, s1b_s, s2_s, s3_s, s4_s, pf_s, ch_s, pc_s, qf_s, qc_s, tb_s, w_s, ag_s, sib_s,
):
    r = lax.axis_index("row")
    c = lax.axis_index("col")
    x = c // 4
    yl = (c // 2) % 2
    e = c % 2
    yh = r // 8
    z = r % 8
    y = 2 * yh + yl
    row0 = r == 0
    chain1 = (r == 1) & (c == 0)
    chain20 = (r == 2) & (c == 0)
    chain2 = (r == 2) & (c == 1)
    row13 = r == 13
    row14 = r == 14
    row15 = r == 15
    late = r >= 13
    back1 = (r == 14) & (c == 13)
    group = 2 * (x % 2) + y % 2
    halves = (pl.ds(0, HALF), pl.ds(HALF, HALF))
    mine = pl.ds(pl.multiple_of(group * CHUNK, CHUNK), CHUNK)

    def remote(src, dst, send, recv, row, col):
        return pltpu.make_async_remote_copy(
            src_ref=src, dst_ref=dst, send_sem=send, recv_sem=recv, device_id=(row, col), device_id_type=MESH
        )

    def got(ref, sem):
        remote(ref, ref, sem, sem, r, c).wait_recv()

    def sent(ref, sem):
        remote(ref, ref, sem, sem, r, c).wait_send()

    def rows(index, count):
        return pl.ds(pl.multiple_of(index * count, count), count)

    uses_l = ((c < STEPS) & (r > c)) | (late & (c < r))
    uses_d = row0 | chain1 | chain2 | late
    needs = (uses_d, r >= 0, uses_l, late)
    pairs = ((inverse, dv), (rhs, bv), (factor, lv), (start, uv))
    loads = [pltpu.make_async_copy(source, target, ld_s.at[k]) for k, (source, target) in enumerate(pairs)]
    for need, load in zip(needs, loads):
        pl.when(need)(load.start)
    barrier = pltpu.get_barrier_semaphore()

    def greet(row, col):
        pl.semaphore_signal(barrier, inc=1, device_id=(row, col), device_id_type=MESH)

    def greet_other(row, col):
        pl.when((row != r) | (col != c))(lambda: greet(row, col))

    @pl.when(chain1)
    def _():
        for col in (0, 2, 4, 12):
            greet(0, col)

    @pl.when(chain20)
    def _():
        for col in (6, 8, 13, 14):
            greet(0, col)

    @pl.when(chain2)
    def _():
        greet(1, 0)

    greet(r, c + 1 - 2 * e)
    loop(7, lambda k: greet(r, lax.rem(c + 2 + 2 * k, 16)))
    loop(8, lambda k: greet(lax.rem(r + 8, 16), 2 * k + e))
    pl.when((r == 1) & (c != 0))(lambda: greet(1, 0))
    pl.when(c != 1)(lambda: greet(r, 1))
    pl.when(c != 2)(lambda: greet(r, 2))
    pl.when(r != 13)(lambda: greet(13, c))
    pl.when(r != 14)(lambda: greet(14, c))
    pl.when(r != 15)(lambda: greet(15, c))

    def depth(j):
        return lax.rem(z - j + 8, 8)

    def column(j, far):
        return yh * 8 + lax.rem(far + j, 8)

    def with_children(j, run):
        for parent, children in ((0, (2, 7, 1)), (2, (4, 3)), (7, (6,)), (6, (5,))):

            @pl.when(depth(j) == parent)
            def _():
                run(children)

    for j in range(STEPS):

        @pl.when(e == SIDE[j])
        def _():
            with_children(j, lambda children: [greet(column(j, far), c) for far in children])

    @pl.when(row14 & (c != 13))
    def _():
        greet(14, 13)

    @pl.when(row13 & (c != 13))
    def _():
        greet(14, 13)

    @pl.when(back1)
    def _():
        greet(15, 14)

    pl.when(uses_d)(loads[0].wait)

    @pl.when(row0)
    def _():
        loads[1].wait()
        value = jnp.dot(dv[...], bv[...], preferred_element_type=F32)
        yr[...] = value.astype(BF16).T

    @pl.when(late)
    def _():
        loads[3].wait()
        ut[...] = uv[...].T

    @pl.when(row15)
    def _():
        value = product(ut[...], dv[...])
        vf[...] = value
        vb[...] = value.astype(BF16)

    pl.when(uses_l)(loads[2].wait)

    @pl.when(chain1 | chain2)
    def _():
        dt[...] = dv[...].T

    @pl.when((c < 3) & (r > c))
    def _():
        lt[...] = lv[...].T

    def source_of(cols):
        found = c == cols[0]
        for col in cols[1:]:
            found = found | (c == col)
        return row0 & found

    to_one = source_of((0, 2, 4, 12))
    to_two = source_of((6, 8, 13, 14))
    count = 16 + jnp.where((c == 1) | (c == 2) | chain1, 15, 0) + jnp.where(late, 15, 0)
    count = count + jnp.where(e == 0, jnp.where(z < 2, 1, 2), jnp.where(z == 2, 0, 1))
    count = count + jnp.where(to_one | to_two | chain1 | (row15 & (c == 14)), 1, 0) + jnp.where(back1, 30, 0)
    pl.semaphore_wait(barrier, count)

    for j in range(STEPS):
        near = jnp.where(depth(j) == 5, 6, jnp.where(depth(j) == 6, 7, jnp.where((depth(j) == 4) | (depth(j) == 3), 2, 0)))

        @pl.when((e == SIDE[j]) & (depth(j) != 0))
        def _():
            pl.semaphore_signal(ready.at[j], inc=1, device_id=(column(j, near), c), device_id_type=MESH)

    def scatter_pf(chunk):
        for k in range(4):
            g = 4 * chunk + k

            @pl.when(g != c)
            def _():
                remote(pf.at[rows(g, PIECE)], rp.at[c], pf_s, rp_r.at[c], r, g).start()

    def scatter_qf(chunk, wanted=lambda h: True):
        for k in range(4):
            h = 4 * chunk + k

            @pl.when((h != r) & wanted(h))
            def _():
                remote(qf.at[rows(h, PIECE)], qr.at[r - 13], qf_s, qr_r.at[r - 13], h, c).start()

    @pl.when(row0)
    def _():
        for col, chunk in ((0, 3), (4, 2), (12, 1), (2, 0)):

            @pl.when(c == col)
            def _():
                part = pl.ds(chunk * CHUNK, CHUNK)
                remote(yr.at[part], yc.at[part], y0_s, yc_r.at[chunk], 1, 0).start()

        for col, chunk in ((6, 3), (8, 2), (14, 1), (13, 0)):

            @pl.when(c == col)
            def _():
                part = pl.ds(chunk * CHUNK, CHUNK)
                remote(yr.at[part], yc.at[part], y0_s, yc_r.at[chunk], 2, 0).start()

        @pl.when(e == SIDE[0])
        def _():
            other = 3 - y
            part = rows(2 * (x % 2) + other % 2, CHUNK)
            for k, side in enumerate(halves):
                to = (8, 4 * x + 2 * (other - 2) + e)
                remote(yr.at[part, side], yt.at[0, part, side], s1_s.at[0], own_r.at[0, k], *to).start()
            yt[0, mine] = yr[mine]

    @pl.when(row15 & (c < 15))
    def _():
        def one(step):
            chunk = lax.rem(6 - step, 4)
            part = rows(chunk, CHUNK)
            qf[part] = product(vb[part], lv[...]).astype(BF16)
            for col, target, recv in ((14, qc, qc_r), (13, pc, pc_r)):

                @pl.when(c == col)
                def _():
                    remote(qf.at[part], target.at[part], qc_s.at[chunk], recv.at[chunk], 14, 13).start()

        loop(4, one)

    @pl.when(jnp.logical_not(row0))
    def _():
        loads[1].wait()

    bt[...] = bv[...].T

    def scatter_s1(j, chunk):
        part = rows(chunk, CHUNK)
        a, b = chunk // 2, chunk % 2
        if chunk == 0:
            yt[j, part] = yr[part]
            return
        for side in range(2):
            far = pl.ds(side * HALF, HALF)
            row = j + (8 * b if side else 0)
            col = (12 * a if side else 4 * a) + 2 * b + SIDE[j]
            remote(yr.at[part, far], yt.at[j, part, far], s1_s.at[chunk], own_r.at[j, side], row, col).start()

    heads = ((x < 2) & (y < 2), ((x == 0) | (x == 3)) & ((y == 0) | (y == 3)))

    def spread(j):
        local = (row0 & (j == 0)) | (chain1 & (j == 1)) | (chain2 & (j == 2))
        starts = (z == j) & (j > 0)
        turned = starts & heads[1] & jnp.logical_not(heads[0])

        for step in range(2):
            side = jnp.where(turned, 1 - step, step)
            part = yt.at[j, mine, pl.ds(pl.multiple_of(side * HALF, HALF), HALF)]

            def to_chip(send, recv, tx, ty):
                remote(part, part, send, recv, 8 * (ty // 2) + z, 4 * tx + 2 * (ty % 2) + e).start()

            @pl.when(jnp.logical_not(local))
            def _():
                got(part, own_r.at[j, side])

            @pl.when(starts & jnp.where(side == 0, heads[0], heads[1]))
            def _():
                x2, y2 = lax.rem(x + 2, 4), lax.rem(y + 2, 4)
                to_chip(s1b_s.at[side], own_r.at[j, side], x2, y2)
                to_chip(s1b_s.at[side], own_r.at[j, side], x2, y)
                to_chip(s1b_s.at[side], own_r.at[j, side], x, y2)

            def run(children):
                if step == 0:
                    pl.semaphore_wait(ready.at[j], len(children))
                for far in children:
                    remote(part, part, s2_s.at[j], own_r.at[j, side], column(j, far), c).start()

            with_children(j, run)
            x1, y1 = lax.rem(x + 1 + 2 * side, 4), lax.rem(y + 1 + 2 * side, 4)
            to_chip(s3_s.at[j], s3_r.at[j, group], x1, y1)
            to_chip(s3_s.at[j], s3_r.at[j, group], x1, y)
            to_chip(s3_s.at[j], s3_r.at[j, group], x, y1)

        block = yt.at[j, mine]
        remote(block, block, s4_s.at[j], s4_r.at[j, group], r, c + 1 - 2 * e).start()

    def collect(j):
        def one(step):
            chunk = 3 - step
            block = yt.at[j, rows(chunk, CHUNK)]

            @pl.when(chunk != group)
            def _():
                got(block, s3_r.at[j, chunk])
                remote(block, block, s4_s.at[j], s4_r.at[j, chunk], r, c + 1 - 2 * e).start()

        loop(4, one)

    def apply(j):
        def one(step):
            chunk = 3 - step
            part = rows(chunk, CHUNK)

            @pl.when(e != SIDE[j])
            def _():
                got(yt.at[j, part], s4_r.at[j, chunk])

            @pl.when((c == j) & (r >= 3))
            def _():
                partial = product(yt[j, part], lt[...]).astype(BF16)
                if j == 1:
                    got(pc.at[part], pc_r.at[chunk])
                    partial = (pc[part].astype(F32) + partial.astype(F32)).astype(BF16)
                pf[part] = partial
                if j == 0:
                    remote(pf.at[part], pc.at[part], pc_s.at[chunk], pc_r.at[chunk], r, 1).start()
                else:
                    scatter_pf(chunk)

        loop(4, one)

    def centre():
        block = wg.at[x, yl, e]

        @pl.when(row13)
        def _():
            got(tb, tb_r.at[0])
            block[...] = (ut[rows(c, PIECE)].astype(F32) - tb[...].astype(F32)).astype(BF16)

        @pl.when(row14 & (c != 13))
        def _():
            got(block, tb_r.at[0])

        @pl.when(row14 | row13)
        def _():
            def one(k):
                to = lax.rem(2 * x + yl + 1 + k, 8)
                remote(block, block, ag_s, ag_r.at[x], r, 2 * to + e).start()

            loop(7, one)

    def gather():
        @pl.when(row14 | row13)
        def _():
            def one(step):
                chunk = lax.rem(6 - step, 4)

                @pl.when(chunk == x)
                def _():
                    got(wg.at[chunk, 0, e], ag_r.at[chunk])

                @pl.when(chunk != x)
                def _():
                    got(wg.at[chunk, :, e], ag_r.at[chunk])

                block = wg.at[chunk, :, e]
                remote(block, block, sib_s.at[chunk], sib_r.at[chunk], r, c + 1 - 2 * e).start()

            loop(4, one)

    def solve():
        @pl.when(row14 | row13)
        def _():
            def one(step):
                chunk = lax.rem(6 - step, 4)
                part = rows(chunk, CHUNK)
                got(wg.at[chunk, :, 1 - e], sib_r.at[chunk])
                answer = product(wg[chunk].reshape(CHUNK, NB), dv[...])
                vf[part] = answer

                @pl.when((c < r) & jnp.logical_not(back1))
                def _():
                    qf[part] = product(answer.astype(BF16), lv[...]).astype(BF16)
                    scatter_qf(chunk)

            loop(4, one)

            @pl.when(back1)
            def _():
                loop(4, scatter_qf)

    @pl.when(chain1)
    def _():
        def one(step):
            chunk = 3 - step
            part = rows(chunk, CHUNK)
            got(yc.at[part], yc_r.at[chunk])
            partial = product(yc[part], lt[...]).astype(BF16)
            pf[part] = partial
            residue = (bt[part].astype(F32) - partial.astype(F32)).astype(BF16)
            yr[part] = product(residue, dt[...]).astype(BF16)
            remote(yr.at[part], yc.at[part], ch_s.at[chunk], yc_r.at[chunk], 2, 1).start()
            for k in range(4):
                pl.when(chunk == k)(lambda: scatter_s1(1, k))

        loop(4, one)

    @pl.when(chain20)
    def _():
        def one(step):
            chunk = 3 - step
            part = rows(chunk, CHUNK)
            got(yc.at[part], yc_r.at[chunk])
            pf[part] = product(yc[part], lt[...]).astype(BF16)
            remote(pf.at[part], pc.at[part], pc_s.at[chunk], pc_r.at[chunk], 2, 1).start()

        loop(4, one)

    @pl.when(chain2)
    def _():
        def one(step):
            chunk = 3 - step
            part = rows(chunk, CHUNK)
            got(yc.at[part], yc_r.at[chunk])
            partial = product(yc[part], lt[...]).astype(BF16)
            got(pc.at[part], pc_r.at[chunk])
            total = pc[part].astype(F32) + partial.astype(F32)
            pf[part] = total.astype(BF16)
            residue = (bt[part].astype(F32) - total).astype(BF16)
            yr[part] = product(residue, dt[...]).astype(BF16)
            for k in range(4):
                pl.when(chunk == k)(lambda: scatter_s1(2, k))

        loop(4, one)

    @pl.when(back1)
    def _():
        def one(step):
            chunk = lax.rem(6 - step, 4)
            part = rows(chunk, CHUNK)
            got(qc.at[part], qc_r.at[chunk])
            centred = (ut[part].astype(F32) - qc[part].astype(F32)).astype(BF16)
            wl[part] = centred
            answer = product(centred, dv[...]).astype(BF16)
            partial = product(answer, lv[...]).astype(BF16)
            qf[part] = partial
            got(pc.at[part], pc_r.at[chunk])
            yc[part] = (pc[part].astype(F32) + partial.astype(F32)).astype(BF16)
            for k in range(4):
                g = 4 * chunk + k
                remote(yc.at[rows(g, PIECE)], tb, tb_s, tb_r.at[0], 13, g).start()
            for k in range(4):
                piece = rows(4 * chunk + k, PIECE)
                target = wg.at[chunk, k // 2, k % 2]

                @pl.when(4 * chunk + k != c)
                def _():
                    remote(wl.at[piece], target, w_s, tb_r.at[0], 14, 4 * chunk + k).start()

                @pl.when(4 * chunk + k == c)
                def _():
                    target[...] = wl[piece]

        loop(4, one)

    middle = row13 | row14
    first_two = (jnp.where(z == 1, 1, 0), jnp.where(e == 1, 2, jnp.where(z == 1, 0, 1)))

    def below(h):
        return (h % 8 >= 4) & (h % 8 < 7)

    @pl.when((e == 0) & jnp.logical_not(row13))
    def _():
        spread(first_two[0])

    @pl.when(row15 & (c < 15))
    def _():
        loop(4, lambda chunk: scatter_qf(chunk, lambda h: jnp.logical_not(below(h))))

    centre()

    @pl.when(jnp.logical_not(middle))
    def _():
        spread(first_two[1])

    @pl.when(row15 & (c < 15))
    def _():
        loop(4, lambda chunk: scatter_qf(chunk, below))

    @pl.when((e == 0) & jnp.logical_not(middle))
    def _():
        collect(0)
        apply(0)

    gather()

    @pl.when((e == 0) & row13)
    def _():
        spread(0)

    solve()

    @pl.when(middle)
    def _():
        spread(first_two[1])

    @pl.when((e == 0) & middle)
    def _():
        collect(0)
        apply(0)

    @pl.when(chain1 | chain2)
    def _():
        loop(4, scatter_pf)

    @pl.when(e == 0)
    def _():
        collect(1)
        apply(1)

    @pl.when(e == 1)
    def _():
        collect(2)
        apply(0)
        apply(1)

    apply(2)

    for j in range(STEPS):

        @pl.when(e == SIDE[j])
        def _():
            sent(yt.at[j, pl.ds(0, 192)], s3_s.at[j])
            sent(yt.at[j], s4_s.at[j])
            with_children(j, lambda children: sent(yt.at[j, pl.ds(0, len(children) * CHUNK)], s2_s.at[j]))

    for k in range(2):

        @pl.when(((z == 1) & (e == 0) | (z == 2) & (e == 1)) & heads[k])
        def _():
            sent(yt.at[0, pl.ds(0, 192), halves[k]], s1b_s.at[k])

    @pl.when(row0)
    def _():
        @pl.when(to_one | to_two)
        def _():
            sent(yr.at[pl.ds(0, CHUNK)], y0_s)

        @pl.when(e == SIDE[0])
        def _():
            sent(yr.at[pl.ds(0, CHUNK)], s1_s.at[0])

    @pl.when(chain1 | chain2)
    def _():
        for k in range(1, 4):
            sent(yr.at[pl.ds(0, CHUNK)], s1_s.at[k])

    @pl.when(chain1)
    def _():
        for k in range(4):
            sent(yr.at[pl.ds(0, CHUNK)], ch_s.at[k])

    @pl.when((c == 0) & (r >= 2))
    def _():
        for k in range(4):
            sent(pf.at[pl.ds(0, CHUNK)], pc_s.at[k])

    @pl.when(chain1 | ((c == 1) & (r >= 2)) | ((c == 2) & (r >= 3)))
    def _():
        sent(pf.at[pl.ds(0, 240)], pf_s)

    @pl.when(late & (c < r))
    def _():
        sent(qf.at[pl.ds(0, 240)], qf_s)

    @pl.when(row15 & ((c == 13) | (c == 14)))
    def _():
        for k in range(4):
            sent(qf.at[pl.ds(0, CHUNK)], qc_s.at[k])

    @pl.when(back1)
    def _():
        sent(qf, tb_s)

    @pl.when(back1)
    def _():
        sent(qf.at[pl.ds(0, 240)], w_s)

    @pl.when(row14 | row13)
    def _():
        sent(qf.at[pl.ds(0, 112)], ag_s)
        for k in range(4):
            sent(wg.at[0, :, 0], sib_s.at[k])

    rest_out[...] = bt[rows(c, PIECE)].astype(F32)
    for j in range(STEPS):

        @pl.when((r == 1) if j == 0 else (r > j))
        def _():
            @pl.when(c == j)
            def _():
                rest_out[...] -= pf[rows(c, PIECE)].astype(F32)

            @pl.when(c != j)
            def _():
                got(rp.at[j], rp_r.at[j])
                rest_out[...] -= rp[j].astype(F32)

    back_out[...] = jnp.zeros_like(back_out)
    for j in range(STEPS):

        @pl.when(c < 13 + j)
        def _():
            @pl.when(r == 13 + j)
            def _():
                back_out[...] += qf[rows(r, PIECE)].astype(F32)

            @pl.when(r != 13 + j)
            def _():
                got(qr.at[j], qr_r.at[j])
                back_out[...] += qr[j].astype(F32)


def hand_over(yt, rest, back, vf, solved_out, rest_out, back_out, solution_out, so, sl, sems):
    late = lax.axis_index("row") >= 13
    answer = pltpu.make_async_copy(sl, solution_out, sems.at[5])
    stores = [pltpu.make_async_copy(rest, rest_out, sems.at[3]), pltpu.make_async_copy(back, back_out, sems.at[4])]
    for store in stores:
        store.start()

    @pl.when(jnp.logical_not(late))
    def _():
        sl[...] = jnp.zeros_like(sl)

    @pl.when(late)
    def _():
        sl[...] = vf[...].T

    answer.start()
    for j in range(STEPS):
        whole = pl.ds(j * NB, NB)
        so[whole] = yt[j].T
        stores.append(pltpu.make_async_copy(so.at[whole], solved_out.at[whole], sems.at[j]))
        stores[-1].start()
    for store in stores:
        store.wait()
    answer.wait()


def local(factor, diag_inv, rhs, forward_values):
    anywhere = pl.BlockSpec(memory_space=pl.ANY)
    vmem = pl.BlockSpec(memory_space=pltpu.VMEM)
    dma = pltpu.SemaphoreType.DMA
    square = pltpu.VMEM((NB, NB), BF16)
    tall = pltpu.VMEM((NB, COLS), BF16)
    wide = pltpu.VMEM((COLS, NB), BF16)
    results = pl.pallas_call(
        kernel,
        name="solves",
        out_shape=(
            pltpu.VMEM((STEPS, COLS, NB), BF16),
            pltpu.VMEM((PIECE, NB), F32),
            pltpu.VMEM((PIECE, NB), F32),
            pltpu.VMEM((COLS, NB), F32),
        ),
        in_specs=[anywhere] * 4,
        out_specs=(vmem,) * 4,
        scratch_shapes=[
            square, square, tall, tall, square, square, wide, wide,
            wide, wide, wide, wide,
            pltpu.VMEM((STEPS, PIECE, NB), BF16),
            wide,
            pltpu.VMEM((STEPS, PIECE, NB), BF16),
            wide,
            pltpu.VMEM((PIECE, NB), BF16),
            pltpu.VMEM((4, 2, 2, PIECE, NB), BF16),
            wide,
            wide,
            pltpu.SemaphoreType.REGULAR((3,)), dma((4,)),
            dma((4,)), dma((4,)), dma((3, 2)), dma((3, 4)), dma((3, 4)), dma((3,)), dma((3,)), dma((4,)), dma((2,)),
            dma((4,)), dma((4,)),
            dma(()), dma((4,)), dma((2,)), dma((3,)), dma((3,)), dma((3,)), dma(()), dma((4,)), dma((4,)),
            dma(()), dma((4,)), dma(()), dma(()), dma(()), dma((4,)),
        ],
        compiler_params=pltpu.CompilerParams(
            collective_id=0, has_side_effects=True, vmem_limit_bytes=60 * 1024 * 1024
        ),
    )(factor, diag_inv, rhs, forward_values)
    solved, rest, back, answer = pl.pallas_call(
        hand_over,
        name="hand_over",
        out_shape=(
            jax.ShapeDtypeStruct((STEPS * NB, COLS), BF16),
            jax.ShapeDtypeStruct((PIECE, NB), F32),
            jax.ShapeDtypeStruct((PIECE, NB), F32),
            jax.ShapeDtypeStruct((NB, COLS), F32),
        ),
        in_specs=[vmem] * 4,
        out_specs=(anywhere,) * 4,
        scratch_shapes=[pltpu.VMEM((STEPS * NB, COLS), BF16), pltpu.VMEM((NB, COLS), F32), dma((6,))],
        compiler_params=pltpu.CompilerParams(vmem_limit_bytes=32 * 1024 * 1024),
    )(*results)
    return solved, rest.T, back.T, answer


def solution(mesh):
    placed = (P("row", "col"), P("row", None), P("row", None), P("row", None))
    return jax.shard_map(
        local,
        mesh=mesh,
        in_specs=placed,
        out_specs=(P(), P("row", "col"), P("col", "row"), P("row", None)),
        check_vma=False,
    )
```

```python
import jax
import jax.numpy as jnp
from jax import lax
from jax.experimental import pallas as pl
from jax.experimental.pallas import tpu as pltpu
from jax.sharding import PartitionSpec as P

NB = 1024
COLS = 256
STEPS = 3
NROW = 16
NCOL = 16
PIECE = 16
CHUNK = 64
HALF = 512
SIDE = (0, 0, 1)
MESH = pl.DeviceIdType.MESH
F32 = jnp.float32
BF16 = jnp.bfloat16


def product(left, right):
    return lax.dot_general(left, right, (((1,), (0,)), ((), ())), preferred_element_type=F32)


def loop(count, body):
    def step(index, carry):
        body(index)
        return carry

    lax.fori_loop(0, count, step, 0)


def kernel(
    factor, inverse, rhs, start,
    yt, rest_out, back_out, vf,
    lv, dv, bv, uv, lt, dt, bt, ut,
    yc, pc, yr, pf, rp, qf, qr, qc, tb, wg, wl, vb,
    ready, joined, ld_s,
    yc_r, pc_r, own_r, s3_r, s4_r, rp_r, qr_r, qc_r, tb_r, ag_r, sib_r,
    y0_s, s1_s, s1b_s, s2_s, s3_s, s4_s, pf_s, ch_s, pc_s, qf_s, qc_s, tb_s, w_s, ag_s, sib_s,
):
    r = lax.axis_index("row")
    c = lax.axis_index("col")
    x = c // 4
    yl = (c // 2) % 2
    e = c % 2
    yh = r // 8
    z = r % 8
    y = 2 * yh + yl
    row0 = r == 0
    chain1 = (r == 1) & (c == 0)
    chain20 = (r == 2) & (c == 0)
    chain2 = (r == 2) & (c == 1)
    row13 = r == 13
    row14 = r == 14
    row15 = r == 15
    late = r >= 13
    back1 = (r == 14) & (c == 13)
    group = 2 * (x % 2) + y % 2
    halves = (pl.ds(0, HALF), pl.ds(HALF, HALF))
    mine = pl.ds(pl.multiple_of(group * CHUNK, CHUNK), CHUNK)

    def back_order(step):
        return jnp.where(step == 3, 3, lax.rem(2 * step, 3))

    def remote(src, dst, send, recv, row, col):
        return pltpu.make_async_remote_copy(
            src_ref=src, dst_ref=dst, send_sem=send, recv_sem=recv, device_id=(row, col), device_id_type=MESH
        )

    def got(ref, sem):
        remote(ref, ref, sem, sem, r, c).wait_recv()

    def sent(ref, sem):
        remote(ref, ref, sem, sem, r, c).wait_send()

    def rows(index, count):
        return pl.ds(pl.multiple_of(index * count, count), count)

    uses_l = ((c < STEPS) & (r > c)) | (late & (c < r))
    uses_d = row0 | chain1 | chain2 | late
    needs = (uses_d, r >= 0, uses_l, late)
    pairs = ((inverse, dv), (rhs, bv), (factor, lv), (start, uv))
    loads = [pltpu.make_async_copy(source, target, ld_s.at[k]) for k, (source, target) in enumerate(pairs)]
    for need, load in zip(needs, loads):
        pl.when(need)(load.start)
    def source_of(cols):
        found = c == cols[0]
        for col in cols[1:]:
            found = found | (c == col)
        return row0 & found

    to_one = source_of((1, 3, 5, 13))
    to_two = source_of((6, 8, 12, 14))
    barrier = pltpu.get_barrier_semaphore()

    def greet(row, col):
        pl.semaphore_signal(barrier, inc=1, device_id=(row, col), device_id_type=MESH)

    def is_early(row, col):
        return (row == 0) & ((col == 1) | (col == 3) | (col == 5) | (col == 13))

    def meet(run):
        run(r, c + 1 - 2 * e)
        loop(7, lambda k: run(r, lax.rem(c + 2 + 2 * k, 16)))
        loop(8, lambda k: run(lax.rem(r + 8, 16), 2 * k + e))

    def greet_late(row, col):
        pl.when(jnp.logical_not(is_early(row, col)))(lambda: greet(row, col))

    def join(row, col):
        @pl.when(is_early(row, col))
        def _():
            pl.semaphore_signal(joined, inc=1, device_id=(row, col), device_id_type=MESH)

    @pl.when(chain1)
    def _():
        for col in (1, 3, 5, 13):
            greet(0, col)

    @pl.when(chain20)
    def _():
        for col in (6, 8, 12, 14):
            greet(0, col)

    @pl.when(chain2)
    def _():
        greet(1, 0)

    meet(greet_late)
    pl.when((r == 1) & (c != 0))(lambda: greet(1, 0))
    pl.when((r > 0) & (c != 1))(lambda: greet(r, 1))
    pl.when((r > 0) & (c != 2))(lambda: greet(r, 2))
    pl.when(to_one)(lambda: greet(1, c))
    pl.when(r != 13)(lambda: greet(13, c))
    pl.when(r != 14)(lambda: greet(14, c))
    pl.when(r != 15)(lambda: greet(15, c))

    def depth(j):
        return lax.rem(z - j + 8, 8)

    def column(j, far):
        return yh * 8 + lax.rem(far + j, 8)

    def with_children(j, run):
        for parent, children in ((0, (2, 7, 1)), (2, (4, 3)), (7, (6,)), (6, (5,))):

            @pl.when(depth(j) == parent)
            def _():
                run(children)

    for j in range(STEPS):

        @pl.when(e == SIDE[j])
        def _():
            with_children(j, lambda children: [greet_late(column(j, far), c) for far in children])

    @pl.when(row14 & (c != 13))
    def _():
        greet(14, 13)

    @pl.when(row13 & (c != 13))
    def _():
        greet(14, 13)

    @pl.when(back1)
    def _():
        greet(15, 14)

    pl.when(uses_d)(loads[0].wait)

    @pl.when(row0)
    def _():
        loads[1].wait()
        value = jnp.dot(dv[...], bv[...], preferred_element_type=F32)
        yr[...] = value.astype(BF16).T

    @pl.when(late)
    def _():
        loads[3].wait()
        ut[...] = uv[...].T

    @pl.when(row15)
    def _():
        value = product(ut[...], dv[...])
        vf[...] = value
        vb[...] = value.astype(BF16)

    pl.when(uses_l)(loads[2].wait)

    @pl.when(chain1 | chain2)
    def _():
        dt[...] = dv[...].T

    @pl.when((c < 3) & (r > c))
    def _():
        lt[...] = lv[...].T

    count = 16 + jnp.where(((c == 1) | (c == 2)) & (r > 0) | chain1, 15, 0) + jnp.where(late, 15, 0)
    count = count + jnp.where(e == 0, jnp.where(z < 2, 1, 2), jnp.where(z == 2, 0, 1))
    count = count + jnp.where(to_two | chain1 | (row15 & (c == 14)), 1, 0) + jnp.where(back1, 30, 0)
    count = count + jnp.where((r == 1) & ((c == 1) | (c == 3) | (c == 5) | (c == 13)), 1, 0)
    pl.semaphore_wait(barrier, jnp.where(to_one, 1, count))

    @pl.when(to_one)
    def _():
        for col, chunk in ((1, 3), (5, 2), (13, 1), (3, 0)):

            @pl.when(c == col)
            def _():
                part = pl.ds(chunk * CHUNK, CHUNK)
                remote(yr.at[part], yc.at[part], y0_s, yc_r.at[chunk], 1, 0).start()

        pl.semaphore_wait(joined, 14)

    @pl.when(jnp.logical_not(to_one))
    def _():
        meet(join)
        pl.when((r == 1) & (e == 1))(lambda: join(0, c))

    for j in range(STEPS):
        near = jnp.where(depth(j) == 5, 6, jnp.where(depth(j) == 6, 7, jnp.where((depth(j) == 4) | (depth(j) == 3), 2, 0)))

        @pl.when((e == SIDE[j]) & (depth(j) != 0))
        def _():
            pl.semaphore_signal(ready.at[j], inc=1, device_id=(column(j, near), c), device_id_type=MESH)

    def scatter_pf(chunk):
        for k in range(4):
            g = 4 * chunk + k

            @pl.when(g != c)
            def _():
                remote(pf.at[rows(g, PIECE)], rp.at[c], pf_s, rp_r.at[c], r, g).start()

    def scatter_qf(chunk, wanted=lambda h: True):
        for k in range(4):
            h = 4 * chunk + k

            @pl.when((h != r) & wanted(h))
            def _():
                remote(qf.at[rows(h, PIECE)], qr.at[r - 13], qf_s, qr_r.at[r - 13], h, c).start()

    @pl.when(row0)
    def _():
        for col, chunk in ((6, 3), (8, 2), (14, 1), (12, 0)):

            @pl.when(c == col)
            def _():
                part = pl.ds(chunk * CHUNK, CHUNK)
                remote(yr.at[part], yc.at[part], y0_s, yc_r.at[chunk], 2, 0).start()

        @pl.when(e == SIDE[0])
        def _():
            other = 3 - y
            part = rows(2 * (x % 2) + other % 2, CHUNK)
            for k, side in enumerate(halves):
                to = (8, 4 * x + 2 * (other - 2) + e)
                remote(yr.at[part, side], yt.at[0, part, side], s1_s.at[0], own_r.at[0, k], *to).start()
            yt[0, mine] = yr[mine]

    @pl.when(row15 & (c < 15))
    def _():
        def one(step):
            chunk = back_order(step)
            part = rows(chunk, CHUNK)
            qf[part] = product(vb[part], lv[...]).astype(BF16)
            for col, target, recv in ((14, qc, qc_r), (13, pc, pc_r)):

                @pl.when(c == col)
                def _():
                    remote(qf.at[part], target.at[part], qc_s.at[chunk], recv.at[chunk], 14, 13).start()

        loop(4, one)

    @pl.when(jnp.logical_not(row0))
    def _():
        loads[1].wait()

    bt[...] = bv[...].T

    def scatter_s1(j, chunk):
        part = rows(chunk, CHUNK)
        a, b = chunk // 2, chunk % 2
        if chunk == 0:
            yt[j, part] = yr[part]
            return
        for side in range(2):
            far = pl.ds(side * HALF, HALF)
            row = j + (8 * b if side else 0)
            col = (12 * a if side else 4 * a) + 2 * b + SIDE[j]
            remote(yr.at[part, far], yt.at[j, part, far], s1_s.at[chunk], own_r.at[j, side], row, col).start()

    heads = ((x < 2) & (y < 2), ((x == 0) | (x == 3)) & ((y == 0) | (y == 3)))

    def spread(j):
        local = (row0 & (j == 0)) | (chain1 & (j == 1)) | (chain2 & (j == 2))
        starts = (z == j) & (j > 0)
        turned = starts & heads[1] & jnp.logical_not(heads[0])

        for step in range(2):
            side = jnp.where(turned, 1 - step, step)
            part = yt.at[j, mine, pl.ds(pl.multiple_of(side * HALF, HALF), HALF)]

            def to_chip(send, recv, tx, ty):
                remote(part, part, send, recv, 8 * (ty // 2) + z, 4 * tx + 2 * (ty % 2) + e).start()

            @pl.when(jnp.logical_not(local))
            def _():
                got(part, own_r.at[j, side])

            @pl.when(starts & jnp.where(side == 0, heads[0], heads[1]))
            def _():
                x2, y2 = lax.rem(x + 2, 4), lax.rem(y + 2, 4)
                to_chip(s1b_s.at[side], own_r.at[j, side], x2, y2)
                to_chip(s1b_s.at[side], own_r.at[j, side], x2, y)
                to_chip(s1b_s.at[side], own_r.at[j, side], x, y2)

            def run(children):
                if step == 0:
                    pl.semaphore_wait(ready.at[j], len(children))
                for far in children:
                    remote(part, part, s2_s.at[j], own_r.at[j, side], column(j, far), c).start()

            with_children(j, run)
            x1, y1 = lax.rem(x + 1 + 2 * side, 4), lax.rem(y + 1 + 2 * side, 4)
            to_chip(s3_s.at[j], s3_r.at[j, group], x1, y1)
            to_chip(s3_s.at[j], s3_r.at[j, group], x1, y)
            to_chip(s3_s.at[j], s3_r.at[j, group], x, y1)

        block = yt.at[j, mine]
        remote(block, block, s4_s.at[j], s4_r.at[j, group], r, c + 1 - 2 * e).start()

    def collect(j):
        def one(step):
            chunk = 3 - step
            block = yt.at[j, rows(chunk, CHUNK)]

            @pl.when(chunk != group)
            def _():
                got(block, s3_r.at[j, chunk])
                remote(block, block, s4_s.at[j], s4_r.at[j, chunk], r, c + 1 - 2 * e).start()

        loop(4, one)

    def await_other(j):
        loop(4, lambda step: got(yt.at[j, rows(3 - step, CHUNK)], s4_r.at[j, 3 - step]))

    def apply(j):
        def one(step):
            chunk = 3 - step
            part = rows(chunk, CHUNK)

            @pl.when(e != SIDE[j])
            def _():
                got(yt.at[j, part], s4_r.at[j, chunk])

            @pl.when((c == j) & (r >= 3))
            def _():
                partial = product(yt[j, part], lt[...]).astype(BF16)
                if j == 1:
                    got(pc.at[part], pc_r.at[chunk])
                    partial = (pc[part].astype(F32) + partial.astype(F32)).astype(BF16)
                pf[part] = partial
                if j == 0:
                    remote(pf.at[part], pc.at[part], pc_s.at[chunk], pc_r.at[chunk], r, 1).start()
                else:
                    scatter_pf(chunk)

        loop(4, one)

    def centre():
        block = wg.at[x, yl, e]

        @pl.when(row13)
        def _():
            got(tb, tb_r.at[0])
            block[...] = (ut[rows(c, PIECE)].astype(F32) - tb[...].astype(F32)).astype(BF16)

        @pl.when(row14 & (c != 13))
        def _():
            got(block, tb_r.at[0])

        @pl.when(row14 | row13)
        def _():
            def one(k):
                to = lax.rem(2 * x + yl + 1 + k, 8)
                remote(block, block, ag_s, ag_r.at[x], r, 2 * to + e).start()

            loop(7, one)

    def gather():
        @pl.when(row14 | row13)
        def _():
            def one(step):
                chunk = back_order(step)

                @pl.when(chunk == x)
                def _():
                    got(wg.at[chunk, 0, e], ag_r.at[chunk])

                @pl.when(chunk != x)
                def _():
                    got(wg.at[chunk, :, e], ag_r.at[chunk])

                block = wg.at[chunk, :, e]
                remote(block, block, sib_s.at[chunk], sib_r.at[chunk], r, c + 1 - 2 * e).start()

            loop(4, one)

    def solve():
        @pl.when(row14 | row13)
        def _():
            def one(step):
                chunk = back_order(step)
                part = rows(chunk, CHUNK)
                got(wg.at[chunk, :, 1 - e], sib_r.at[chunk])
                answer = product(wg[chunk].reshape(CHUNK, NB), dv[...])
                vf[part] = answer

                @pl.when((c < r) & jnp.logical_not(back1))
                def _():
                    qf[part] = product(answer.astype(BF16), lv[...]).astype(BF16)
                    scatter_qf(chunk)

            loop(4, one)

            @pl.when(back1)
            def _():
                loop(4, scatter_qf)

    @pl.when(chain1)
    def _():
        def one(step):
            chunk = 3 - step
            part = rows(chunk, CHUNK)
            got(yc.at[part], yc_r.at[chunk])
            partial = product(yc[part], lt[...]).astype(BF16)
            pf[part] = partial
            residue = (bt[part].astype(F32) - partial.astype(F32)).astype(BF16)
            yr[part] = product(residue, dt[...]).astype(BF16)
            remote(yr.at[part], yc.at[part], ch_s.at[chunk], yc_r.at[chunk], 2, 1).start()
            for k in range(4):
                pl.when(chunk == k)(lambda: scatter_s1(1, k))

        loop(4, one)

    @pl.when(chain20)
    def _():
        def one(step):
            chunk = 3 - step
            part = rows(chunk, CHUNK)
            got(yc.at[part], yc_r.at[chunk])
            pf[part] = product(yc[part], lt[...]).astype(BF16)
            remote(pf.at[part], pc.at[part], pc_s.at[chunk], pc_r.at[chunk], 2, 1).start()

        loop(4, one)

    @pl.when(chain2)
    def _():
        def one(step):
            chunk = 3 - step
            part = rows(chunk, CHUNK)
            got(yc.at[part], yc_r.at[chunk])
            partial = product(yc[part], lt[...]).astype(BF16)
            got(pc.at[part], pc_r.at[chunk])
            total = pc[part].astype(F32) + partial.astype(F32)
            pf[part] = total.astype(BF16)
            residue = (bt[part].astype(F32) - total).astype(BF16)
            yr[part] = product(residue, dt[...]).astype(BF16)
            for k in range(4):
                pl.when(chunk == k)(lambda: scatter_s1(2, k))

        loop(4, one)

    @pl.when(back1)
    def _():
        def one(step):
            chunk = back_order(step)
            part = rows(chunk, CHUNK)
            got(qc.at[part], qc_r.at[chunk])
            centred = (ut[part].astype(F32) - qc[part].astype(F32)).astype(BF16)
            wl[part] = centred
            answer = product(centred, dv[...]).astype(BF16)
            partial = product(answer, lv[...]).astype(BF16)
            qf[part] = partial
            got(pc.at[part], pc_r.at[chunk])
            yc[part] = (pc[part].astype(F32) + partial.astype(F32)).astype(BF16)
            for k in range(4):
                g = 4 * chunk + k
                remote(yc.at[rows(g, PIECE)], tb, tb_s, tb_r.at[0], 13, g).start()
            for k in range(4):
                piece = rows(4 * chunk + k, PIECE)
                target = wg.at[chunk, k // 2, k % 2]

                @pl.when(4 * chunk + k != c)
                def _():
                    remote(wl.at[piece], target, w_s, tb_r.at[0], 14, 4 * chunk + k).start()

                @pl.when(4 * chunk + k == c)
                def _():
                    target[...] = wl[piece]

        loop(4, one)

    middle = row13 | row14
    first_two = (jnp.where(z == 1, 1, 0), jnp.where(e == 1, 2, jnp.where(z == 1, 0, 1)))

    def below(h):
        return (h % 8 >= 3) & (h % 8 < 7)

    @pl.when((e == 0) & jnp.logical_not(row13))
    def _():
        spread(first_two[0])

    @pl.when(row15 & (c < 15))
    def _():
        loop(4, lambda chunk: scatter_qf(chunk, lambda h: jnp.logical_not(below(h))))

    centre()

    @pl.when((e == 0) & row13)
    def _():
        spread(0)

    pl.when((e == 1) & row15)(lambda: await_other(0))

    @pl.when((e == 1) & row15 & (c < 15))
    def _():
        loop(4, lambda chunk: scatter_qf(chunk, below))

    @pl.when(jnp.logical_not(middle))
    def _():
        spread(first_two[1])

    @pl.when((e == 0) & row15)
    def _():
        loop(4, lambda chunk: scatter_qf(chunk, below))

    @pl.when((e == 0) & jnp.logical_not(middle))
    def _():
        collect(0)
        apply(0)

    gather()

    @pl.when((e == 0) & row13)
    def _():
        spread(1)

    solve()

    @pl.when(row14 | (row13 & (e == 1)))
    def _():
        spread(first_two[1])

    @pl.when((e == 0) & middle)
    def _():
        collect(0)
        apply(0)

    @pl.when(chain1 | chain2)
    def _():
        loop(4, scatter_pf)

    @pl.when(e == 0)
    def _():
        collect(1)
        apply(1)

    @pl.when(e == 1)
    def _():
        collect(2)
        pl.when(jnp.logical_not(row15))(lambda: await_other(0))
        apply(1)

    apply(2)

    for j in range(STEPS):

        @pl.when(e == SIDE[j])
        def _():
            sent(yt.at[j, pl.ds(0, 192)], s3_s.at[j])
            sent(yt.at[j], s4_s.at[j])
            with_children(j, lambda children: sent(yt.at[j, pl.ds(0, len(children) * CHUNK)], s2_s.at[j]))

    for k in range(2):

        @pl.when(((z == 1) & (e == 0) | (z == 2) & (e == 1)) & heads[k])
        def _():
            sent(yt.at[0, pl.ds(0, 192), halves[k]], s1b_s.at[k])

    @pl.when(row0)
    def _():
        @pl.when(to_one | to_two)
        def _():
            sent(yr.at[pl.ds(0, CHUNK)], y0_s)

        @pl.when(e == SIDE[0])
        def _():
            sent(yr.at[pl.ds(0, CHUNK)], s1_s.at[0])

    @pl.when(chain1 | chain2)
    def _():
        for k in range(1, 4):
            sent(yr.at[pl.ds(0, CHUNK)], s1_s.at[k])

    @pl.when(chain1)
    def _():
        for k in range(4):
            sent(yr.at[pl.ds(0, CHUNK)], ch_s.at[k])

    @pl.when((c == 0) & (r >= 2))
    def _():
        for k in range(4):
            sent(pf.at[pl.ds(0, CHUNK)], pc_s.at[k])

    @pl.when(chain1 | ((c == 1) & (r >= 2)) | ((c == 2) & (r >= 3)))
    def _():
        sent(pf.at[pl.ds(0, 240)], pf_s)

    @pl.when(late & (c < r))
    def _():
        sent(qf.at[pl.ds(0, 240)], qf_s)

    @pl.when(row15 & ((c == 13) | (c == 14)))
    def _():
        for k in range(4):
            sent(qf.at[pl.ds(0, CHUNK)], qc_s.at[k])

    @pl.when(back1)
    def _():
        sent(qf, tb_s)

    @pl.when(back1)
    def _():
        sent(qf.at[pl.ds(0, 240)], w_s)

    @pl.when(row14 | row13)
    def _():
        sent(qf.at[pl.ds(0, 112)], ag_s)
        for k in range(4):
            sent(wg.at[0, :, 0], sib_s.at[k])

    rest_out[...] = bt[rows(c, PIECE)].astype(F32)
    for j in range(STEPS):

        @pl.when((r == 1) if j == 0 else (r > j))
        def _():
            @pl.when(c == j)
            def _():
                rest_out[...] -= pf[rows(c, PIECE)].astype(F32)

            @pl.when(c != j)
            def _():
                got(rp.at[j], rp_r.at[j])
                rest_out[...] -= rp[j].astype(F32)

    back_out[...] = jnp.zeros_like(back_out)
    for j in range(STEPS):

        @pl.when(c < 13 + j)
        def _():
            @pl.when(r == 13 + j)
            def _():
                back_out[...] += qf[rows(r, PIECE)].astype(F32)

            @pl.when(r != 13 + j)
            def _():
                got(qr.at[j], qr_r.at[j])
                back_out[...] += qr[j].astype(F32)


def hand_over(yt, rest, back, vf, solved_out, rest_out, back_out, solution_out, so, sl, sems):
    late = lax.axis_index("row") >= 13
    answer = pltpu.make_async_copy(sl, solution_out, sems.at[5])
    stores = [pltpu.make_async_copy(rest, rest_out, sems.at[3]), pltpu.make_async_copy(back, back_out, sems.at[4])]
    for store in stores:
        store.start()

    @pl.when(jnp.logical_not(late))
    def _():
        sl[...] = jnp.zeros_like(sl)

    @pl.when(late)
    def _():
        sl[...] = vf[...].T

    answer.start()
    for j in range(STEPS):
        whole = pl.ds(j * NB, NB)
        so[whole] = yt[j].T
        stores.append(pltpu.make_async_copy(so.at[whole], solved_out.at[whole], sems.at[j]))
        stores[-1].start()
    for store in stores:
        store.wait()
    answer.wait()


def local(factor, diag_inv, rhs, forward_values):
    anywhere = pl.BlockSpec(memory_space=pl.ANY)
    vmem = pl.BlockSpec(memory_space=pltpu.VMEM)
    dma = pltpu.SemaphoreType.DMA
    square = pltpu.VMEM((NB, NB), BF16)
    tall = pltpu.VMEM((NB, COLS), BF16)
    wide = pltpu.VMEM((COLS, NB), BF16)
    results = pl.pallas_call(
        kernel,
        name="solves",
        out_shape=(
            pltpu.VMEM((STEPS, COLS, NB), BF16),
            pltpu.VMEM((PIECE, NB), F32),
            pltpu.VMEM((PIECE, NB), F32),
            pltpu.VMEM((COLS, NB), F32),
        ),
        in_specs=[anywhere] * 4,
        out_specs=(vmem,) * 4,
        scratch_shapes=[
            square, square, tall, tall, square, square, wide, wide,
            wide, wide, wide, wide,
            pltpu.VMEM((STEPS, PIECE, NB), BF16),
            wide,
            pltpu.VMEM((STEPS, PIECE, NB), BF16),
            wide,
            pltpu.VMEM((PIECE, NB), BF16),
            pltpu.VMEM((4, 2, 2, PIECE, NB), BF16),
            wide,
            wide,
            pltpu.SemaphoreType.REGULAR((3,)), pltpu.SemaphoreType.REGULAR, dma((4,)),
            dma((4,)), dma((4,)), dma((3, 2)), dma((3, 4)), dma((3, 4)), dma((3,)), dma((3,)), dma((4,)), dma((2,)),
            dma((4,)), dma((4,)),
            dma(()), dma((4,)), dma((2,)), dma((3,)), dma((3,)), dma((3,)), dma(()), dma((4,)), dma((4,)),
            dma(()), dma((4,)), dma(()), dma(()), dma(()), dma((4,)),
        ],
        compiler_params=pltpu.CompilerParams(
            collective_id=0, has_side_effects=True, vmem_limit_bytes=60 * 1024 * 1024
        ),
    )(factor, diag_inv, rhs, forward_values)
    solved, rest, back, answer = pl.pallas_call(
        hand_over,
        name="hand_over",
        out_shape=(
            jax.ShapeDtypeStruct((STEPS * NB, COLS), BF16),
            jax.ShapeDtypeStruct((PIECE, NB), F32),
            jax.ShapeDtypeStruct((PIECE, NB), F32),
            jax.ShapeDtypeStruct((NB, COLS), F32),
        ),
        in_specs=[vmem] * 4,
        out_specs=(anywhere,) * 4,
        scratch_shapes=[pltpu.VMEM((STEPS * NB, COLS), BF16), pltpu.VMEM((NB, COLS), F32), dma((6,))],
        compiler_params=pltpu.CompilerParams(vmem_limit_bytes=32 * 1024 * 1024),
    )(*results)
    return solved, rest.T, back.T, answer


def solution(mesh):
    placed = (P("row", "col"), P("row", None), P("row", None), P("row", None))
    return jax.shard_map(
        local,
        mesh=mesh,
        in_specs=placed,
        out_specs=(P(), P("row", "col"), P("col", "row"), P("row", None)),
        check_vma=False,
    )
```

```python
import jax
import jax.numpy as jnp
from jax import lax
from jax.experimental import pallas as pl
from jax.experimental.pallas import tpu as pltpu
from jax.sharding import PartitionSpec as P

NB = 1024
COLS = 256
STEPS = 3
NROW = 16
NCOL = 16
PIECE = 16
CHUNK = 64
HALF = 512
SIDE = (0, 0, 1)
MESH = pl.DeviceIdType.MESH
F32 = jnp.float32
BF16 = jnp.bfloat16


def product(left, right):
    return lax.dot_general(left, right, (((1,), (0,)), ((), ())), preferred_element_type=F32)


def loop(count, body):
    def step(index, carry):
        body(index)
        return carry

    lax.fori_loop(0, count, step, 0)


def kernel(
    factor, inverse, rhs, start,
    so, rest_out, back_out, sl,
    lv, dv, bv, uv, lt, dt, bt, ut,
    yt, vf, yc, pc, yr, pf, rp, qf, qr, qc, tb, wg, wl, vb,
    ready, joined, ld_s,
    yc_r, pc_r, own_r, s3_r, s4_r, rp_r, qr_r, qc_r, tb_r, ag_r, sib_r,
    y0_s, s1_s, s1b_s, s2_s, s3_s, s4_s, pf_s, ch_s, pc_s, qf_s, qc_s, tb_s, w_s, ag_s, sib_s,
):
    r = lax.axis_index("row")
    c = lax.axis_index("col")
    x = c // 4
    yl = (c // 2) % 2
    e = c % 2
    yh = r // 8
    z = r % 8
    y = 2 * yh + yl
    row0 = r == 0
    chain1 = (r == 1) & (c == 0)
    chain20 = (r == 2) & (c == 0)
    chain2 = (r == 2) & (c == 1)
    row13 = r == 13
    row14 = r == 14
    row15 = r == 15
    late = r >= 13
    back1 = (r == 14) & (c == 13)
    group = 2 * (x % 2) + y % 2
    halves = (pl.ds(0, HALF), pl.ds(HALF, HALF))
    mine = pl.ds(pl.multiple_of(group * CHUNK, CHUNK), CHUNK)

    def remote(src, dst, send, recv, row, col):
        return pltpu.make_async_remote_copy(
            src_ref=src, dst_ref=dst, send_sem=send, recv_sem=recv, device_id=(row, col), device_id_type=MESH
        )

    def got(ref, sem):
        remote(ref, ref, sem, sem, r, c).wait_recv()

    def sent(ref, sem):
        remote(ref, ref, sem, sem, r, c).wait_send()

    def rows(index, count):
        return pl.ds(pl.multiple_of(index * count, count), count)

    uses_l = ((c < STEPS) & (r > c)) | (late & (c < r))
    uses_d = row0 | chain1 | chain2 | late
    needs = (uses_d, r >= 0, uses_l, late)
    pairs = ((inverse, dv), (rhs, bv), (factor, lv), (start, uv))
    loads = [pltpu.make_async_copy(source, target, ld_s.at[k]) for k, (source, target) in enumerate(pairs)]
    for k in (0, 3, 1, 2):
        pl.when(needs[k])(loads[k].start)
    def source_of(cols):
        found = c == cols[0]
        for col in cols[1:]:
            found = found | (c == col)
        return row0 & found

    to_one = source_of((1, 3, 5, 13))
    to_two = source_of((6, 8, 12, 14))
    barrier = pltpu.get_barrier_semaphore()

    def greet(row, col):
        pl.semaphore_signal(barrier, inc=1, device_id=(row, col), device_id_type=MESH)

    def is_early(row, col):
        return (row == 0) & ((col == 1) | (col == 3) | (col == 5) | (col == 13))

    def meet(run):
        run(r, c + 1 - 2 * e)
        loop(7, lambda k: run(r, lax.rem(c + 2 + 2 * k, 16)))
        loop(8, lambda k: run(lax.rem(r + 8, 16), 2 * k + e))

    def greet_late(row, col):
        pl.when(jnp.logical_not(is_early(row, col)))(lambda: greet(row, col))

    def join(row, col):
        @pl.when(is_early(row, col))
        def _():
            pl.semaphore_signal(joined, inc=1, device_id=(row, col), device_id_type=MESH)

    @pl.when(chain1)
    def _():
        for col in (1, 3, 5, 13):
            greet(0, col)

    @pl.when(chain20)
    def _():
        for col in (6, 8, 12, 14):
            greet(0, col)

    @pl.when(chain2)
    def _():
        greet(1, 0)

    meet(greet_late)
    pl.when((r == 1) & (c != 0))(lambda: greet(1, 0))
    pl.when((r > 0) & (c != 1))(lambda: greet(r, 1))
    pl.when((r > 0) & (c != 2))(lambda: greet(r, 2))
    pl.when(to_one)(lambda: greet(1, c))
    pl.when(r != 13)(lambda: greet(13, c))
    pl.when(r != 14)(lambda: greet(14, c))
    pl.when(r != 15)(lambda: greet(15, c))

    def depth(j):
        return lax.rem(z - j + 8, 8)

    def column(j, far):
        return yh * 8 + lax.rem(far + j, 8)

    def with_children(j, run):
        for parent, children in ((0, (2, 7, 1)), (2, (4, 3)), (7, (6,)), (6, (5,))):

            @pl.when(depth(j) == parent)
            def _():
                run(children)

    for j in range(STEPS):

        @pl.when(e == SIDE[j])
        def _():
            with_children(j, lambda children: [greet_late(column(j, far), c) for far in children])

    @pl.when(row14 & (c != 13))
    def _():
        greet(14, 13)

    @pl.when(row13 & (c != 13))
    def _():
        greet(14, 13)

    @pl.when(back1)
    def _():
        greet(15, 14)

    pl.when(uses_d)(loads[0].wait)

    @pl.when(row0)
    def _():
        loads[1].wait()
        value = jnp.dot(dv[...], bv[...], preferred_element_type=F32)
        yr[...] = value.astype(BF16).T

    @pl.when(late)
    def _():
        loads[3].wait()
        ut[...] = uv[...].T

    def solve_15(step):
        part = rows(step, 2 * CHUNK)
        value = product(ut[part], dv[...])
        vf[part] = value
        vb[part] = value.astype(BF16)

    pl.when(row15)(lambda: solve_15(0))
    pl.when(uses_l)(loads[2].wait)

    @pl.when(chain1 | chain2)
    def _():
        dt[...] = dv[...].T

    @pl.when((c < 3) & (r > c))
    def _():
        lt[...] = lv[...].T

    count = 16 + jnp.where(((c == 1) | (c == 2)) & (r > 0) | chain1, 15, 0) + jnp.where(late, 15, 0)
    count = count + jnp.where(e == 0, jnp.where(z < 2, 1, 2), jnp.where(z == 2, 0, 1))
    count = count + jnp.where(to_two | chain1 | (row15 & (c == 14)), 1, 0) + jnp.where(back1, 30, 0)
    count = count + jnp.where((r == 1) & ((c == 1) | (c == 3) | (c == 5) | (c == 13)), 1, 0)
    pl.semaphore_wait(barrier, jnp.where(to_one, 1, count))

    @pl.when(to_one)
    def _():
        for col, chunk in ((1, 3), (5, 2), (13, 1), (3, 0)):

            @pl.when(c == col)
            def _():
                part = pl.ds(chunk * CHUNK, CHUNK)
                remote(yr.at[part], yc.at[part], y0_s, yc_r.at[chunk], 1, 0).start()

        pl.semaphore_wait(joined, 14)

    @pl.when(jnp.logical_not(to_one))
    def _():
        meet(join)
        pl.when((r == 1) & (e == 1))(lambda: join(0, c))

    for j in range(STEPS):
        near = jnp.where(depth(j) == 5, 6, jnp.where(depth(j) == 6, 7, jnp.where((depth(j) == 4) | (depth(j) == 3), 2, 0)))

        @pl.when((e == SIDE[j]) & (depth(j) != 0))
        def _():
            pl.semaphore_signal(ready.at[j], inc=1, device_id=(column(j, near), c), device_id_type=MESH)

    def scatter_pf(chunk):
        for k in range(4):
            g = 4 * chunk + k

            @pl.when(g != c)
            def _():
                remote(pf.at[rows(g, PIECE)], rp.at[c], pf_s, rp_r.at[c], r, g).start()

    def scatter_qf(chunk, wanted=lambda h: True):
        for k in range(4):
            h = 4 * chunk + k

            @pl.when((h != r) & wanted(h))
            def _():
                remote(qf.at[rows(h, PIECE)], qr.at[r - 13], qf_s, qr_r.at[r - 13], h, c).start()

    @pl.when(row0)
    def _():
        for col, chunk in ((6, 3), (8, 2), (14, 1), (12, 0)):

            @pl.when(c == col)
            def _():
                part = pl.ds(chunk * CHUNK, CHUNK)
                remote(yr.at[part], yc.at[part], y0_s, yc_r.at[chunk], 2, 0).start()

        @pl.when(e == SIDE[0])
        def _():
            other = 3 - y
            part = rows(2 * (x % 2) + other % 2, CHUNK)
            for k, side in enumerate(halves):
                to = (8, 4 * x + 2 * (other - 2) + e)
                remote(yr.at[part, side], yt.at[0, part, side], s1_s.at[0], own_r.at[0, k], *to).start()
            yt[0, mine] = yr[mine]

    @pl.when(row15)
    def _():
        def one(step):
            part = rows(step, CHUNK)
            pl.when(step == 2)(lambda: solve_15(1))

            @pl.when(c < 15)
            def _():
                qf[part] = product(vb[part], lv[...]).astype(BF16)

            for col, target, recv in ((14, qc, qc_r), (13, pc, pc_r)):

                @pl.when(c == col)
                def _():
                    remote(qf.at[part], target.at[part], qc_s.at[step], recv.at[step], 14, 13).start()

        loop(4, one)

    @pl.when(jnp.logical_not(row0))
    def _():
        loads[1].wait()

    bt[...] = bv[...].T

    def scatter_s1(j, chunk):
        part = rows(chunk, CHUNK)
        a, b = chunk // 2, chunk % 2
        if chunk == 0:
            yt[j, part] = yr[part]
            return
        for side in range(2):
            far = pl.ds(side * HALF, HALF)
            row = j + (8 * b if side else 0)
            col = (12 * a if side else 4 * a) + 2 * b + SIDE[j]
            remote(yr.at[part, far], yt.at[j, part, far], s1_s.at[chunk], own_r.at[j, side], row, col).start()

    heads = ((x < 2) & (y < 2), ((x == 0) | (x == 3)) & ((y == 0) | (y == 3)))

    def spread(j):
        local = (row0 & (j == 0)) | (chain1 & (j == 1)) | (chain2 & (j == 2))
        starts = (z == j) & (j > 0)
        turned = starts & heads[1] & jnp.logical_not(heads[0])

        for step in range(2):
            side = jnp.where(turned, 1 - step, step)
            part = yt.at[j, mine, pl.ds(pl.multiple_of(side * HALF, HALF), HALF)]

            def to_chip(send, recv, tx, ty):
                remote(part, part, send, recv, 8 * (ty // 2) + z, 4 * tx + 2 * (ty % 2) + e).start()

            @pl.when(jnp.logical_not(local))
            def _():
                got(part, own_r.at[j, side])

            @pl.when(starts & jnp.where(side == 0, heads[0], heads[1]))
            def _():
                x2, y2 = lax.rem(x + 2, 4), lax.rem(y + 2, 4)
                to_chip(s1b_s.at[side], own_r.at[j, side], x2, y2)
                to_chip(s1b_s.at[side], own_r.at[j, side], x2, y)
                to_chip(s1b_s.at[side], own_r.at[j, side], x, y2)

            def run(children):
                if step == 0:
                    pl.semaphore_wait(ready.at[j], len(children))
                for far in children:
                    remote(part, part, s2_s.at[j], own_r.at[j, side], column(j, far), c).start()

            with_children(j, run)
            x1, y1 = lax.rem(x + 1 + 2 * side, 4), lax.rem(y + 1 + 2 * side, 4)
            to_chip(s3_s.at[j], s3_r.at[j, group], x1, y1)
            to_chip(s3_s.at[j], s3_r.at[j, group], x1, y)
            to_chip(s3_s.at[j], s3_r.at[j, group], x, y1)

        block = yt.at[j, mine]
        remote(block, block, s4_s.at[j], s4_r.at[j, group], r, c + 1 - 2 * e).start()

    def collect(j):
        def one(step):
            chunk = 3 - step
            block = yt.at[j, rows(chunk, CHUNK)]

            @pl.when(chunk != group)
            def _():
                got(block, s3_r.at[j, chunk])
                remote(block, block, s4_s.at[j], s4_r.at[j, chunk], r, c + 1 - 2 * e).start()

        loop(4, one)

    def await_other(j):
        loop(4, lambda step: got(yt.at[j, rows(3 - step, CHUNK)], s4_r.at[j, 3 - step]))

    def apply(j):
        def one(step):
            part = rows(1 - step, 2 * CHUNK)
            pair = (3 - 2 * step, 2 - 2 * step)

            @pl.when(e != SIDE[j])
            def _():
                for chunk in pair:
                    got(yt.at[j, rows(chunk, CHUNK)], s4_r.at[j, chunk])

            @pl.when((c == j) & (r >= 3))
            def _():
                partial = product(yt[j, part], lt[...]).astype(BF16)
                if j == 1:
                    for chunk in pair:
                        got(pc.at[rows(chunk, CHUNK)], pc_r.at[chunk])
                    partial = (pc[part].astype(F32) + partial.astype(F32)).astype(BF16)
                pf[part] = partial
                for chunk in pair:
                    if j == 0:
                        half = rows(chunk, CHUNK)
                        remote(pf.at[half], pc.at[half], pc_s.at[chunk], pc_r.at[chunk], r, 1).start()
                    else:
                        scatter_pf(chunk)

        loop(2, one)
        so[pl.ds(j * NB, NB)] = yt[j].T

    def centre():
        block = wg.at[x, yl, e]

        @pl.when(row13)
        def _():
            got(tb, tb_r.at[0])
            block[...] = (ut[rows(c, PIECE)].astype(F32) - tb[...].astype(F32)).astype(BF16)

        @pl.when(row14 & (c != 13))
        def _():
            got(block, tb_r.at[0])

        @pl.when(row14 | row13)
        def _():
            def one(k):
                to = lax.rem(2 * x + yl + 1 + k, 8)
                remote(block, block, ag_s, ag_r.at[x], r, 2 * to + e).start()

            loop(7, one)

    def gather_and_solve(between):
        def one(step):
            for k in range(2):
                chunk = 2 * step + k

                @pl.when(chunk == x)
                def _():
                    got(wg.at[chunk, 0, e], ag_r.at[chunk])

                @pl.when(chunk != x)
                def _():
                    got(wg.at[chunk, :, e], ag_r.at[chunk])

                block = wg.at[chunk, :, e]
                remote(block, block, sib_s.at[chunk], sib_r.at[chunk], r, c + 1 - 2 * e).start()

            part = rows(step, 2 * CHUNK)
            for k in range(2):
                got(wg.at[2 * step + k, :, 1 - e], sib_r.at[2 * step + k])
            answer = product(wg[pl.ds(2 * step, 2)].reshape(2 * CHUNK, NB), dv[...])
            vf[part] = answer

            @pl.when((c < r) & jnp.logical_not(back1))
            def _():
                qf[part] = product(answer.astype(BF16), lv[...]).astype(BF16)

            @pl.when(c < r)
            def _():
                scatter_qf(2 * step)
                scatter_qf(2 * step + 1)

            pl.when((step == 0) & (e == 0))(between)

        loop(2, one)
        pl.when(e == 1)(between)

    @pl.when(chain1)
    def _():
        def one(step):
            chunk = 3 - step
            part = rows(chunk, CHUNK)
            got(yc.at[part], yc_r.at[chunk])
            partial = product(yc[part], lt[...]).astype(BF16)
            pf[part] = partial
            residue = (bt[part].astype(F32) - partial.astype(F32)).astype(BF16)
            yr[part] = product(residue, dt[...]).astype(BF16)
            remote(yr.at[part], yc.at[part], ch_s.at[chunk], yc_r.at[chunk], 2, 1).start()
            for k in range(4):
                pl.when(chunk == k)(lambda: scatter_s1(1, k))

        loop(4, one)

    @pl.when(chain20)
    def _():
        def one(step):
            chunk = 3 - step
            part = rows(chunk, CHUNK)
            got(yc.at[part], yc_r.at[chunk])
            pf[part] = product(yc[part], lt[...]).astype(BF16)
            remote(pf.at[part], pc.at[part], pc_s.at[chunk], pc_r.at[chunk], 2, 1).start()

        loop(4, one)

    @pl.when(chain2)
    def _():
        def one(step):
            chunk = 3 - step
            part = rows(chunk, CHUNK)
            got(yc.at[part], yc_r.at[chunk])
            partial = product(yc[part], lt[...]).astype(BF16)
            got(pc.at[part], pc_r.at[chunk])
            total = pc[part].astype(F32) + partial.astype(F32)
            pf[part] = total.astype(BF16)
            residue = (bt[part].astype(F32) - total).astype(BF16)
            yr[part] = product(residue, dt[...]).astype(BF16)
            for k in range(4):
                pl.when(chunk == k)(lambda: scatter_s1(2, k))

        loop(4, one)

    @pl.when(back1)
    def _():
        def one(step):
            chunk = step
            part = rows(chunk, CHUNK)
            got(qc.at[part], qc_r.at[chunk])
            centred = (ut[part].astype(F32) - qc[part].astype(F32)).astype(BF16)
            wl[part] = centred
            answer = product(centred, dv[...]).astype(BF16)
            partial = product(answer, lv[...]).astype(BF16)
            qf[part] = partial
            got(pc.at[part], pc_r.at[chunk])
            yc[part] = (pc[part].astype(F32) + partial.astype(F32)).astype(BF16)
            for k in range(4):
                g = 4 * chunk + k
                remote(yc.at[rows(g, PIECE)], tb, tb_s, tb_r.at[0], 13, g).start()
            for k in range(4):
                piece = rows(4 * chunk + k, PIECE)
                target = wg.at[chunk, k // 2, k % 2]

                @pl.when(4 * chunk + k != c)
                def _():
                    remote(wl.at[piece], target, w_s, tb_r.at[0], 14, 4 * chunk + k).start()

                @pl.when(4 * chunk + k == c)
                def _():
                    target[...] = wl[piece]

        loop(4, one)

    middle = row13 | row14
    first_two = (jnp.where(z == 1, 1, 0), jnp.where(e == 1, 2, jnp.where(z == 1, 0, 1)))

    def below(h):
        return (h % 8 >= 3) & (h % 8 < 7)

    @pl.when((e == 0) & jnp.logical_not(row13))
    def _():
        spread(first_two[0])

    @pl.when(row15 & (c < 15))
    def _():
        loop(4, lambda chunk: scatter_qf(chunk, lambda h: jnp.logical_not(below(h))))

    centre()

    @pl.when((e == 0) & row13)
    def _():
        spread(0)

    pl.when((e == 1) & row15)(lambda: await_other(0))

    @pl.when((e == 1) & row15 & (c < 15))
    def _():
        loop(4, lambda chunk: scatter_qf(chunk, below))

    @pl.when(jnp.logical_not(middle))
    def _():
        spread(first_two[1])

    @pl.when((e == 0) & row15)
    def _():
        loop(4, lambda chunk: scatter_qf(chunk, below))

    @pl.when((e == 0) & jnp.logical_not(middle))
    def _():
        collect(0)
        apply(0)

    @pl.when(middle)
    def _():
        gather_and_solve(lambda: spread(first_two[1]))

    @pl.when((e == 0) & middle)
    def _():
        collect(0)
        apply(0)

    @pl.when(chain1 | chain2)
    def _():
        loop(4, scatter_pf)

    @pl.when(e == 0)
    def _():
        collect(1)
        apply(1)

    @pl.when(e == 1)
    def _():
        collect(2)
        pl.when(jnp.logical_not(row15))(lambda: await_other(0))
        so[pl.ds(0, NB)] = yt[0].T
        apply(1)

    apply(2)

    @pl.when(late)
    def _():
        sl[...] = vf[...].T

    @pl.when(jnp.logical_not(late))
    def _():
        sl[...] = jnp.zeros_like(sl)

    for j in range(STEPS):

        @pl.when(e == SIDE[j])
        def _():
            sent(yt.at[j, pl.ds(0, 192)], s3_s.at[j])
            sent(yt.at[j], s4_s.at[j])
            with_children(j, lambda children: sent(yt.at[j, pl.ds(0, len(children) * CHUNK)], s2_s.at[j]))

    for k in range(2):

        @pl.when(((z == 1) & (e == 0) | (z == 2) & (e == 1)) & heads[k])
        def _():
            sent(yt.at[0, pl.ds(0, 192), halves[k]], s1b_s.at[k])

    @pl.when(row0)
    def _():
        @pl.when(to_one | to_two)
        def _():
            sent(yr.at[pl.ds(0, CHUNK)], y0_s)

        @pl.when(e == SIDE[0])
        def _():
            sent(yr.at[pl.ds(0, CHUNK)], s1_s.at[0])

    @pl.when(chain1 | chain2)
    def _():
        for k in range(1, 4):
            sent(yr.at[pl.ds(0, CHUNK)], s1_s.at[k])

    @pl.when(chain1)
    def _():
        for k in range(4):
            sent(yr.at[pl.ds(0, CHUNK)], ch_s.at[k])

    @pl.when((c == 0) & (r >= 2))
    def _():
        for k in range(4):
            sent(pf.at[pl.ds(0, CHUNK)], pc_s.at[k])

    @pl.when(chain1 | ((c == 1) & (r >= 2)) | ((c == 2) & (r >= 3)))
    def _():
        sent(pf.at[pl.ds(0, 240)], pf_s)

    @pl.when(late & (c < r))
    def _():
        sent(qf.at[pl.ds(0, 240)], qf_s)

    @pl.when(row15 & ((c == 13) | (c == 14)))
    def _():
        for k in range(4):
            sent(qf.at[pl.ds(0, CHUNK)], qc_s.at[k])

    @pl.when(back1)
    def _():
        sent(qf, tb_s)

    @pl.when(back1)
    def _():
        sent(qf.at[pl.ds(0, 240)], w_s)

    @pl.when(row14 | row13)
    def _():
        sent(qf.at[pl.ds(0, 112)], ag_s)
        for k in range(4):
            sent(wg.at[0, :, 0], sib_s.at[k])

    rest_out[...] = bt[rows(c, PIECE)].astype(F32)
    for j in range(STEPS):

        @pl.when((r == 1) if j == 0 else (r > j))
        def _():
            @pl.when(c == j)
            def _():
                rest_out[...] -= pf[rows(c, PIECE)].astype(F32)

            @pl.when(c != j)
            def _():
                got(rp.at[j], rp_r.at[j])
                rest_out[...] -= rp[j].astype(F32)

    back_out[...] = jnp.zeros_like(back_out)
    for j in range(STEPS):

        @pl.when(c < 13 + j)
        def _():
            @pl.when(r == 13 + j)
            def _():
                back_out[...] += qf[rows(r, PIECE)].astype(F32)

            @pl.when(r != 13 + j)
            def _():
                got(qr.at[j], qr_r.at[j])
                back_out[...] += qr[j].astype(F32)


def hand_over(*refs):
    sems = refs[-1]
    copies = [pltpu.make_async_copy(refs[k], refs[k + 4], sems.at[k]) for k in range(4)]
    for copy in copies:
        copy.start()
    for copy in copies:
        copy.wait()


def local(factor, diag_inv, rhs, forward_values):
    anywhere = pl.BlockSpec(memory_space=pl.ANY)
    vmem = pl.BlockSpec(memory_space=pltpu.VMEM)
    dma = pltpu.SemaphoreType.DMA
    square = pltpu.VMEM((NB, NB), BF16)
    tall = pltpu.VMEM((NB, COLS), BF16)
    wide = pltpu.VMEM((COLS, NB), BF16)
    results = pl.pallas_call(
        kernel,
        name="solves",
        out_shape=(
            pltpu.VMEM((STEPS * NB, COLS), BF16),
            pltpu.VMEM((PIECE, NB), F32),
            pltpu.VMEM((PIECE, NB), F32),
            pltpu.VMEM((NB, COLS), F32),
        ),
        in_specs=[anywhere] * 4,
        out_specs=(vmem,) * 4,
        scratch_shapes=[
            square, square, tall, tall, square, square, wide, wide,
            pltpu.VMEM((STEPS, COLS, NB), BF16),
            pltpu.VMEM((COLS, NB), F32),
            wide, wide, wide, wide,
            pltpu.VMEM((STEPS, PIECE, NB), BF16),
            wide,
            pltpu.VMEM((STEPS, PIECE, NB), BF16),
            wide,
            pltpu.VMEM((PIECE, NB), BF16),
            pltpu.VMEM((4, 2, 2, PIECE, NB), BF16),
            wide,
            wide,
            pltpu.SemaphoreType.REGULAR((3,)), pltpu.SemaphoreType.REGULAR, dma((4,)),
            dma((4,)), dma((4,)), dma((3, 2)), dma((3, 4)), dma((3, 4)), dma((3,)), dma((3,)), dma((4,)), dma((2,)),
            dma((4,)), dma((4,)),
            dma(()), dma((4,)), dma((2,)), dma((3,)), dma((3,)), dma((3,)), dma(()), dma((4,)), dma((4,)),
            dma(()), dma((4,)), dma(()), dma(()), dma(()), dma((4,)),
        ],
        compiler_params=pltpu.CompilerParams(
            collective_id=0, has_side_effects=True, vmem_limit_bytes=60 * 1024 * 1024
        ),
    )(factor, diag_inv, rhs, forward_values)
    solved, rest, back, answer = pl.pallas_call(
        hand_over,
        name="hand_over",
        out_shape=(
            jax.ShapeDtypeStruct((STEPS * NB, COLS), BF16),
            jax.ShapeDtypeStruct((PIECE, NB), F32),
            jax.ShapeDtypeStruct((PIECE, NB), F32),
            jax.ShapeDtypeStruct((NB, COLS), F32),
        ),
        in_specs=[vmem] * 4,
        out_specs=(anywhere,) * 4,
        scratch_shapes=[dma((4,))],
        compiler_params=pltpu.CompilerParams(vmem_limit_bytes=32 * 1024 * 1024),
    )(*results)
    return solved, rest.T, back.T, answer


def solution(mesh):
    placed = (P("row", "col"), P("row", None), P("row", None), P("row", None))
    return jax.shard_map(
        local,
        mesh=mesh,
        in_specs=placed,
        out_specs=(P(), P("row", "col"), P("col", "row"), P("row", None)),
        check_vma=False,
    )
```

```python
import jax
import jax.numpy as jnp
from jax import lax
from jax.experimental import pallas as pl
from jax.experimental.pallas import tpu as pltpu
from jax.sharding import PartitionSpec as P

NB = 1024
COLS = 256
STEPS = 3
NROW = 16
NCOL = 16
PIECE = 16
CHUNK = 64
HALF = 512
TILE = 256
SIDE = (0, 0, 1)
MESH = pl.DeviceIdType.MESH
F32 = jnp.float32
BF16 = jnp.bfloat16


def product(left, right):
    return lax.dot_general(left, right, (((1,), (0,)), ((), ())), preferred_element_type=F32)


def times_lower(left, block):
    parts = []
    for k in range(0, NB, TILE):
        parts.append(product(left[:, k:], block[pl.ds(k, NB - k), pl.ds(k, TILE)]))
    return jnp.concatenate(parts, axis=1)


def times_upper(left, block):
    parts = []
    for k in range(0, NB, TILE):
        parts.append(product(left[:, : k + TILE], block[pl.ds(0, k + TILE), pl.ds(k, TILE)]))
    return jnp.concatenate(parts, axis=1)


def loop(count, body):
    def step(index, carry):
        body(index)
        return carry

    lax.fori_loop(0, count, step, 0)


def kernel(
    factor, inverse, rhs, start,
    so, rest_out, back_out, sl,
    lv, dv, bv, uv, lt, dt, bt, ut,
    yt, vf, yc, pc, yr, pf, rp, qf, qr, qc, tb, wg, wl, vb,
    ready, joined, ld_s,
    yc_r, pc_r, own_r, s3_r, s4_r, rp_r, qr_r, qc_r, tb_r, ag_r, sib_r,
    y0_s, s1_s, s1b_s, s2_s, s3_s, s4_s, pf_s, ch_s, pc_s, qf_s, qc_s, tb_s, w_s, ag_s, sib_s,
):
    r = lax.axis_index("row")
    c = lax.axis_index("col")
    x = c // 4
    yl = (c // 2) % 2
    e = c % 2
    yh = r // 8
    z = r % 8
    y = 2 * yh + yl
    row0 = r == 0
    chain1 = (r == 1) & (c == 0)
    chain20 = (r == 2) & (c == 0)
    chain2 = (r == 2) & (c == 1)
    row13 = r == 13
    row14 = r == 14
    row15 = r == 15
    late = r >= 13
    back1 = (r == 14) & (c == 13)
    group = 2 * (x % 2) + y % 2
    halves = (pl.ds(0, HALF), pl.ds(HALF, HALF))
    mine = pl.ds(pl.multiple_of(group * CHUNK, CHUNK), CHUNK)

    def swap(index):
        return jnp.where(index == 1, 2, jnp.where(index == 2, 1, index))

    def remote(src, dst, send, recv, row, col):
        return pltpu.make_async_remote_copy(
            src_ref=src, dst_ref=dst, send_sem=send, recv_sem=recv, device_id=(row, col), device_id_type=MESH
        )

    def got(ref, sem):
        remote(ref, ref, sem, sem, r, c).wait_recv()

    def sent(ref, sem):
        remote(ref, ref, sem, sem, r, c).wait_send()

    def rows(index, count):
        return pl.ds(pl.multiple_of(index * count, count), count)

    uses_l = ((c < STEPS) & (r > c)) | (late & (c < r))
    uses_d = row0 | chain1 | chain2 | late
    needs = (uses_d, r >= 0, uses_l, late)
    pairs = ((inverse, dv), (rhs, bv), (factor, lv), (start, uv))
    loads = [pltpu.make_async_copy(source, target, ld_s.at[k]) for k, (source, target) in enumerate(pairs)]
    for k in (0, 3, 1, 2):
        pl.when(needs[k])(loads[k].start)
    def source_of(cols):
        found = c == cols[0]
        for col in cols[1:]:
            found = found | (c == col)
        return row0 & found

    to_one = source_of((1, 3, 5, 13))
    to_two = source_of((6, 8, 12, 14))
    barrier = pltpu.get_barrier_semaphore()

    def greet(row, col):
        pl.semaphore_signal(barrier, inc=1, device_id=(row, col), device_id_type=MESH)

    def is_early(row, col):
        return (row == 0) & ((col == 1) | (col == 3) | (col == 5) | (col == 13))

    def meet(run):
        run(r, c + 1 - 2 * e)
        loop(7, lambda k: run(r, lax.rem(c + 2 + 2 * k, 16)))
        loop(8, lambda k: run(lax.rem(r + 8, 16), 2 * k + e))

    def greet_late(row, col):
        pl.when(jnp.logical_not(is_early(row, col)))(lambda: greet(row, col))

    def join(row, col):
        @pl.when(is_early(row, col))
        def _():
            pl.semaphore_signal(joined, inc=1, device_id=(row, col), device_id_type=MESH)

    @pl.when(chain1)
    def _():
        for col in (1, 3, 5, 13):
            greet(0, col)

    @pl.when(chain20)
    def _():
        for col in (6, 8, 12, 14):
            greet(0, col)

    @pl.when(chain2)
    def _():
        greet(1, 0)

    meet(greet_late)
    pl.when((r == 1) & (c != 0))(lambda: greet(1, 0))
    pl.when((r > 0) & (c != 1))(lambda: greet(r, 1))
    pl.when((r > 0) & (c != 2))(lambda: greet(r, 2))
    pl.when(to_one)(lambda: greet(1, c))
    pl.when(r != 13)(lambda: greet(13, c))
    pl.when(r != 14)(lambda: greet(14, c))
    pl.when(r != 15)(lambda: greet(15, c))

    def depth(j):
        return lax.rem(z - j + 8, 8)

    def column(j, far):
        return yh * 8 + lax.rem(far + j, 8)

    def with_children(j, run):
        for parent, children in ((0, (2, 7, 1)), (2, (4, 3)), (7, (6,)), (6, (5,))):

            @pl.when(depth(j) == parent)
            def _():
                run(children)

    for j in range(STEPS):

        @pl.when(e == SIDE[j])
        def _():
            with_children(j, lambda children: [greet_late(column(j, far), c) for far in children])

    @pl.when(row14 & (c != 13))
    def _():
        greet(14, 13)

    @pl.when(row13 & (c != 13))
    def _():
        greet(14, 13)

    @pl.when(back1)
    def _():
        greet(15, 14)

    pl.when(uses_d)(loads[0].wait)

    @pl.when(row0)
    def _():
        loads[1].wait()
        for k in range(0, NB, TILE):
            span = pl.ds(k, TILE)
            value = product(dv[span, pl.ds(0, k + TILE)], bv[pl.ds(0, k + TILE)])
            yr[:, span] = value.astype(BF16).T

    @pl.when(late)
    def _():
        loads[3].wait()
        ut[...] = uv[...].T

    def solve_15(step):
        part = rows(step, 2 * CHUNK)
        value = times_lower(ut[part], dv)
        vf[part] = value
        vb[part] = value.astype(BF16)

    pl.when(row15)(lambda: solve_15(0))
    pl.when(uses_l)(loads[2].wait)

    @pl.when(chain1 | chain2)
    def _():
        dt[...] = dv[...].T

    @pl.when((c < 3) & (r > c))
    def _():
        lt[...] = lv[...].T

    count = 16 + jnp.where(((c == 1) | (c == 2)) & (r > 0) | chain1, 15, 0) + jnp.where(late, 15, 0)
    count = count + jnp.where(e == 0, jnp.where(z < 2, 1, 2), jnp.where(z == 2, 0, 1))
    count = count + jnp.where(to_two | chain1 | (row15 & (c == 14)), 1, 0) + jnp.where(back1, 30, 0)
    count = count + jnp.where((r == 1) & ((c == 1) | (c == 3) | (c == 5) | (c == 13)), 1, 0)
    pl.semaphore_wait(barrier, jnp.where(to_one, 1, count))

    @pl.when(to_one)
    def _():
        for col, chunk in ((1, 3), (5, 2), (13, 1), (3, 0)):

            @pl.when(c == col)
            def _():
                part = pl.ds(chunk * CHUNK, CHUNK)
                remote(yr.at[part], yc.at[part], y0_s, yc_r.at[chunk], 1, 0).start()

        pl.semaphore_wait(joined, 14)

    @pl.when(jnp.logical_not(to_one))
    def _():
        meet(join)
        pl.when((r == 1) & (e == 1))(lambda: join(0, c))

    for j in range(STEPS):
        near = jnp.where(depth(j) == 5, 6, jnp.where(depth(j) == 6, 7, jnp.where((depth(j) == 4) | (depth(j) == 3), 2, 0)))

        @pl.when((e == SIDE[j]) & (depth(j) != 0))
        def _():
            pl.semaphore_signal(ready.at[j], inc=1, device_id=(column(j, near), c), device_id_type=MESH)

    def scatter_pf(chunk):
        for k in range(4):
            g = 4 * chunk + k

            @pl.when(g != c)
            def _():
                remote(pf.at[rows(g, PIECE)], rp.at[c], pf_s, rp_r.at[c], r, g).start()

    def scatter_qf(chunk, wanted=lambda h: True):
        for k in range(4):
            h = 4 * chunk + k

            @pl.when((h != r) & wanted(h))
            def _():
                remote(qf.at[rows(h, PIECE)], qr.at[r - 13], qf_s, qr_r.at[r - 13], h, c).start()

    @pl.when(row0)
    def _():
        for col, chunk in ((6, 3), (8, 2), (14, 1), (12, 0)):

            @pl.when(c == col)
            def _():
                part = pl.ds(chunk * CHUNK, CHUNK)
                remote(yr.at[part], yc.at[part], y0_s, yc_r.at[chunk], 2, 0).start()

        @pl.when(e == SIDE[0])
        def _():
            other = 3 - y
            part = rows(2 * (x % 2) + other % 2, CHUNK)
            for k, side in enumerate(halves):
                to = (8, 4 * x + 2 * (other - 2) + e)
                remote(yr.at[part, side], yt.at[0, part, side], s1_s.at[0], own_r.at[0, k], *to).start()
            yt[0, mine] = yr[mine]

    @pl.when(row15)
    def _():
        def one(step):
            chunk = swap(step)
            part = rows(chunk, CHUNK)
            pl.when(step == 1)(lambda: solve_15(1))

            @pl.when(c < 15)
            def _():
                qf[part] = product(vb[part], lv[...]).astype(BF16)

            for col, target, recv in ((14, qc, qc_r), (13, pc, pc_r)):

                @pl.when(c == col)
                def _():
                    remote(qf.at[part], target.at[part], qc_s.at[chunk], recv.at[chunk], 14, 13).start()

        loop(4, one)

    @pl.when(jnp.logical_not(row0))
    def _():
        loads[1].wait()

    bt[...] = bv[...].T

    def scatter_s1(j, chunk):
        part = rows(chunk, CHUNK)
        a, b = chunk // 2, chunk % 2
        if chunk == 0:
            yt[j, part] = yr[part]
            return
        for side in range(2):
            far = pl.ds(side * HALF, HALF)
            row = j + (8 * b if side else 0)
            col = (12 * a if side else 4 * a) + 2 * b + SIDE[j]
            remote(yr.at[part, far], yt.at[j, part, far], s1_s.at[chunk], own_r.at[j, side], row, col).start()

    heads = ((x < 2) & (y < 2), ((x == 0) | (x == 3)) & ((y == 0) | (y == 3)))

    def spread(j):
        root = (chain1 & (j == 1)) | (chain2 & (j == 2))
        local = root | (row0 & (j == 0))
        starts = (z == j) & (j > 0)
        turned = starts & heads[1] & jnp.logical_not(heads[0])

        def part_of(side):
            return yt.at[j, mine, pl.ds(pl.multiple_of(side * HALF, HALF), HALF)]

        def to_chip(side, send, recv, tx, ty):
            part = part_of(side)
            remote(part, part, send, recv, 8 * (ty // 2) + z, 4 * tx + 2 * (ty % 2) + e).start()

        def around(side):
            x2, y2 = lax.rem(x + 2, 4), lax.rem(y + 2, 4)
            to_chip(side, s1b_s.at[side], own_r.at[j, side], x2, y2)
            to_chip(side, s1b_s.at[side], own_r.at[j, side], x2, y)
            to_chip(side, s1b_s.at[side], own_r.at[j, side], x, y2)

        def along(side, opening):
            def run(children):
                if opening:
                    pl.semaphore_wait(ready.at[j], len(children))
                part = part_of(side)
                for far in children:
                    remote(part, part, s2_s.at[j], own_r.at[j, side], column(j, far), c).start()

            with_children(j, run)

        def across(side):
            x1, y1 = lax.rem(x + 1 + 2 * side, 4), lax.rem(y + 1 + 2 * side, 4)
            to_chip(side, s3_s.at[j], s3_r.at[j, group], x1, y1)
            to_chip(side, s3_s.at[j], s3_r.at[j, group], x1, y)
            to_chip(side, s3_s.at[j], s3_r.at[j, group], x, y1)

        for step in range(2):
            side = jnp.where(turned, 1 - step, step)

            @pl.when(jnp.logical_not(local))
            def _():
                got(part_of(side), own_r.at[j, side])

            @pl.when(starts & jnp.where(side == 0, heads[0], heads[1]))
            def _():
                around(side)

            @pl.when(jnp.logical_not(root))
            def _():
                along(side, step == 0)
                across(side)

        @pl.when(root)
        def _():
            @pl.when(chain1)
            def _():
                for k in range(4):
                    sent(yr.at[pl.ds(0, CHUNK)], ch_s.at[k])

            for side in range(2):
                along(side, side == 0)
            for side in range(2):
                sent(yt.at[0, pl.ds(0, 192), halves[side]], s1b_s.at[side])
            for side in range(2):
                across(side)

        block = yt.at[j, mine]
        remote(block, block, s4_s.at[j], s4_r.at[j, group], r, c + 1 - 2 * e).start()

    def collect(j):
        def one(step):
            chunk = 3 - step
            block = yt.at[j, rows(chunk, CHUNK)]

            @pl.when(chunk != group)
            def _():
                got(block, s3_r.at[j, chunk])
                remote(block, block, s4_s.at[j], s4_r.at[j, chunk], r, c + 1 - 2 * e).start()

        loop(4, one)

    def await_other(j):
        loop(4, lambda step: got(yt.at[j, rows(3 - step, CHUNK)], s4_r.at[j, 3 - step]))

    def apply(j):
        def one(step):
            part = rows(1 - step, 2 * CHUNK)
            pair = (3 - 2 * step, 2 - 2 * step)

            @pl.when(e != SIDE[j])
            def _():
                for chunk in pair:
                    got(yt.at[j, rows(chunk, CHUNK)], s4_r.at[j, chunk])

            @pl.when((c == j) & (r >= 3))
            def _():
                partial = product(yt[j, part], lt[...]).astype(BF16)
                if j == 1:
                    for chunk in pair:
                        got(pc.at[rows(chunk, CHUNK)], pc_r.at[chunk])
                    partial = (pc[part].astype(F32) + partial.astype(F32)).astype(BF16)
                pf[part] = partial
                for chunk in pair:
                    if j == 0:
                        half = rows(chunk, CHUNK)
                        remote(pf.at[half], pc.at[half], pc_s.at[chunk], pc_r.at[chunk], r, 1).start()
                    else:
                        scatter_pf(chunk)

        loop(2, one)
        so[pl.ds(j * NB, NB)] = yt[j].T

    def centre():
        block = wg.at[x, yl, e]

        @pl.when(row13)
        def _():
            got(tb, tb_r.at[0])
            block[...] = (ut[rows(c, PIECE)].astype(F32) - tb[...].astype(F32)).astype(BF16)

        @pl.when(row14 & (c != 13))
        def _():
            got(block, tb_r.at[0])

        @pl.when(row14 | row13)
        def _():
            def one(k):
                to = lax.rem(2 * x + yl + 1 + k, 8)
                remote(block, block, ag_s, ag_r.at[x], r, 2 * to + e).start()

            loop(7, one)

    def gather_and_solve():
        def one(step):
            pair = (step, step + 2)
            for chunk in pair:

                @pl.when(chunk == x)
                def _():
                    got(wg.at[chunk, 0, e], ag_r.at[chunk])

                @pl.when(chunk != x)
                def _():
                    got(wg.at[chunk, :, e], ag_r.at[chunk])

                block = wg.at[chunk, :, e]
                remote(block, block, sib_s.at[chunk], sib_r.at[chunk], r, c + 1 - 2 * e).start()

            for chunk in pair:
                got(wg.at[chunk, :, 1 - e], sib_r.at[chunk])
            operand = jnp.concatenate([wg[chunk].reshape(CHUNK, NB) for chunk in pair], axis=0)
            answer = times_lower(operand, dv)
            for k, chunk in enumerate(pair):
                vf[rows(chunk, CHUNK)] = answer[k * CHUNK:(k + 1) * CHUNK]

            @pl.when((c < r) & jnp.logical_not(back1))
            def _():
                partial = product(answer.astype(BF16), lv[...]).astype(BF16)
                for k, chunk in enumerate(pair):
                    qf[rows(chunk, CHUNK)] = partial[k * CHUNK:(k + 1) * CHUNK]

            @pl.when(c < r)
            def _():
                for chunk in pair:
                    scatter_qf(chunk)

            @pl.when((step == 0) & (e == 0))
            def _():
                spread(1)

        loop(2, one)

        @pl.when(e == 1)
        def _():
            spread(2)

    @pl.when(chain1)
    def _():
        def one(step):
            chunk = 3 - step
            part = rows(chunk, CHUNK)
            got(yc.at[part], yc_r.at[chunk])
            partial = product(yc[part], lt[...]).astype(BF16)
            pf[part] = partial
            residue = (bt[part].astype(F32) - partial.astype(F32)).astype(BF16)
            yr[part] = times_upper(residue, dt).astype(BF16)
            remote(yr.at[part], yc.at[part], ch_s.at[chunk], yc_r.at[chunk], 2, 1).start()
            for k in range(4):
                pl.when(chunk == k)(lambda: scatter_s1(1, k))

        loop(4, one)

    @pl.when(chain20)
    def _():
        def one(step):
            chunk = 3 - step
            part = rows(chunk, CHUNK)
            got(yc.at[part], yc_r.at[chunk])
            pf[part] = product(yc[part], lt[...]).astype(BF16)
            remote(pf.at[part], pc.at[part], pc_s.at[chunk], pc_r.at[chunk], 2, 1).start()

        loop(4, one)

    @pl.when(chain2)
    def _():
        def one(step):
            chunk = 3 - step
            part = rows(chunk, CHUNK)
            got(yc.at[part], yc_r.at[chunk])
            partial = product(yc[part], lt[...]).astype(BF16)
            got(pc.at[part], pc_r.at[chunk])
            total = pc[part].astype(F32) + partial.astype(F32)
            pf[part] = total.astype(BF16)
            residue = (bt[part].astype(F32) - total).astype(BF16)
            yr[part] = times_upper(residue, dt).astype(BF16)
            for k in range(4):
                pl.when(chunk == k)(lambda: scatter_s1(2, k))

        loop(4, one)

    @pl.when(back1)
    def _():
        def one(step):
            chunk = swap(step)
            part = rows(chunk, CHUNK)
            got(qc.at[part], qc_r.at[chunk])
            centred = (ut[part].astype(F32) - qc[part].astype(F32)).astype(BF16)
            wl[part] = centred
            for k in range(4):
                piece = rows(4 * chunk + k, PIECE)
                to = 4 * chunk + k
                target = wg.at[chunk, k // 2, k % 2]

                @pl.when(to != c)
                def _():
                    remote(wl.at[piece], target, w_s, tb_r.at[0], 14, to).start()

                @pl.when(to == c)
                def _():
                    target[...] = wl[piece]

            answer = times_lower(centred, dv).astype(BF16)
            partial = product(answer, lv[...]).astype(BF16)
            qf[part] = partial
            got(pc.at[part], pc_r.at[chunk])
            yc[part] = (pc[part].astype(F32) + partial.astype(F32)).astype(BF16)
            for k in range(4):
                piece = rows(4 * chunk + k, PIECE)
                to = 4 * chunk + k
                remote(yc.at[piece], tb, tb_s, tb_r.at[0], 13, to).start()
        loop(4, one)

    middle = row13 | row14
    first_two = (jnp.where(z == 1, 1, 0), jnp.where(e == 1, 2, jnp.where(z == 1, 0, 1)))

    def below(h):
        return (h % 8 >= 3) & (h % 8 < 7)

    @pl.when((e == 0) & jnp.logical_not(row13))
    def _():
        spread(first_two[0])

    @pl.when(row15 & (c < 15))
    def _():
        loop(4, lambda chunk: scatter_qf(chunk, lambda h: jnp.logical_not(below(h))))

    centre()

    @pl.when((e == 0) & row13)
    def _():
        spread(0)

    pl.when((e == 1) & row15)(lambda: await_other(0))

    @pl.when((e == 1) & row15 & (c < 15))
    def _():
        loop(4, lambda chunk: scatter_qf(chunk, below))

    @pl.when(jnp.logical_not(middle))
    def _():
        spread(first_two[1])

    @pl.when((e == 0) & row15)
    def _():
        loop(4, lambda chunk: scatter_qf(chunk, below))

    @pl.when((e == 0) & jnp.logical_not(middle))
    def _():
        collect(0)
        apply(0)

    @pl.when(middle)
    def _():
        gather_and_solve()

    @pl.when((e == 0) & middle)
    def _():
        collect(0)
        apply(0)

    @pl.when(chain1 | chain2)
    def _():
        loop(4, scatter_pf)

    @pl.when(e == 0)
    def _():
        collect(1)
        apply(1)

    @pl.when(e == 1)
    def _():
        collect(2)
        pl.when(jnp.logical_not(row15))(lambda: await_other(0))
        so[pl.ds(0, NB)] = yt[0].T
        apply(1)

    apply(2)

    @pl.when(late)
    def _():
        sl[...] = vf[...].T

    @pl.when(jnp.logical_not(late))
    def _():
        sl[...] = jnp.zeros_like(sl)

    for j in range(STEPS):

        @pl.when(e == SIDE[j])
        def _():
            sent(yt.at[j, pl.ds(0, 192)], s3_s.at[j])
            sent(yt.at[j], s4_s.at[j])
            with_children(j, lambda children: sent(yt.at[j, pl.ds(0, len(children) * CHUNK)], s2_s.at[j]))

    for k in range(2):

        @pl.when(((z == 1) & (e == 0) | (z == 2) & (e == 1)) & heads[k] & jnp.logical_not(chain1 | chain2))
        def _():
            sent(yt.at[0, pl.ds(0, 192), halves[k]], s1b_s.at[k])

    @pl.when(row0)
    def _():
        @pl.when(to_one | to_two)
        def _():
            sent(yr.at[pl.ds(0, CHUNK)], y0_s)

        @pl.when(e == SIDE[0])
        def _():
            sent(yr.at[pl.ds(0, CHUNK)], s1_s.at[0])

    @pl.when(chain1 | chain2)
    def _():
        for k in range(1, 4):
            sent(yr.at[pl.ds(0, CHUNK)], s1_s.at[k])

    @pl.when((c == 0) & (r >= 2))
    def _():
        for k in range(4):
            sent(pf.at[pl.ds(0, CHUNK)], pc_s.at[k])

    @pl.when(chain1 | ((c == 1) & (r >= 2)) | ((c == 2) & (r >= 3)))
    def _():
        sent(pf.at[pl.ds(0, 240)], pf_s)

    @pl.when(late & (c < r))
    def _():
        sent(qf.at[pl.ds(0, 240)], qf_s)

    @pl.when(row15 & ((c == 13) | (c == 14)))
    def _():
        for k in range(4):
            sent(qf.at[pl.ds(0, CHUNK)], qc_s.at[k])

    @pl.when(back1)
    def _():
        sent(qf, tb_s)

    @pl.when(back1)
    def _():
        sent(qf.at[pl.ds(0, 240)], w_s)

    @pl.when(row14 | row13)
    def _():
        sent(qf.at[pl.ds(0, 112)], ag_s)
        for k in range(4):
            sent(wg.at[0, :, 0], sib_s.at[k])

    rest_out[...] = bt[rows(c, PIECE)].astype(F32)
    for j in range(STEPS):

        @pl.when((r == 1) if j == 0 else (r > j))
        def _():
            @pl.when(c == j)
            def _():
                rest_out[...] -= pf[rows(c, PIECE)].astype(F32)

            @pl.when(c != j)
            def _():
                got(rp.at[j], rp_r.at[j])
                rest_out[...] -= rp[j].astype(F32)

    back_out[...] = jnp.zeros_like(back_out)
    for j in range(STEPS):

        @pl.when(c < 13 + j)
        def _():
            @pl.when(r == 13 + j)
            def _():
                back_out[...] += qf[rows(r, PIECE)].astype(F32)

            @pl.when(r != 13 + j)
            def _():
                got(qr.at[j], qr_r.at[j])
                back_out[...] += qr[j].astype(F32)


def hand_over(*refs):
    sems = refs[-1]
    copies = [pltpu.make_async_copy(refs[k], refs[k + 4], sems.at[k]) for k in range(4)]
    for copy in copies:
        copy.start()
    for copy in copies:
        copy.wait()


def local(factor, diag_inv, rhs, forward_values):
    anywhere = pl.BlockSpec(memory_space=pl.ANY)
    vmem = pl.BlockSpec(memory_space=pltpu.VMEM)
    dma = pltpu.SemaphoreType.DMA
    square = pltpu.VMEM((NB, NB), BF16)
    tall = pltpu.VMEM((NB, COLS), BF16)
    wide = pltpu.VMEM((COLS, NB), BF16)
    results = pl.pallas_call(
        kernel,
        name="solves",
        out_shape=(
            pltpu.VMEM((STEPS * NB, COLS), BF16),
            pltpu.VMEM((PIECE, NB), F32),
            pltpu.VMEM((PIECE, NB), F32),
            pltpu.VMEM((NB, COLS), F32),
        ),
        in_specs=[anywhere] * 4,
        out_specs=(vmem,) * 4,
        scratch_shapes=[
            square, square, tall, tall, square, square, wide, wide,
            pltpu.VMEM((STEPS, COLS, NB), BF16),
            pltpu.VMEM((COLS, NB), F32),
            wide, wide, wide, wide,
            pltpu.VMEM((STEPS, PIECE, NB), BF16),
            wide,
            pltpu.VMEM((STEPS, PIECE, NB), BF16),
            wide,
            pltpu.VMEM((PIECE, NB), BF16),
            pltpu.VMEM((4, 2, 2, PIECE, NB), BF16),
            wide,
            wide,
            pltpu.SemaphoreType.REGULAR((3,)), pltpu.SemaphoreType.REGULAR, dma((4,)),
            dma((4,)), dma((4,)), dma((3, 2)), dma((3, 4)), dma((3, 4)), dma((3,)), dma((3,)), dma((4,)), dma((2,)),
            dma((4,)), dma((4,)),
            dma(()), dma((4,)), dma((2,)), dma((3,)), dma((3,)), dma((3,)), dma(()), dma((4,)), dma((4,)),
            dma(()), dma((4,)), dma(()), dma(()), dma(()), dma((4,)),
        ],
        compiler_params=pltpu.CompilerParams(
            collective_id=0, has_side_effects=True, vmem_limit_bytes=60 * 1024 * 1024
        ),
    )(factor, diag_inv, rhs, forward_values)
    solved, rest, back, answer = pl.pallas_call(
        hand_over,
        name="hand_over",
        out_shape=(
            jax.ShapeDtypeStruct((STEPS * NB, COLS), BF16),
            jax.ShapeDtypeStruct((PIECE, NB), F32),
            jax.ShapeDtypeStruct((PIECE, NB), F32),
            jax.ShapeDtypeStruct((NB, COLS), F32),
        ),
        in_specs=[vmem] * 4,
        out_specs=(anywhere,) * 4,
        scratch_shapes=[dma((4,))],
        compiler_params=pltpu.CompilerParams(vmem_limit_bytes=32 * 1024 * 1024),
    )(*results)
    return solved, rest.T, back.T, answer


def solution(mesh):
    placed = (P("row", "col"), P("row", None), P("row", None), P("row", None))
    return jax.shard_map(
        local,
        mesh=mesh,
        in_specs=placed,
        out_specs=(P(), P("row", "col"), P("col", "row"), P("row", None)),
        check_vma=False,
    )
```

```python
import jax
import jax.numpy as jnp
from jax import lax
from jax.experimental import pallas as pl
from jax.experimental.pallas import tpu as pltpu
from jax.sharding import PartitionSpec as P

NB = 1024
COLS = 256
STEPS = 3
NROW = 16
NCOL = 16
PIECE = 16
CHUNK = 64
HALF = 512
TILE = 256
SIDE = (0, 0, 1)
MESH = pl.DeviceIdType.MESH
F32 = jnp.float32
BF16 = jnp.bfloat16


def product(left, right):
    return lax.dot_general(left, right, (((1,), (0,)), ((), ())), preferred_element_type=F32)


def times_lower(left, block):
    parts = []
    for k in range(0, NB, TILE):
        parts.append(product(left[:, k:], block[pl.ds(k, NB - k), pl.ds(k, TILE)]))
    return jnp.concatenate(parts, axis=1)


def times_upper(left, block):
    parts = []
    for k in range(0, NB, TILE):
        parts.append(product(left[:, : k + TILE], block[pl.ds(0, k + TILE), pl.ds(k, TILE)]))
    return jnp.concatenate(parts, axis=1)


def loop(count, body):
    def step(index, carry):
        body(index)
        return carry

    lax.fori_loop(0, count, step, 0)


def kernel(
    factor, inverse, rhs, start,
    so, rest_out, back_out, sl,
    lv, dv, bv, uv, lt, dt, bt, ut,
    yt, vf, yc, pc, yr, pf, rp, qf, qr, qc, tb, wg, wl, vb,
    ready, joined, ld_s,
    yc_r, pc_r, own_r, s3_r, s4_r, rp_r, qr_r, tb_r, ag_r, sib_r,
    y0_s, s1_s, s1b_s, s2_s, s3_s, s4_s, pf_s, ch_s, qf_s, w_s, ag_s,
):
    qc_r, pc_s, qc_s, sib_s, tb_s = yc_r, ch_s, ch_s, s1_s, y0_s
    r = lax.axis_index("row")
    c = lax.axis_index("col")
    x = c // 4
    yl = (c // 2) % 2
    e = c % 2
    yh = r // 8
    z = r % 8
    y = 2 * yh + yl
    row0 = r == 0
    chain1 = (r == 1) & (c == 0)
    chain20 = (r == 2) & (c == 0)
    chain2 = (r == 2) & (c == 1)
    row13 = r == 13
    row14 = r == 14
    row15 = r == 15
    late = r >= 13
    back1 = (r == 14) & (c == 13)
    group = 2 * (x % 2) + y % 2
    halves = (pl.ds(0, HALF), pl.ds(HALF, HALF))
    mine = pl.ds(pl.multiple_of(group * CHUNK, CHUNK), CHUNK)

    def swap(index):
        return jnp.where(index == 1, 2, jnp.where(index == 2, 1, index))

    def remote(src, dst, send, recv, row, col):
        return pltpu.make_async_remote_copy(
            src_ref=src, dst_ref=dst, send_sem=send, recv_sem=recv, device_id=(row, col), device_id_type=MESH
        )

    def got(ref, sem):
        remote(ref, ref, sem, sem, r, c).wait_recv()

    def sent(ref, sem):
        remote(ref, ref, sem, sem, r, c).wait_send()

    def rows(index, count):
        return pl.ds(pl.multiple_of(index * count, count), count)

    uses_l = ((c < STEPS) & (r > c)) | (late & (c < r))
    uses_d = row0 | chain1 | chain2 | late
    needs = (uses_d, r >= 0, uses_l, late)
    pairs = ((inverse, dv), (rhs, bv), (factor, lv), (start, uv))
    loads = [pltpu.make_async_copy(source, target, ld_s.at[k]) for k, (source, target) in enumerate(pairs)]
    for k in (0, 3, 1, 2):
        pl.when(needs[k])(loads[k].start)
    def source_of(cols):
        found = c == cols[0]
        for col in cols[1:]:
            found = found | (c == col)
        return row0 & found

    to_one = source_of((1, 3, 5, 13))
    to_two = source_of((6, 8, 12, 14))
    barrier = pltpu.get_barrier_semaphore()

    def greet(row, col):
        pl.semaphore_signal(barrier, inc=1, device_id=(row, col), device_id_type=MESH)

    def is_early(row, col):
        return (row == 0) & ((col == 1) | (col == 3) | (col == 5) | (col == 13))

    def meet(run):
        run(r, c + 1 - 2 * e)
        loop(7, lambda k: run(r, lax.rem(c + 2 + 2 * k, 16)))
        loop(8, lambda k: run(lax.rem(r + 8, 16), 2 * k + e))

    def greet_late(row, col):
        pl.when(jnp.logical_not(is_early(row, col)))(lambda: greet(row, col))

    def join(row, col):
        @pl.when(is_early(row, col))
        def _():
            pl.semaphore_signal(joined, inc=1, device_id=(row, col), device_id_type=MESH)

    @pl.when(chain1)
    def _():
        for col in (1, 3, 5, 13):
            greet(0, col)

    @pl.when(chain20)
    def _():
        for col in (6, 8, 12, 14):
            greet(0, col)

    @pl.when(chain2)
    def _():
        greet(1, 0)

    meet(greet_late)
    pl.when((r == 1) & (c != 0))(lambda: greet(1, 0))
    pl.when((r > 0) & (c != 1))(lambda: greet(r, 1))
    pl.when((r > 0) & (c != 2))(lambda: greet(r, 2))
    pl.when(to_one)(lambda: greet(1, c))
    pl.when(r != 13)(lambda: greet(13, c))
    pl.when(r != 14)(lambda: greet(14, c))
    pl.when(r != 15)(lambda: greet(15, c))

    def depth(j):
        return lax.rem(z - j + 8, 8)

    def column(j, far):
        return yh * 8 + lax.rem(far + j, 8)

    def with_children(j, run):
        for parent, children in ((0, (2, 7, 1)), (2, (4, 3)), (7, (6,)), (6, (5,))):

            @pl.when(depth(j) == parent)
            def _():
                run(children)

    for j in range(STEPS):

        @pl.when(e == SIDE[j])
        def _():
            with_children(j, lambda children: [greet_late(column(j, far), c) for far in children])

    @pl.when(row14 & (c != 13))
    def _():
        greet(14, 13)

    @pl.when(row13 & (c != 13))
    def _():
        greet(14, 13)

    @pl.when(back1)
    def _():
        greet(15, 14)

    pl.when(uses_d)(loads[0].wait)

    @pl.when(row0)
    def _():
        loads[1].wait()
        for k in range(0, NB, TILE):
            span = pl.ds(k, TILE)
            value = product(dv[span, pl.ds(0, k + TILE)], bv[pl.ds(0, k + TILE)])
            yr[:, span] = value.astype(BF16).T

    @pl.when(late)
    def _():
        loads[3].wait()
        ut[...] = uv[...].T

    def solve_15(step):
        part = rows(step, 2 * CHUNK)
        value = times_lower(ut[part], dv)
        vf[part] = value
        vb[part] = value.astype(BF16)

    pl.when(row15)(lambda: solve_15(0))
    pl.when(uses_l)(loads[2].wait)

    @pl.when(chain1 | chain2)
    def _():
        dt[...] = dv[...].T

    @pl.when((c < 3) & (r > c))
    def _():
        lt[...] = lv[...].T

    count = 16 + jnp.where(((c == 1) | (c == 2)) & (r > 0) | chain1, 15, 0) + jnp.where(late, 15, 0)
    count = count + jnp.where(e == 0, jnp.where(z < 2, 1, 2), jnp.where(z == 2, 0, 1))
    count = count + jnp.where(to_two | chain1 | (row15 & (c == 14)), 1, 0) + jnp.where(back1, 30, 0)
    count = count + jnp.where((r == 1) & ((c == 1) | (c == 3) | (c == 5) | (c == 13)), 1, 0)
    pl.semaphore_wait(barrier, jnp.where(to_one, 1, count))

    @pl.when(to_one)
    def _():
        for col, chunk in ((1, 3), (5, 2), (13, 1), (3, 0)):

            @pl.when(c == col)
            def _():
                part = pl.ds(chunk * CHUNK, CHUNK)
                remote(yr.at[part], yc.at[part], y0_s, yc_r.at[chunk], 1, 0).start()

        pl.semaphore_wait(joined, 14)

    @pl.when(jnp.logical_not(to_one))
    def _():
        meet(join)
        pl.when((r == 1) & (e == 1))(lambda: join(0, c))

    for j in range(STEPS):
        near = jnp.where(depth(j) == 5, 6, jnp.where(depth(j) == 6, 7, jnp.where((depth(j) == 4) | (depth(j) == 3), 2, 0)))

        @pl.when((e == SIDE[j]) & (depth(j) != 0))
        def _():
            pl.semaphore_signal(ready.at[j % 2], inc=1, device_id=(column(j, near), c), device_id_type=MESH)

    def scatter_pf(chunk):
        for k in range(4):
            g = 4 * chunk + k

            @pl.when(g != c)
            def _():
                remote(pf.at[rows(g, PIECE)], rp.at[c], pf_s, rp_r.at[c], r, g).start()

    def scatter_qf(chunk, wanted=lambda h: True):
        for k in range(4):
            h = 4 * chunk + k

            @pl.when((h != r) & wanted(h))
            def _():
                remote(qf.at[rows(h, PIECE)], qr.at[r - 13], qf_s, qr_r.at[r - 13], h, c).start()

    @pl.when(row0)
    def _():
        for col, chunk in ((6, 3), (8, 2), (14, 1), (12, 0)):

            @pl.when(c == col)
            def _():
                part = pl.ds(chunk * CHUNK, CHUNK)
                remote(yr.at[part], yc.at[part], y0_s, yc_r.at[chunk], 2, 0).start()

        @pl.when(e == SIDE[0])
        def _():
            other = 3 - y
            part = rows(2 * (x % 2) + other % 2, CHUNK)
            for k, side in enumerate(halves):
                to = (8, 4 * x + 2 * (other - 2) + e)
                remote(yr.at[part, side], yt.at[0, part, side], s1_s.at[0], own_r.at[0, k], *to).start()
            yt[0, mine] = yr[mine]

    @pl.when(row15)
    def _():
        def one(step):
            chunk = swap(step)
            part = rows(chunk, CHUNK)
            pl.when(step == 1)(lambda: solve_15(1))

            @pl.when(c < 15)
            def _():
                qf[part] = product(vb[part], lv[...]).astype(BF16)

            for col, target, recv in ((14, qc, qc_r), (13, pc, pc_r)):

                @pl.when(c == col)
                def _():
                    remote(qf.at[part], target.at[part], qc_s.at[chunk], recv.at[chunk], 14, 13).start()

        loop(4, one)

    @pl.when(jnp.logical_not(row0))
    def _():
        loads[1].wait()

    bt[...] = bv[...].T

    def scatter_s1(j, chunk):
        part = rows(chunk, CHUNK)
        a, b = chunk // 2, chunk % 2
        if chunk == 0:
            yt[j, part] = yr[part]
            return
        for side in range(2):
            far = pl.ds(side * HALF, HALF)
            row = j + (8 * b if side else 0)
            col = (12 * a if side else 4 * a) + 2 * b + SIDE[j]
            remote(yr.at[part, far], yt.at[j, part, far], s1_s.at[chunk], own_r.at[j % 2, side], row, col).start()

    heads = ((x < 2) & (y < 2), ((x == 0) | (x == 3)) & ((y == 0) | (y == 3)))

    def spread(j):
        root = (chain1 & (j == 1)) | (chain2 & (j == 2))
        local = root | (row0 & (j == 0))
        starts = (z == j) & (j > 0)
        turned = starts & heads[1] & jnp.logical_not(heads[0])

        def part_of(side):
            return yt.at[j, mine, pl.ds(pl.multiple_of(side * HALF, HALF), HALF)]

        def to_chip(side, send, recv, tx, ty):
            part = part_of(side)
            remote(part, part, send, recv, 8 * (ty // 2) + z, 4 * tx + 2 * (ty % 2) + e).start()

        def around(side):
            x2, y2 = lax.rem(x + 2, 4), lax.rem(y + 2, 4)
            to_chip(side, s1b_s.at[side], own_r.at[j % 2, side], x2, y2)
            to_chip(side, s1b_s.at[side], own_r.at[j % 2, side], x2, y)
            to_chip(side, s1b_s.at[side], own_r.at[j % 2, side], x, y2)

        def along(side, opening):
            def run(children):
                if opening:
                    pl.semaphore_wait(ready.at[j % 2], len(children))
                part = part_of(side)
                for far in children:
                    remote(part, part, s2_s.at[j % 2], own_r.at[j % 2, side], column(j, far), c).start()

            with_children(j, run)

        def across(side):
            x1, y1 = lax.rem(x + 1 + 2 * side, 4), lax.rem(y + 1 + 2 * side, 4)
            to_chip(side, s3_s.at[j % 2], s3_r.at[j % 2, group], x1, y1)
            to_chip(side, s3_s.at[j % 2], s3_r.at[j % 2, group], x1, y)
            to_chip(side, s3_s.at[j % 2], s3_r.at[j % 2, group], x, y1)

        for step in range(2):
            side = jnp.where(turned, 1 - step, step)

            @pl.when(jnp.logical_not(local))
            def _():
                got(part_of(side), own_r.at[j % 2, side])

            @pl.when(starts & jnp.where(side == 0, heads[0], heads[1]))
            def _():
                around(side)

            @pl.when(jnp.logical_not(root))
            def _():
                along(side, step == 0)
                across(side)

        @pl.when(root)
        def _():
            @pl.when(chain1)
            def _():
                for k in range(4):
                    sent(yr.at[pl.ds(0, CHUNK)], ch_s.at[k])

            for side in range(2):
                along(side, side == 0)
            for side in range(2):
                sent(yt.at[0, pl.ds(0, 192), halves[side]], s1b_s.at[side])
            for side in range(2):
                across(side)

        block = yt.at[j, mine]
        remote(block, block, s4_s.at[j % 2], s4_r.at[j % 2, group], r, c + 1 - 2 * e).start()

    def collect(j):
        def one(step):
            chunk = 3 - step
            block = yt.at[j, rows(chunk, CHUNK)]

            @pl.when(chunk != group)
            def _():
                got(block, s3_r.at[j % 2, chunk])
                remote(block, block, s4_s.at[j % 2], s4_r.at[j % 2, chunk], r, c + 1 - 2 * e).start()

        loop(4, one)

    def await_other(j):
        loop(4, lambda step: got(yt.at[j, rows(3 - step, CHUNK)], s4_r.at[j % 2, 3 - step]))

    def apply(j):
        def one(step):
            part = rows(1 - step, 2 * CHUNK)
            pair = (3 - 2 * step, 2 - 2 * step)

            @pl.when(e != SIDE[j])
            def _():
                for chunk in pair:
                    got(yt.at[j, rows(chunk, CHUNK)], s4_r.at[j % 2, chunk])

            @pl.when((c == j) & (r >= 3))
            def _():
                partial = product(yt[j, part], lt[...]).astype(BF16)
                if j == 1:
                    for chunk in pair:
                        got(pc.at[rows(chunk, CHUNK)], pc_r.at[chunk])
                    partial = (pc[part].astype(F32) + partial.astype(F32)).astype(BF16)
                pf[part] = partial
                for chunk in pair:
                    if j == 0:
                        half = rows(chunk, CHUNK)
                        remote(pf.at[half], pc.at[half], pc_s.at[chunk], pc_r.at[chunk], r, 1).start()
                    else:
                        scatter_pf(chunk)

        loop(2, one)
        so[pl.ds(j * NB, NB)] = yt[j].T

    def centre():
        block = wg.at[x, yl, e]

        @pl.when(row13)
        def _():
            got(tb, tb_r.at[0])
            block[...] = (ut[rows(c, PIECE)].astype(F32) - tb[...].astype(F32)).astype(BF16)

        @pl.when(row14 & (c != 13))
        def _():
            got(block, tb_r.at[0])

        @pl.when(row14 | row13)
        def _():
            for ahead in (4, 5, 3, 2, 6, 7, 1):
                to = lax.rem(2 * x + yl + ahead, 8)
                remote(block, block, ag_s, ag_r.at[x], r, 2 * to + e).start()

    def gather_and_solve():
        def one(step):
            pair = (step, step + 2)
            for chunk in pair:

                @pl.when(chunk == x)
                def _():
                    got(wg.at[chunk, 0, e], ag_r.at[chunk])

                @pl.when(chunk != x)
                def _():
                    got(wg.at[chunk, :, e], ag_r.at[chunk])

                block = wg.at[chunk, :, e]
                remote(block, block, sib_s.at[chunk], sib_r.at[chunk], r, c + 1 - 2 * e).start()

            for chunk in pair:
                got(wg.at[chunk, :, 1 - e], sib_r.at[chunk])
            operand = jnp.concatenate([wg[chunk].reshape(CHUNK, NB) for chunk in pair], axis=0)
            answer = times_lower(operand, dv)
            for k, chunk in enumerate(pair):
                vf[rows(chunk, CHUNK)] = answer[k * CHUNK:(k + 1) * CHUNK]

            @pl.when((c < r) & jnp.logical_not(back1))
            def _():
                partial = product(answer.astype(BF16), lv[...]).astype(BF16)
                for k, chunk in enumerate(pair):
                    qf[rows(chunk, CHUNK)] = partial[k * CHUNK:(k + 1) * CHUNK]

            @pl.when(c < r)
            def _():
                for chunk in pair:
                    scatter_qf(chunk)

            @pl.when((step == 0) & (e == 0))
            def _():
                spread(1)

        loop(2, one)

        @pl.when(e == 1)
        def _():
            spread(2)

    @pl.when(chain1)
    def _():
        def one(step):
            chunk = 3 - step
            part = rows(chunk, CHUNK)
            got(yc.at[part], yc_r.at[chunk])
            partial = product(yc[part], lt[...]).astype(BF16)
            pf[part] = partial
            residue = (bt[part].astype(F32) - partial.astype(F32)).astype(BF16)
            yr[part] = times_upper(residue, dt).astype(BF16)
            remote(yr.at[part], yc.at[part], ch_s.at[chunk], yc_r.at[chunk], 2, 1).start()
            for k in range(4):
                pl.when(chunk == k)(lambda: scatter_s1(1, k))

        loop(4, one)

    @pl.when(chain20)
    def _():
        def one(step):
            chunk = 3 - step
            part = rows(chunk, CHUNK)
            got(yc.at[part], yc_r.at[chunk])
            pf[part] = product(yc[part], lt[...]).astype(BF16)
            remote(pf.at[part], pc.at[part], pc_s.at[chunk], pc_r.at[chunk], 2, 1).start()

        loop(4, one)

    @pl.when(chain2)
    def _():
        def one(step):
            chunk = 3 - step
            part = rows(chunk, CHUNK)
            got(yc.at[part], yc_r.at[chunk])
            partial = product(yc[part], lt[...]).astype(BF16)
            got(pc.at[part], pc_r.at[chunk])
            total = pc[part].astype(F32) + partial.astype(F32)
            pf[part] = total.astype(BF16)
            residue = (bt[part].astype(F32) - total).astype(BF16)
            yr[part] = times_upper(residue, dt).astype(BF16)
            for k in range(4):
                pl.when(chunk == k)(lambda: scatter_s1(2, k))

        loop(4, one)

    @pl.when(back1)
    def _():
        def one(step):
            chunk = swap(step)
            part = rows(chunk, CHUNK)
            got(qc.at[part], qc_r.at[chunk])
            centred = (ut[part].astype(F32) - qc[part].astype(F32)).astype(BF16)
            wl[part] = centred
            for k in range(4):
                piece = rows(4 * chunk + k, PIECE)
                to = 4 * chunk + k
                target = wg.at[chunk, k // 2, k % 2]

                @pl.when(to != c)
                def _():
                    remote(wl.at[piece], target, w_s, tb_r.at[0], 14, to).start()

                @pl.when(to == c)
                def _():
                    target[...] = wl[piece]

            answer = times_lower(centred, dv).astype(BF16)
            partial = product(answer, lv[...]).astype(BF16)
            qf[part] = partial
            got(pc.at[part], pc_r.at[chunk])
            yc[part] = (pc[part].astype(F32) + partial.astype(F32)).astype(BF16)
            for k in range(4):
                piece = rows(4 * chunk + k, PIECE)
                to = 4 * chunk + k
                remote(yc.at[piece], tb, tb_s, tb_r.at[0], 13, to).start()
        loop(4, one)

    middle = row13 | row14
    first_two = (jnp.where(z == 1, 1, 0), jnp.where(e == 1, 2, jnp.where(z == 1, 0, 1)))

    def below(h):
        return (h % 8 >= 3) & (h % 8 < 7)

    @pl.when((e == 0) & jnp.logical_not(row13))
    def _():
        spread(first_two[0])

    @pl.when(row15 & (c < 15))
    def _():
        loop(4, lambda chunk: scatter_qf(chunk, lambda h: jnp.logical_not(below(h))))

    centre()

    @pl.when((e == 0) & row13)
    def _():
        spread(0)

    pl.when((e == 1) & row15)(lambda: await_other(0))

    @pl.when((e == 1) & row15 & (c < 15))
    def _():
        loop(4, lambda chunk: scatter_qf(chunk, below))

    @pl.when(jnp.logical_not(middle))
    def _():
        spread(first_two[1])

    @pl.when((e == 0) & row15)
    def _():
        loop(4, lambda chunk: scatter_qf(chunk, below))

    @pl.when((e == 0) & jnp.logical_not(middle))
    def _():
        collect(0)
        apply(0)

    @pl.when(middle)
    def _():
        gather_and_solve()

    @pl.when((e == 0) & middle)
    def _():
        collect(0)
        apply(0)

    @pl.when(chain1 | chain2)
    def _():
        loop(4, scatter_pf)

    @pl.when(e == 0)
    def _():
        collect(1)
        apply(1)

    @pl.when(e == 1)
    def _():
        collect(2)
        pl.when(jnp.logical_not(row15))(lambda: await_other(0))
        so[pl.ds(0, NB)] = yt[0].T
        apply(1)

    apply(2)

    @pl.when(late)
    def _():
        sl[...] = vf[...].T

    @pl.when(jnp.logical_not(late))
    def _():
        sl[...] = jnp.zeros_like(sl)

    for j in range(STEPS):

        @pl.when(e == SIDE[j])
        def _():
            sent(yt.at[j, pl.ds(0, 192)], s3_s.at[j % 2])
            sent(yt.at[j], s4_s.at[j % 2])
            with_children(j, lambda children: sent(yt.at[j, pl.ds(0, len(children) * CHUNK)], s2_s.at[j % 2]))

    for k in range(2):

        @pl.when(((z == 1) & (e == 0) | (z == 2) & (e == 1)) & heads[k] & jnp.logical_not(chain1 | chain2))
        def _():
            sent(yt.at[0, pl.ds(0, 192), halves[k]], s1b_s.at[k])

    @pl.when(row0)
    def _():
        @pl.when(to_one | to_two)
        def _():
            sent(yr.at[pl.ds(0, CHUNK)], y0_s)

        @pl.when(e == SIDE[0])
        def _():
            sent(yr.at[pl.ds(0, CHUNK)], s1_s.at[0])

    @pl.when(chain1 | chain2)
    def _():
        for k in range(1, 4):
            sent(yr.at[pl.ds(0, CHUNK)], s1_s.at[k])

    @pl.when((c == 0) & (r >= 2))
    def _():
        for k in range(4):
            sent(pf.at[pl.ds(0, CHUNK)], pc_s.at[k])

    @pl.when(chain1 | ((c == 1) & (r >= 2)) | ((c == 2) & (r >= 3)))
    def _():
        sent(pf.at[pl.ds(0, 240)], pf_s)

    @pl.when(late & (c < r))
    def _():
        sent(qf.at[pl.ds(0, 240)], qf_s)

    @pl.when(row15 & ((c == 13) | (c == 14)))
    def _():
        for k in range(4):
            sent(qf.at[pl.ds(0, CHUNK)], qc_s.at[k])

    @pl.when(back1)
    def _():
        sent(qf, tb_s)

    @pl.when(back1)
    def _():
        sent(qf.at[pl.ds(0, 240)], w_s)

    @pl.when(row14 | row13)
    def _():
        sent(qf.at[pl.ds(0, 112)], ag_s)
        for k in range(4):
            sent(wg.at[0, :, 0], sib_s.at[k])

    rest_out[...] = bt[rows(c, PIECE)].astype(F32)
    for j in range(STEPS):

        @pl.when((r == 1) if j == 0 else (r > j))
        def _():
            @pl.when(c == j)
            def _():
                rest_out[...] -= pf[rows(c, PIECE)].astype(F32)

            @pl.when(c != j)
            def _():
                got(rp.at[j], rp_r.at[j])
                rest_out[...] -= rp[j].astype(F32)

    back_out[...] = jnp.zeros_like(back_out)
    for j in range(STEPS):

        @pl.when(c < 13 + j)
        def _():
            @pl.when(r == 13 + j)
            def _():
                back_out[...] += qf[rows(r, PIECE)].astype(F32)

            @pl.when(r != 13 + j)
            def _():
                got(qr.at[j], qr_r.at[j])
                back_out[...] += qr[j].astype(F32)


def hand_over(*refs):
    sems = refs[-1]
    copies = [pltpu.make_async_copy(refs[k], refs[k + 4], sems.at[k]) for k in range(4)]
    for copy in copies:
        copy.start()
    for copy in copies:
        copy.wait()


def local(factor, diag_inv, rhs, forward_values):
    anywhere = pl.BlockSpec(memory_space=pl.ANY)
    vmem = pl.BlockSpec(memory_space=pltpu.VMEM)
    dma = pltpu.SemaphoreType.DMA
    square = pltpu.VMEM((NB, NB), BF16)
    tall = pltpu.VMEM((NB, COLS), BF16)
    wide = pltpu.VMEM((COLS, NB), BF16)
    results = pl.pallas_call(
        kernel,
        name="solves",
        out_shape=(
            pltpu.VMEM((STEPS * NB, COLS), BF16),
            pltpu.VMEM((PIECE, NB), F32),
            pltpu.VMEM((PIECE, NB), F32),
            pltpu.VMEM((NB, COLS), F32),
        ),
        in_specs=[anywhere] * 4,
        out_specs=(vmem,) * 4,
        scratch_shapes=[
            square, square, tall, tall, square, square, wide, wide,
            pltpu.VMEM((STEPS, COLS, NB), BF16),
            pltpu.VMEM((COLS, NB), F32),
            wide, wide, wide, wide,
            pltpu.VMEM((STEPS, PIECE, NB), BF16),
            wide,
            pltpu.VMEM((STEPS, PIECE, NB), BF16),
            wide,
            pltpu.VMEM((PIECE, NB), BF16),
            pltpu.VMEM((4, 2, 2, PIECE, NB), BF16),
            wide,
            wide,
            pltpu.SemaphoreType.REGULAR((2,)), pltpu.SemaphoreType.REGULAR, dma((4,)),
            dma((4,)), dma((4,)), dma((2, 2)), dma((2, 4)), dma((2, 4)), dma((3,)), dma((3,)), dma((2,)), dma((4,)), dma((4,)),
            dma(()), dma((4,)), dma((2,)), dma((2,)), dma((2,)), dma((2,)), dma(()), dma((4,)), dma(()), dma(()), dma(()),
        ],
        compiler_params=pltpu.CompilerParams(
            collective_id=0, has_side_effects=True, vmem_limit_bytes=60 * 1024 * 1024
        ),
    )(factor, diag_inv, rhs, forward_values)
    solved, rest, back, answer = pl.pallas_call(
        hand_over,
        name="hand_over",
        out_shape=(
            jax.ShapeDtypeStruct((STEPS * NB, COLS), BF16),
            jax.ShapeDtypeStruct((PIECE, NB), F32),
            jax.ShapeDtypeStruct((PIECE, NB), F32),
            jax.ShapeDtypeStruct((NB, COLS), F32),
        ),
        in_specs=[vmem] * 4,
        out_specs=(anywhere,) * 4,
        scratch_shapes=[dma((4,))],
        compiler_params=pltpu.CompilerParams(vmem_limit_bytes=32 * 1024 * 1024),
    )(*results)
    return solved, rest.T, back.T, answer


def solution(mesh):
    placed = (P("row", "col"), P("row", None), P("row", None), P("row", None))
    return jax.shard_map(
        local,
        mesh=mesh,
        in_specs=placed,
        out_specs=(P(), P("row", "col"), P("col", "row"), P("row", None)),
        check_vma=False,
    )
```
